32 devices in a mesh: fields: 2 (over x), vel: 8 (over z, y), rows: 2 (over core).
Axes of the slice: x: 2, y: 2, z: 4, core: 2. Of those that a mesh axis runs over, the one named last changes fastest.
Arguments:
- images: float32 [16, 64, 4096], P(('fields', 'vel'), 'rows'), parts along dimension 0, may hold values from -6 to 6
- variance: float32 [16, 64, 4096], P(('fields', 'vel'), 'rows'), parts along dimension 0, may hold values from 0.5 to 2
- spread_kernel: float32 [21, 21], replicated, may hold values from 0.05 to 1
- shifts: int32 [576, 3, 2], P(('fields', 'vel')), parts along dimension 0, may hold values from -16 to 16, as said below
- epoch_owner: int32 [6], P('fields'), parts along dimension 0, may hold values from 0 to 7, as said below
- valid_rows: int32 [6, 2], P('fields'), parts along dimension 0, may hold values from 0 to 64, as said below
Outputs:
- likelihood: float32 [576, 64, 4096], P(('fields', 'vel'), 'rows'), parts along dimension 0
The draws below stay inside these ranges and needn't reach their ends.
There are 2 independent parts, one for each index of `fields`. The reference program is written for one: setup_inputs(seed, part) draws one part's arguments, and reference() takes and returns one part's arrays. A program takes and returns all parts, laid end to end along the dimension named above; an argument that names none is the same for every part. Nothing has to cross between parts.
Inputs may be any that keep to these rules, and one draw needn't show every extreme that they name: `shifts`: each entry lies in -16 to 16; both ends are taken in every draw. `epoch_owner`: the epochs are held by distinct slots. `valid_rows`: in each row the first entry is below the second; the first epoch starts at row 0 and the last ends at row 64.
All inputs are finite; a program needn't handle non-finite values.
Results may differ from the reference program's by a relative error of at most 0.0003.
Values sent between devices are 32-bit elements; how exact they have to be, the bound alone decides.
No kernel may reach another device: no remote copies, remote signals or barrier semaphores. Data moves between devices by JAX's collectives and lax.ppermute only.
A program may use at most 128 MiB of HBM per device.

```python
import math
import jax
import jax.numpy as jnp
from jax import lax

COLS = 4096
KSIZE = 21
MAXS = 16
EPOCHS = 3
ROWS = 64
VELOCITIES = 288
SLOTS = 8


def draw_shifts(key, part):
    values = jax.random.randint(key, (VELOCITIES, EPOCHS, 2), -MAXS, MAXS + 1)
    values = values.at[0, EPOCHS - 1].set(MAXS)
    values = values.at[VELOCITIES - 1, 0].set(-MAXS)
    return values.astype(jnp.int32)


def draw_epoch_owner(key, part):
    return jax.random.permutation(key, SLOTS)[:EPOCHS].astype(jnp.int32)


def draw_valid_rows(key, part):
    lower_rows = jax.random.randint(jax.random.fold_in(key, 11), (EPOCHS,), 0, ROWS // 4)
    upper_rows = ROWS - jax.random.randint(jax.random.fold_in(key, 12), (EPOCHS,), 0, ROWS // 4)
    lower_rows = lower_rows.at[0].set(0)
    upper_rows = upper_rows.at[EPOCHS - 1].set(ROWS)
    return jnp.stack([lower_rows, upper_rows], axis=1).astype(jnp.int32)


def block_scale(key, extent, shards, low, high):
    def one(axis_at, blocks):
        heights = jax.random.uniform(jax.random.fold_in(jax.random.fold_in(key, 6), axis_at), (blocks,), jnp.float32, low / len(shards), high / len(shards))
        return jnp.repeat(jnp.exp(heights), extent[axis_at] // blocks).reshape((-1,) + (1,) * (len(extent) - axis_at - 1))

    loudness = one(*shards[0])
    for cut in shards[1:]:
        loudness = loudness * one(*cut)
    return loudness


def normal_values(rng, shape, deviation, most, pieces=(), kind=jnp.bfloat16):
    array = deviation * jax.random.normal(rng, shape, jnp.float32)
    if pieces:
        array = array * block_scale(rng, shape, pieces, -0.22, 0.18)
    return jnp.clip(array, -most, most).astype(kind)


def setup_inputs(seed: int = 0, part: int = 0) -> dict:
    arg_keys = jax.random.split(jax.random.key(seed), 7)
    part_keys = jax.random.split(jax.random.fold_in(arg_keys[6], part), 7)
    images = normal_values(part_keys[0], (SLOTS, ROWS, COLS), 1.0, 6.0, ((0, 8), (1, 2)), jnp.float32)
    variance = jnp.clip(0.5 + 1.5 * jax.random.uniform(part_keys[1], (SLOTS, ROWS, COLS), jnp.float32) ** block_scale(part_keys[1], (SLOTS, ROWS, COLS), ((0, 8), (1, 2)), -0.2, 0.2), 0.5, 2.0)
    spread_kernel = jnp.clip(jnp.exp(jax.random.uniform(arg_keys[2], (KSIZE, KSIZE), jnp.float32, math.log(0.05), math.log(1.0))), 0.05, 1.0)
    shifts = draw_shifts(jax.random.fold_in(jax.random.fold_in(arg_keys[6], part), 71), part)
    epoch_owner = draw_epoch_owner(jax.random.fold_in(jax.random.fold_in(arg_keys[6], part), 71), part)
    valid_rows = draw_valid_rows(jax.random.fold_in(jax.random.fold_in(arg_keys[6], part), 71), part)
    return {"images": images, "variance": variance, "spread_kernel": spread_kernel, "shifts": shifts, "epoch_owner": epoch_owner, "valid_rows": valid_rows}


def correlate(field, kernel):
    half = KSIZE // 2
    padded = jnp.pad(field, half)
    summed = jnp.zeros_like(field)
    for row_off in range(KSIZE):
        for col_off in range(KSIZE):
            summed = summed + kernel[row_off, col_off] * padded[row_off:row_off + ROWS, col_off:col_off + COLS]
    return summed

def reference(images, variance, spread_kernel, shifts, epoch_owner, valid_rows):
    kernel_norm = spread_kernel / jnp.sum(spread_kernel)
    kernel_sq = kernel_norm * kernel_norm
    floor = 0.5 * jnp.sum(kernel_sq)
    row_ids = jnp.arange(ROWS, dtype=jnp.int32)[:, None]
    stacked = []
    for epoch in range(EPOCHS):
        slot = epoch_owner[epoch]
        exposure = images[slot]
        noise_var = variance[slot]
        usable = (row_ids >= valid_rows[epoch, 0]) & (row_ids < valid_rows[epoch, 1])
        weighted = jnp.where(usable, exposure / noise_var, jnp.float32(0.0))
        inverse = jnp.where(usable, 1.0 / noise_var, jnp.float32(0.0))
        pair = jnp.stack([correlate(weighted, kernel_norm), correlate(inverse, kernel_sq)])
        stacked.append(jnp.pad(pair, ((0, 0), (MAXS, MAXS), (MAXS, MAXS))))
    padded_all = jnp.stack(stacked)

    def one_velocity(shift):
        summed = jnp.zeros((2, ROWS, COLS), jnp.float32)
        for epoch in range(EPOCHS):
            start_row = (MAXS + shift[epoch, 0]).astype(jnp.int32)
            start_col = (MAXS + shift[epoch, 1]).astype(jnp.int32)
            summed = summed + lax.dynamic_slice(padded_all[epoch], (jnp.int32(0), start_row, start_col), (2, ROWS, COLS))
        return summed[0] / jnp.sqrt(jnp.maximum(summed[1], floor))
    return lax.map(one_velocity, shifts)
```

```python
import functools
import jax
import jax.numpy as jnp
from jax import lax
from jax.experimental import pallas as pl
from jax.experimental.pallas import tpu as pltpu
from jax.sharding import PartitionSpec as P

LANES = 128
MAXS = 16
VMEM = 48 << 20


def band_kernel(taps, high_ref, both_ref):
    kinds, ksize = both_ref.shape[0], both_ref.shape[1]
    skip = LANES - MAXS - ksize // 2
    inner = lax.broadcasted_iota(jnp.int32, (2 * LANES, LANES), 0)
    outer = lax.broadcasted_iota(jnp.int32, (2 * LANES, LANES), 1)
    offset = inner - outer - skip

    def one(index, _):
        kind, row = index // ksize, index % ksize
        band = jnp.zeros((2 * LANES, LANES), jnp.float32)
        for col in range(ksize):
            band = jnp.where(offset == col, taps[index * ksize + col], band)
        high = band.astype(jnp.bfloat16)
        low = (band - high.astype(jnp.float32)).astype(jnp.bfloat16)
        high_ref[kind, row] = high
        both_ref[kind, row, :, :LANES] = high
        both_ref[kind, row, :, LANES:] = low
        return 0

    lax.fori_loop(0, kinds * ksize, one, 0)


def bands(taps, ksize):
    shape = (2, ksize, 2 * LANES)
    return pl.pallas_call(
        band_kernel,
        in_specs=[pl.BlockSpec(memory_space=pltpu.SMEM)],
        out_specs=[pl.BlockSpec(memory_space=pltpu.VMEM)] * 2,
        out_shape=[
            jax.ShapeDtypeStruct(shape + (LANES,), jnp.bfloat16),
            jax.ShapeDtypeStruct(shape + (2 * LANES,), jnp.bfloat16),
        ],
        compiler_params=pltpu.CompilerParams(vmem_limit_bytes=VMEM),
        cost_estimate=pl.CostEstimate(flops=0, bytes_accessed=24 << 20, transcendentals=0),
    )(taps)


def correlate_kernel(place, wide, border, high_ref, both_ref, edge_ref, inner_ref, ext, summed):
    epochs, kinds, height, width = wide.shape
    ksize = high_ref.shape[1]
    tiles = width // LANES - 1
    first, lower = place[0] == 0, place[1]
    at_border = pl.multiple_of((1 - lower) * (MAXS + height), MAXS)
    ext[...] = jnp.zeros_like(ext)
    for tile in range(tiles + 1):
        columns = slice(tile * LANES, (tile + 1) * LANES)
        ext[:, :, tile, MAXS : MAXS + height] = wide[:, :, :, columns]
        ext[:, :, tile, pl.ds(at_border, MAXS)] = border[:, :, :, columns]

    blank = tiles + 1
    ahead = jnp.where(first, blank, 0)
    windows = [(ahead, 1)] + [(tile, tile + 1) for tile in range(1, tiles)] + [(0, blank)]
    lane = lax.broadcasted_iota(jnp.int32, (height, LANES), 1)
    wrapped = jnp.logical_and(first, lane < MAXS)
    for kind in range(kinds):
        summed[...] = jnp.zeros_like(summed)

        def add_row(row, _):
            rows = pl.ds(row + MAXS - ksize // 2, height)
            window = jnp.concatenate(
                [
                    jnp.concatenate([ext[epoch, kind, left, rows], ext[epoch, kind, right, rows]], axis=1)
                    for epoch in range(epochs)
                    for left, right in windows
                ],
                axis=0,
            )
            high = window.astype(jnp.bfloat16)
            low = (window - high.astype(jnp.float32)).astype(jnp.bfloat16)
            pair = jnp.dot(high, both_ref[kind, row], preferred_element_type=jnp.float32)
            rest = jnp.dot(low, high_ref[kind, row], preferred_element_type=jnp.float32)
            summed[...] += pair[:, :LANES] + (pair[:, LANES:] + rest)
            return 0

        lax.fori_loop(0, ksize, add_row, 0)
        for epoch in range(epochs):
            base = epoch * (tiles + 1) * height
            over = base + tiles * height
            summed[base : base + height] = jnp.where(
                wrapped, summed[over : over + height], summed[base : base + height]
            )
            for tile in range(tiles):
                start = base + tile * height
                at_edge = pl.multiple_of(start + (1 - lower) * (height - MAXS), MAXS)
                at_inner = pl.multiple_of(start + lower * MAXS, MAXS)
                edge_ref[epoch, kind, tile] = summed[pl.ds(at_edge, MAXS)]
                inner_ref[epoch, kind, tile] = summed[pl.ds(at_inner, MAXS)]


def correlate(place, wide, border, high, both):
    epochs, kinds, height, width = wide.shape
    tiles = width // LANES - 1
    half = jax.ShapeDtypeStruct((epochs, kinds, tiles, MAXS, LANES), jnp.float32)
    flops = 3 * 2 * epochs * kinds * (tiles + 1) * height * high.shape[1] * 2 * LANES * LANES
    return pl.pallas_call(
        correlate_kernel,
        in_specs=[pl.BlockSpec(memory_space=pltpu.SMEM)] + [pl.BlockSpec(memory_space=pltpu.VMEM)] * 4,
        out_specs=[pl.BlockSpec(memory_space=pltpu.VMEM)] * 2,
        out_shape=[half, half],
        scratch_shapes=[
            pltpu.VMEM((epochs, kinds, tiles + 2, height + 2 * MAXS, LANES), jnp.float32),
            pltpu.VMEM((epochs * (tiles + 1) * height, LANES), jnp.float32),
        ],
        compiler_params=pltpu.CompilerParams(vmem_limit_bytes=VMEM),
        cost_estimate=pl.CostEstimate(flops=flops, bytes_accessed=12 << 20, transcendentals=0),
    )(place, wide, border, high, both)


def stack_kernel(place, shifts, floor, *refs, group, parts, blocks):
    sources, out_ref, held = refs[: 6 * parts], refs[-2], refs[-1]
    part, base = pl.program_id(0), pl.program_id(1) * group
    epochs, kinds, count = held.shape[0], held.shape[1], held.shape[2]
    tiles = count - 1
    lower = place[parts]
    lane = lax.broadcasted_iota(jnp.int32, (1, LANES), 1)
    at = [pl.multiple_of(row, MAXS) for row in (32 - 16 * lower, 16 + 16 * lower, 48 - 48 * lower)]

    for index in range(parts):

        @pl.when(jnp.logical_and(part == index, pl.program_id(1) == 0))
        def _():
            block = place[index]
            keep_first = jnp.where(jnp.logical_and(block == 0, lane < MAXS), 0.0, 1.0) > 0.5
            keep_last = jnp.where(jnp.logical_and(block == blocks - 1, lane >= MAXS), 0.0, 1.0) > 0.5
            blank = pl.multiple_of(48 * lower, MAXS)
            held[:, :, :, pl.ds(blank, MAXS)] = jnp.zeros((epochs, kinds, count, MAXS, LANES), jnp.float32)
            for piece in range(3):
                own, nearby = sources[6 * index + piece], sources[6 * index + 3 + piece]
                rows = pl.ds(at[piece], MAXS)
                for epoch in range(epochs):
                    for kind in range(kinds):
                        held[epoch, kind, 0, rows] = jnp.where(keep_first, own[epoch, kind, 0], 0.0)
                        for tile in range(1, tiles):
                            held[epoch, kind, tile, rows] = own[epoch, kind, tile]
                        held[epoch, kind, tiles, rows] = jnp.where(keep_last, nearby[epoch, kind, 0], 0.0)

    low = floor[0]
    height = out_ref.shape[1]
    across = lax.broadcasted_iota(jnp.int32, (8, LANES), 1)

    def one_velocity(local_index, _):
        start = (base + local_index) * epochs * 2
        rows = [shifts[start + 2 * epoch] + MAXS for epoch in range(epochs)]
        cols = [shifts[start + 2 * epoch + 1] + MAXS for epoch in range(epochs)]
        beyond = [across < col for col in cols]
        turn = [jnp.where(col == 0, 0, LANES - col) for col in cols]
        for top in range(0, height, 8):
            totals = [[None] * tiles for _ in range(kinds)]
            for epoch in range(epochs):
                for kind in range(kinds):
                    loaded = [held[epoch, kind, tile, pl.ds(rows[epoch] + top, 8)] for tile in range(count)]
                    for tile in range(tiles):
                        merged = jnp.where(beyond[epoch], loaded[tile + 1], loaded[tile])
                        moved = pltpu.roll(merged, turn[epoch], 1)
                        totals[kind][tile] = moved if epoch == 0 else totals[kind][tile] + moved
            for tile in range(tiles):
                out_ref[local_index, top : top + 8, tile * LANES : (tile + 1) * LANES] = totals[0][tile] * lax.rsqrt(
                    jnp.maximum(totals[1][tile], low)
                )
        return 0

    lax.fori_loop(0, group, one_velocity, 0)


def stack_blocks(place, shifts, floor, sources, out, out_shape, parts, blocks):
    epochs, kinds, tiles = sources[0].shape[:3]
    velocities, height, columns = out_shape.shape
    group = next(size for size in (12, 9, 8, 6, 4, 3, 2, 1) if velocities % size == 0)
    width = tiles * LANES
    whole = pl.BlockSpec((epochs, kinds, tiles, MAXS, LANES), lambda *_: (0, 0, 0, 0, 0))
    front = pl.BlockSpec((epochs, kinds, 1, MAXS, LANES), lambda *_: (0, 0, 0, 0, 0))
    in_specs = [whole] * 3 + [front] * 3
    in_specs = in_specs * parts
    operands = list(sources)
    aliases = {}
    if out is not None:
        in_specs.append(pl.BlockSpec(memory_space=pl.ANY))
        operands.append(out)
        aliases = {3 + len(sources): 0}
    work = parts * velocities * height * width
    return pl.pallas_call(
        functools.partial(stack_kernel, group=group, parts=parts, blocks=blocks),
        grid_spec=pltpu.PrefetchScalarGridSpec(
            num_scalar_prefetch=3,
            grid=(parts, velocities // group),
            in_specs=in_specs,
            out_specs=pl.BlockSpec((group, height, width), lambda part, chunk, place, *_: (chunk, 0, place[part])),
            scratch_shapes=[pltpu.VMEM((epochs, kinds, tiles + 1, height + 2 * MAXS, LANES), jnp.float32)],
        ),
        out_shape=out_shape,
        input_output_aliases=aliases,
        compiler_params=pltpu.CompilerParams(vmem_limit_bytes=VMEM),
        cost_estimate=pl.CostEstimate(flops=16 * work, bytes_accessed=16 * work, transcendentals=work),
    )(place, shifts, floor, *operands)


def local(images, variance, spread_kernel, shifts, epoch_owner, valid_rows):
    exposure, noise_var = images[0], variance[0]
    height, columns = exposure.shape
    ksize = spread_kernel.shape[0]
    epochs = epoch_owner.shape[0]
    blocks = lax.axis_size("vel")
    width = columns // blocks
    me, lower = lax.axis_index("vel"), lax.axis_index("rows")
    swap = [(0, 1), (1, 0)]

    order = list(range(0, blocks, 2)) + list(range(1, blocks, 2))[::-1]
    right = [(order[i], order[(i + 1) % blocks]) for i in range(blocks)]
    left = [(b, a) for a, b in right]

    def position(index):
        return jnp.where(index % 2 == 0, index // 2, blocks - 1 - index // 2)

    mine = position(me)
    kernel_norm = spread_kernel / jnp.sum(spread_kernel)
    kernel_sq = kernel_norm * kernel_norm
    floor = (0.5 * jnp.sum(kernel_sq)).reshape(1)
    high, both = bands(jnp.stack([kernel_norm, kernel_sq]).reshape(-1), ksize)

    chunks = []
    for step in range(blocks):
        start = position(me ^ step) * width
        chunk = jnp.stack(
            [
                lax.dynamic_slice_in_dim(exposure, start, width, 1),
                lax.dynamic_slice_in_dim(noise_var, start, width, 1),
            ]
        )
        if step:
            chunk = lax.ppermute(chunk, "vel", [(i, i ^ step) for i in range(blocks)])
        chunks.append(chunk)
    row_ids = lower * height + jnp.arange(height, dtype=jnp.int32)[:, None]
    fields = []
    for epoch in range(epochs):
        key = epoch_owner[epoch] ^ me
        chosen = chunks[0]
        for step in range(1, blocks):
            chosen = jnp.where(key == step, chunks[step], chosen)
        usable = (row_ids >= valid_rows[epoch, 0]) & (row_ids < valid_rows[epoch, 1])
        fields.append(
            jnp.stack([jnp.where(usable, chosen[0] / chosen[1], 0.0), jnp.where(usable, 1.0 / chosen[1], 0.0)])
        )
    field = jnp.stack(fields)
    before = lax.ppermute(field[..., width - LANES :], "vel", right)
    wide = jnp.concatenate([before, field], axis=3)
    border = lax.ppermute(jnp.where(lower == 0, wide[:, :, height - MAXS :], wide[:, :, :MAXS]), "rows", swap)
    place = jnp.stack([mine, lower]).astype(jnp.int32)
    edge, inner = correlate(place, wide, border, high, both)

    def with_border(edge, inner):
        return edge, inner, lax.ppermute(edge, "rows", swap)

    flat_shifts = shifts.reshape(-1)
    out_shape = jax.ShapeDtypeStruct((shifts.shape[0], height, columns), jnp.float32)
    have = {0: with_border(edge, inner)}
    out = None
    half = blocks // 2
    for step in range(1, half + 1):
        if step < half:
            for sign, ring in ((-1, right), (1, left)):
                edge, inner, _ = have[sign * (step - 1)]
                have[sign * step] = with_border(
                    lax.ppermute(edge, "vel", ring), lax.ppermute(inner, "vel", ring)
                )
        else:
            edge = lax.ppermute(have[1 - step][0], "vel", right)
            inner = lax.ppermute(have[step - 1][1], "vel", left)
            have[step] = have[-step] = with_border(edge, inner)
        now = [step - 1, -step]
        sources = []
        for offset in now:
            sources += list(have[offset]) + list(have[offset + 1])
        place = jnp.stack([(mine + offset) % blocks for offset in now] + [lower]).astype(jnp.int32)
        out = stack_blocks(place, flat_shifts, floor, sources, out, out_shape, len(now), blocks)
    return out


def solution(mesh):
    in_specs = (
        P(("fields", "vel"), "rows", None),
        P(("fields", "vel"), "rows", None),
        P(),
        P(("fields", "vel"), None, None),
        P("fields"),
        P("fields", None),
    )
    out_specs = P(("fields", "vel"), "rows", None)
    return jax.shard_map(local, mesh=mesh, in_specs=in_specs, out_specs=out_specs, check_vma=False)
```

```python
import functools
import jax
import jax.numpy as jnp
from jax import lax
from jax.experimental import pallas as pl
from jax.experimental.pallas import tpu as pltpu
from jax.sharding import PartitionSpec as P

LANES = 128
MAXS = 16
VMEM = 48 << 20


def band_kernel(taps, high_ref, both_ref):
    kinds, ksize = both_ref.shape[0], both_ref.shape[1]
    skip = LANES - MAXS - ksize // 2
    inner = lax.broadcasted_iota(jnp.int32, (2 * LANES, LANES), 0)
    outer = lax.broadcasted_iota(jnp.int32, (2 * LANES, LANES), 1)
    offset = inner - outer - skip

    def one(index, _):
        kind, row = index // ksize, index % ksize
        band = jnp.zeros((2 * LANES, LANES), jnp.float32)
        for col in range(ksize):
            band = jnp.where(offset == col, taps[index * ksize + col], band)
        high = band.astype(jnp.bfloat16)
        low = (band - high.astype(jnp.float32)).astype(jnp.bfloat16)
        high_ref[kind, row] = high
        both_ref[kind, row, :, :LANES] = high
        both_ref[kind, row, :, LANES:] = low
        return 0

    lax.fori_loop(0, kinds * ksize, one, 0)


def bands(taps, ksize):
    shape = (2, ksize, 2 * LANES)
    return pl.pallas_call(
        band_kernel,
        in_specs=[pl.BlockSpec(memory_space=pltpu.SMEM)],
        out_specs=[pl.BlockSpec(memory_space=pltpu.VMEM)] * 2,
        out_shape=[
            jax.ShapeDtypeStruct(shape + (LANES,), jnp.bfloat16),
            jax.ShapeDtypeStruct(shape + (2 * LANES,), jnp.bfloat16),
        ],
        compiler_params=pltpu.CompilerParams(vmem_limit_bytes=VMEM),
        cost_estimate=pl.CostEstimate(flops=0, bytes_accessed=24 << 20, transcendentals=0),
    )(taps)


def correlate_kernel(place, wide, border, high_ref, both_ref, rows_ref, ext, summed):
    epochs, kinds, height, width = wide.shape
    ksize = high_ref.shape[1]
    tiles = width // LANES - 1
    first, lower = place[0] == 0, place[1]
    at_border = pl.multiple_of((1 - lower) * (MAXS + height), MAXS)
    ext[...] = jnp.zeros_like(ext)
    for tile in range(tiles + 1):
        columns = slice(tile * LANES, (tile + 1) * LANES)
        ext[:, :, tile, MAXS : MAXS + height] = wide[:, :, :, columns]
        ext[:, :, tile, pl.ds(at_border, MAXS)] = border[:, :, :, columns]

    blank = tiles + 1
    ahead = jnp.where(first, blank, 0)
    windows = [(ahead, 1)] + [(tile, tile + 1) for tile in range(1, tiles)] + [(0, blank)]
    lane = lax.broadcasted_iota(jnp.int32, (height, LANES), 1)
    wrapped = jnp.logical_and(first, lane < MAXS)
    for kind in range(kinds):
        summed[...] = jnp.zeros_like(summed)

        def add_row(row, _):
            rows = pl.ds(row + MAXS - ksize // 2, height)
            window = jnp.concatenate(
                [
                    jnp.concatenate([ext[epoch, kind, left, rows], ext[epoch, kind, right, rows]], axis=1)
                    for epoch in range(epochs)
                    for left, right in windows
                ],
                axis=0,
            )
            high = window.astype(jnp.bfloat16)
            low = (window - high.astype(jnp.float32)).astype(jnp.bfloat16)
            pair = jnp.dot(high, both_ref[kind, row], preferred_element_type=jnp.float32)
            rest = jnp.dot(low, high_ref[kind, row], preferred_element_type=jnp.float32)
            summed[...] += pair[:, :LANES] + (pair[:, LANES:] + rest)
            return 0

        lax.fori_loop(0, ksize, add_row, 0)
        for epoch in range(epochs):
            base = epoch * (tiles + 1) * height
            over = base + tiles * height
            summed[base : base + height] = jnp.where(
                wrapped, summed[over : over + height], summed[base : base + height]
            )
            for tile in range(tiles):
                start = base + tile * height
                at_edge = pl.multiple_of(start + (1 - lower) * (height - MAXS), MAXS)
                at_inner = pl.multiple_of(start + lower * MAXS, MAXS)
                rows_ref[0, epoch, kind, tile] = summed[pl.ds(at_edge, MAXS)]
                rows_ref[1, epoch, kind, tile] = summed[pl.ds(at_inner, MAXS)]


def correlate(place, wide, border, high, both):
    epochs, kinds, height, width = wide.shape
    tiles = width // LANES - 1
    flops = 3 * 2 * epochs * kinds * (tiles + 1) * height * high.shape[1] * 2 * LANES * LANES
    return pl.pallas_call(
        correlate_kernel,
        in_specs=[pl.BlockSpec(memory_space=pltpu.SMEM)] + [pl.BlockSpec(memory_space=pltpu.VMEM)] * 4,
        out_specs=pl.BlockSpec(memory_space=pltpu.VMEM),
        out_shape=jax.ShapeDtypeStruct((2, epochs, kinds, tiles, MAXS, LANES), jnp.float32),
        scratch_shapes=[
            pltpu.VMEM((epochs, kinds, tiles + 2, height + 2 * MAXS, LANES), jnp.float32),
            pltpu.VMEM((epochs * (tiles + 1) * height, LANES), jnp.float32),
        ],
        compiler_params=pltpu.CompilerParams(vmem_limit_bytes=VMEM),
        cost_estimate=pl.CostEstimate(flops=flops, bytes_accessed=12 << 20, transcendentals=0),
    )(place, wide, border, high, both)


def stack_kernel(place, shifts, floor, *refs, group, parts, blocks):
    sources, out_ref, held = refs[: 6 * parts], refs[-2], refs[-1]
    part, base = pl.program_id(0), pl.program_id(1) * group
    epochs, kinds, count = held.shape[0], held.shape[1], held.shape[2]
    tiles = count - 1
    lower = place[parts]
    lane = lax.broadcasted_iota(jnp.int32, (1, LANES), 1)
    at = [pl.multiple_of(row, MAXS) for row in (32 - 16 * lower, 16 + 16 * lower, 48 - 48 * lower)]

    for index in range(parts):

        @pl.when(jnp.logical_and(part == index, pl.program_id(1) == 0))
        def _():
            block = place[index]
            keep_first = jnp.where(jnp.logical_and(block == 0, lane < MAXS), 0.0, 1.0) > 0.5
            keep_last = jnp.where(jnp.logical_and(block == blocks - 1, lane >= MAXS), 0.0, 1.0) > 0.5
            blank = pl.multiple_of(48 * lower, MAXS)
            held[:, :, :, pl.ds(blank, MAXS)] = jnp.zeros((epochs, kinds, count, MAXS, LANES), jnp.float32)
            for piece in range(3):
                own, nearby = sources[6 * index + piece], sources[6 * index + 3 + piece]
                rows = pl.ds(at[piece], MAXS)
                for epoch in range(epochs):
                    for kind in range(kinds):
                        held[epoch, kind, 0, rows] = jnp.where(keep_first, own[0, epoch, kind, 0], 0.0)
                        for tile in range(1, tiles):
                            held[epoch, kind, tile, rows] = own[0, epoch, kind, tile]
                        held[epoch, kind, tiles, rows] = jnp.where(keep_last, nearby[0, epoch, kind, 0], 0.0)

    low = floor[0]
    height = out_ref.shape[1]
    across = lax.broadcasted_iota(jnp.int32, (8, LANES), 1)

    def one_velocity(local_index, _):
        start = (base + local_index) * epochs * 2
        rows = [shifts[start + 2 * epoch] + MAXS for epoch in range(epochs)]
        cols = [shifts[start + 2 * epoch + 1] + MAXS for epoch in range(epochs)]
        beyond = [across < col for col in cols]
        turn = [jnp.where(col == 0, 0, LANES - col) for col in cols]
        for top in range(0, height, 8):
            totals = [[None] * tiles for _ in range(kinds)]
            for epoch in range(epochs):
                for kind in range(kinds):
                    loaded = [held[epoch, kind, tile, pl.ds(rows[epoch] + top, 8)] for tile in range(count)]
                    for tile in range(tiles):
                        merged = jnp.where(beyond[epoch], loaded[tile + 1], loaded[tile])
                        moved = pltpu.roll(merged, turn[epoch], 1)
                        totals[kind][tile] = moved if epoch == 0 else totals[kind][tile] + moved
            for tile in range(tiles):
                out_ref[local_index, top : top + 8, tile * LANES : (tile + 1) * LANES] = totals[0][tile] * lax.rsqrt(
                    jnp.maximum(totals[1][tile], low)
                )
        return 0

    lax.fori_loop(0, group, one_velocity, 0)


def stack_blocks(place, shifts, floor, sources, out, out_shape, parts, blocks):
    epochs, kinds, tiles = sources[0][0].shape[1:4]
    velocities, height, columns = out_shape.shape
    group = next(size for size in (12, 9, 8, 6, 4, 3, 2, 1) if velocities % size == 0)
    width = tiles * LANES
    in_specs, operands = [], []
    for index, (array, slot) in enumerate(sources):
        depth = tiles if index % 6 < 3 else 1
        in_specs.append(
            pl.BlockSpec((1, epochs, kinds, depth, MAXS, LANES), functools.partial(lambda at, *_: (at, 0, 0, 0, 0, 0), slot))
        )
        operands.append(array)
    aliases = {}
    if out is not None:
        in_specs.append(pl.BlockSpec(memory_space=pl.ANY))
        operands.append(out)
        aliases = {3 + len(sources): 0}
    work = parts * velocities * height * width
    return pl.pallas_call(
        functools.partial(stack_kernel, group=group, parts=parts, blocks=blocks),
        grid_spec=pltpu.PrefetchScalarGridSpec(
            num_scalar_prefetch=3,
            grid=(parts, velocities // group),
            in_specs=in_specs,
            out_specs=pl.BlockSpec((group, height, width), lambda part, chunk, place, *_: (chunk, 0, place[part])),
            scratch_shapes=[pltpu.VMEM((epochs, kinds, tiles + 1, height + 2 * MAXS, LANES), jnp.float32)],
        ),
        out_shape=out_shape,
        input_output_aliases=aliases,
        compiler_params=pltpu.CompilerParams(vmem_limit_bytes=VMEM),
        cost_estimate=pl.CostEstimate(flops=16 * work, bytes_accessed=24 * work, transcendentals=work),
    )(place, shifts, floor, *operands)


def local(images, variance, spread_kernel, shifts, epoch_owner, valid_rows):
    exposure, noise_var = images[0], variance[0]
    height, columns = exposure.shape
    ksize = spread_kernel.shape[0]
    epochs = epoch_owner.shape[0]
    blocks = lax.axis_size("vel")
    width = columns // blocks
    me, lower = lax.axis_index("vel"), lax.axis_index("rows")
    swap = [(0, 1), (1, 0)]

    order = list(range(0, blocks, 2)) + list(range(1, blocks, 2))[::-1]
    right = [(order[i], order[(i + 1) % blocks]) for i in range(blocks)]
    left = [(b, a) for a, b in right]

    def position(index):
        return jnp.where(index % 2 == 0, index // 2, blocks - 1 - index // 2)

    mine = position(me)
    kernel_norm = spread_kernel / jnp.sum(spread_kernel)
    kernel_sq = kernel_norm * kernel_norm
    floor = (0.5 * jnp.sum(kernel_sq)).reshape(1)
    taps = jnp.stack([kernel_norm, kernel_sq]).reshape(-1)

    chunks = []
    for step in range(blocks):
        start = position(me ^ step) * width
        chunk = jnp.stack(
            [
                lax.dynamic_slice_in_dim(exposure, start, width, 1),
                lax.dynamic_slice_in_dim(noise_var, start, width, 1),
            ]
        )
        if step:
            chunk = lax.ppermute(chunk, "vel", [(i, i ^ step) for i in range(blocks)])
        if step == 1:
            chunk, taps = lax.optimization_barrier((chunk, taps))
        chunks.append(chunk)
    high, both = bands(taps, ksize)
    chunks[-1], high, both = lax.optimization_barrier((chunks[-1], high, both))
    row_ids = lower * height + jnp.arange(height, dtype=jnp.int32)[:, None]
    fields = []
    for epoch in range(epochs):
        key = epoch_owner[epoch] ^ me
        chosen = chunks[0]
        for step in range(1, blocks):
            chosen = jnp.where(key == step, chunks[step], chosen)
        usable = (row_ids >= valid_rows[epoch, 0]) & (row_ids < valid_rows[epoch, 1])
        fields.append(
            jnp.stack([jnp.where(usable, chosen[0] / chosen[1], 0.0), jnp.where(usable, 1.0 / chosen[1], 0.0)])
        )
    field = jnp.stack(fields)
    before = lax.ppermute(field[..., width - LANES :], "vel", right)
    wide = jnp.concatenate([before, field], axis=3)
    border = lax.ppermute(jnp.where(lower == 0, wide[:, :, height - MAXS :], wide[:, :, :MAXS]), "rows", swap)
    place = jnp.stack([mine, lower]).astype(jnp.int32)
    payload = correlate(place, wide, border, high, both)

    flat_shifts = shifts.reshape(-1)
    out_shape = jax.ShapeDtypeStruct((shifts.shape[0], height, columns), jnp.float32)
    border = lax.ppermute(payload[:1], "rows", swap)
    have = {0: ((payload, 0), (payload, 1), (border, 0))}
    behind = ahead = payload
    half = blocks // 2
    out = None
    for step in range(1, half + 1):
        if step < half:
            behind, ahead = lax.ppermute(behind, "vel", right), lax.ppermute(ahead, "vel", left)
            if out is not None:
                behind, ahead, out = lax.optimization_barrier((behind, ahead, out))
            border = lax.ppermute(jnp.concatenate([behind[:1], ahead[:1]]), "rows", swap)
            have[-step] = ((behind, 0), (behind, 1), (border, 0))
            have[step] = ((ahead, 0), (ahead, 1), (border, 1))
        else:
            edge, inner = lax.ppermute(behind[:1], "vel", right), lax.ppermute(ahead[1:], "vel", left)
            if out is not None:
                edge, inner, out = lax.optimization_barrier((edge, inner, out))
            border = lax.ppermute(edge, "rows", swap)
            have[step] = have[-step] = ((edge, 0), (inner, 0), (border, 0))
        now = [step - 1, -step]
        sources = []
        for offset in now:
            sources += list(have[offset]) + list(have[offset + 1])
        place = jnp.stack([(mine + offset) % blocks for offset in now] + [lower]).astype(jnp.int32)
        out = stack_blocks(place, flat_shifts, floor, sources, out, out_shape, len(now), blocks)
    return out


def solution(mesh):
    in_specs = (
        P(("fields", "vel"), "rows", None),
        P(("fields", "vel"), "rows", None),
        P(),
        P(("fields", "vel"), None, None),
        P("fields"),
        P("fields", None),
    )
    out_specs = P(("fields", "vel"), "rows", None)
    return jax.shard_map(local, mesh=mesh, in_specs=in_specs, out_specs=out_specs, check_vma=False)
```

```python
import functools
import jax
import jax.numpy as jnp
from jax import lax
from jax.experimental import pallas as pl
from jax.experimental.pallas import tpu as pltpu
from jax.sharding import PartitionSpec as P

LANES = 128
MAXS = 16
VMEM = 48 << 20


def band_kernel(taps, high_ref, both_ref):
    kinds, ksize = both_ref.shape[0], both_ref.shape[1]
    skip = LANES - MAXS - ksize // 2
    inner = lax.broadcasted_iota(jnp.int32, (2 * LANES, LANES), 0)
    outer = lax.broadcasted_iota(jnp.int32, (2 * LANES, LANES), 1)
    offset = inner - outer - skip

    def one(index, _):
        kind, row = index // ksize, index % ksize
        band = jnp.zeros((2 * LANES, LANES), jnp.float32)
        for col in range(ksize):
            band = jnp.where(offset == col, taps[index * ksize + col], band)
        high = band.astype(jnp.bfloat16)
        low = (band - high.astype(jnp.float32)).astype(jnp.bfloat16)
        high_ref[kind, row] = high
        both_ref[kind, row, :, :LANES] = high
        both_ref[kind, row, :, LANES:] = low
        return 0

    lax.fori_loop(0, kinds * ksize, one, 0)


def bands(taps, ksize):
    shape = (2, ksize, 2 * LANES)
    return pl.pallas_call(
        band_kernel,
        in_specs=[pl.BlockSpec(memory_space=pltpu.SMEM)],
        out_specs=[pl.BlockSpec(memory_space=pltpu.VMEM)] * 2,
        out_shape=[
            jax.ShapeDtypeStruct(shape + (LANES,), jnp.bfloat16),
            jax.ShapeDtypeStruct(shape + (2 * LANES,), jnp.bfloat16),
        ],
        compiler_params=pltpu.CompilerParams(vmem_limit_bytes=VMEM),
        cost_estimate=pl.CostEstimate(flops=0, bytes_accessed=24 << 20, transcendentals=0),
    )(taps)


def correlate_kernel(place, wide, border, high_ref, both_ref, rows_ref, ext, summed):
    epochs, kinds, height, width = wide.shape
    ksize = high_ref.shape[1]
    tiles = width // LANES - 1
    first, lower = place[0] == 0, place[1]
    at_border = pl.multiple_of((1 - lower) * (MAXS + height), MAXS)
    ext[...] = jnp.zeros_like(ext)
    for tile in range(tiles + 1):
        columns = slice(tile * LANES, (tile + 1) * LANES)
        ext[:, :, tile, MAXS : MAXS + height] = wide[:, :, :, columns]
        ext[:, :, tile, pl.ds(at_border, MAXS)] = border[:, :, :, columns]

    blank = tiles + 1
    ahead = jnp.where(first, blank, 0)
    windows = [(ahead, 1)] + [(tile, tile + 1) for tile in range(1, tiles)] + [(0, blank)]
    lane = lax.broadcasted_iota(jnp.int32, (height, LANES), 1)
    wrapped = jnp.logical_and(first, lane < MAXS)
    for kind in range(kinds):
        summed[...] = jnp.zeros_like(summed)

        def add_row(row, _):
            rows = pl.ds(row + MAXS - ksize // 2, height)
            window = jnp.concatenate(
                [
                    jnp.concatenate([ext[epoch, kind, left, rows], ext[epoch, kind, right, rows]], axis=1)
                    for epoch in range(epochs)
                    for left, right in windows
                ],
                axis=0,
            )
            high = window.astype(jnp.bfloat16)
            low = (window - high.astype(jnp.float32)).astype(jnp.bfloat16)
            pair = jnp.dot(high, both_ref[kind, row], preferred_element_type=jnp.float32)
            rest = jnp.dot(low, high_ref[kind, row], preferred_element_type=jnp.float32)
            summed[...] += pair[:, :LANES] + (pair[:, LANES:] + rest)
            return 0

        lax.fori_loop(0, ksize, add_row, 0)
        for epoch in range(epochs):
            base = epoch * (tiles + 1) * height
            over = base + tiles * height
            summed[base : base + height] = jnp.where(
                wrapped, summed[over : over + height], summed[base : base + height]
            )
            for tile in range(tiles):
                start = base + tile * height
                at_edge = pl.multiple_of(start + (1 - lower) * (height - MAXS), MAXS)
                at_inner = pl.multiple_of(start + lower * MAXS, MAXS)
                rows_ref[0, epoch, kind, tile] = summed[pl.ds(at_edge, MAXS)]
                rows_ref[1, epoch, kind, tile] = summed[pl.ds(at_inner, MAXS)]


def correlate(place, wide, border, high, both):
    epochs, kinds, height, width = wide.shape
    tiles = width // LANES - 1
    flops = 3 * 2 * epochs * kinds * (tiles + 1) * height * high.shape[1] * 2 * LANES * LANES
    return pl.pallas_call(
        correlate_kernel,
        in_specs=[pl.BlockSpec(memory_space=pltpu.SMEM)] + [pl.BlockSpec(memory_space=pltpu.VMEM)] * 4,
        out_specs=pl.BlockSpec(memory_space=pltpu.VMEM),
        out_shape=jax.ShapeDtypeStruct((2, epochs, kinds, tiles, MAXS, LANES), jnp.float32),
        scratch_shapes=[
            pltpu.VMEM((epochs, kinds, tiles + 2, height + 2 * MAXS, LANES), jnp.float32),
            pltpu.VMEM((epochs * (tiles + 1) * height, LANES), jnp.float32),
        ],
        compiler_params=pltpu.CompilerParams(vmem_limit_bytes=VMEM),
        cost_estimate=pl.CostEstimate(flops=flops, bytes_accessed=12 << 20, transcendentals=0),
    )(place, wide, border, high, both)


def stack_kernel(place, shifts, floor, *refs, group, parts, blocks):
    sources, out_ref = refs[: 6 * parts], refs[-6]
    raw, whole, packed, near_packed, scale = refs[-5:]
    part, base = pl.program_id(0), pl.program_id(1) * group
    epochs, count, reach = whole.shape[:3]
    tiles = count - 1
    lower = place[parts]
    lane = lax.broadcasted_iota(jnp.int32, (1, LANES), 1)
    at = [pl.multiple_of(row, MAXS) for row in (32 - 16 * lower, 16 + 16 * lower, 48 - 48 * lower)]
    blank = pl.multiple_of(48 * lower, MAXS)
    most_psi = ((1 << 23) - 1) // epochs
    most_high = 255 // epochs
    most_phi = most_high * 64 + 63

    for index in range(parts):

        @pl.when(jnp.logical_and(part == index, pl.program_id(1) == 0))
        def _():
            block = place[index]
            keep_first = jnp.where(jnp.logical_and(block == 0, lane < MAXS), 0.0, 1.0) > 0.5
            keep_last = jnp.where(jnp.logical_and(block == blocks - 1, lane >= MAXS), 0.0, 1.0) > 0.5
            for epoch in range(epochs):
                for kind in range(2):
                    for tile in range(count):
                        raw[epoch, kind, tile, pl.ds(blank, MAXS)] = jnp.zeros((MAXS, LANES), jnp.float32)
            tops = [jnp.zeros((MAXS, LANES), jnp.float32) for _ in range(2)]
            for piece in range(3):
                own, nearby = sources[6 * index + piece], sources[6 * index + 3 + piece]
                rows = pl.ds(at[piece], MAXS)
                for epoch in range(epochs):
                    for kind in range(2):
                        for tile in range(count):
                            if tile == tiles:
                                value = jnp.where(keep_last, nearby[0, epoch, kind, 0], 0.0)
                            elif tile == 0:
                                value = jnp.where(keep_first, own[0, epoch, kind, 0], 0.0)
                            else:
                                value = own[0, epoch, kind, tile]
                            tops[kind] = jnp.maximum(tops[kind], jnp.abs(value))
                            raw[epoch, kind, tile, rows] = value
            tops = [jnp.full((8, LANES), jnp.maximum(jnp.max(top), 1e-30), jnp.float32) for top in tops]
            per_psi, per_phi = most_psi / tops[0], most_phi / tops[1]
            scale[0] = floor[0] * per_phi
            scale[1] = jnp.sqrt(per_phi) / per_psi

            def quantize(index, _):
                rows = pl.ds(pl.multiple_of(index * 8, 8), 8)
                for epoch in range(epochs):
                    lows = []
                    for tile in range(count):
                        psi = jnp.floor(raw[epoch, 0, tile, rows] * per_psi + 0.5).astype(jnp.int32)
                        phi = jnp.floor(jnp.maximum(raw[epoch, 1, tile, rows], 0.0) * per_phi + 0.5).astype(jnp.int32)
                        psi = jnp.clip(psi, -most_psi, most_psi)
                        phi = jnp.minimum(phi, most_phi)
                        whole[epoch, tile, rows] = psi * 256 + (phi >> 6)
                        lows.append(phi & 63)
                    here, nearby = lows[0], lows[1]
                    for tile in range(1, tiles):
                        here = here + (lows[tile] << (8 * tile))
                        nearby = nearby + (lows[tile + 1] << (8 * tile))
                    packed[epoch, rows] = here
                    near_packed[epoch, rows] = nearby
                return 0

            lax.fori_loop(0, reach // 8, quantize, 0)

    height = out_ref.shape[1]
    across = lax.broadcasted_iota(jnp.int32, (8, LANES), 1)
    least, unit = scale[0], scale[1]

    def one_velocity(local_index, _):
        start = (base + local_index) * epochs * 2
        rows = [shifts[start + 2 * epoch] + MAXS for epoch in range(epochs)]
        cols = [shifts[start + 2 * epoch + 1] + MAXS for epoch in range(epochs)]
        beyond = [across < col for col in cols]
        turn = [jnp.where(col == 0, 0, LANES - col) for col in cols]
        for top in range(0, height, 8):
            totals, low_total = [None] * tiles, None
            for epoch in range(epochs):
                here = pl.ds(rows[epoch] + top, 8)
                loaded = [whole[epoch, tile, here] for tile in range(count)]
                for tile in range(tiles):
                    moved = pltpu.roll(jnp.where(beyond[epoch], loaded[tile + 1], loaded[tile]), turn[epoch], 1)
                    totals[tile] = moved if epoch == 0 else totals[tile] + moved
                moved = pltpu.roll(jnp.where(beyond[epoch], near_packed[epoch, here], packed[epoch, here]), turn[epoch], 1)
                low_total = moved if epoch == 0 else low_total + moved
            for tile in range(tiles):
                psi = (totals[tile] >> 8).astype(jnp.float32)
                phi = (((totals[tile] & 255) << 6) + ((low_total >> (8 * tile)) & 255)).astype(jnp.float32)
                out_ref[local_index, top : top + 8, tile * LANES : (tile + 1) * LANES] = (
                    psi * unit * lax.rsqrt(jnp.maximum(phi, least))
                )
        return 0

    lax.fori_loop(0, group, one_velocity, 0, unroll=True)


def stack_blocks(place, shifts, floor, sources, out, out_shape, parts, blocks):
    epochs, kinds, tiles = sources[0][0].shape[1:4]
    velocities, height, columns = out_shape.shape
    group = next(size for size in (12, 9, 8, 6, 4, 3, 2, 1) if velocities % size == 0)
    width, reach = tiles * LANES, height + 2 * MAXS
    in_specs, operands = [], []
    for index, (array, slot) in enumerate(sources):
        depth = tiles if index % 6 < 3 else 1
        in_specs.append(
            pl.BlockSpec((1, epochs, kinds, depth, MAXS, LANES), functools.partial(lambda at, *_: (at, 0, 0, 0, 0, 0), slot))
        )
        operands.append(array)
    aliases = {}
    if out is not None:
        in_specs.append(pl.BlockSpec(memory_space=pl.ANY))
        operands.append(out)
        aliases = {3 + len(sources): 0}
    work = parts * velocities * height * width
    return pl.pallas_call(
        functools.partial(stack_kernel, group=group, parts=parts, blocks=blocks),
        grid_spec=pltpu.PrefetchScalarGridSpec(
            num_scalar_prefetch=3,
            grid=(parts, velocities // group),
            in_specs=in_specs,
            out_specs=pl.BlockSpec((group, height, width), lambda part, chunk, place, *_: (chunk, 0, place[part])),
            scratch_shapes=[
                pltpu.VMEM((epochs, kinds, tiles + 1, reach, LANES), jnp.float32),
                pltpu.VMEM((epochs, tiles + 1, reach, LANES), jnp.int32),
                pltpu.VMEM((epochs, reach, LANES), jnp.int32),
                pltpu.VMEM((epochs, reach, LANES), jnp.int32),
                pltpu.VMEM((2, 8, LANES), jnp.float32),
            ],
        ),
        out_shape=out_shape,
        input_output_aliases=aliases,
        compiler_params=pltpu.CompilerParams(vmem_limit_bytes=VMEM),
        cost_estimate=pl.CostEstimate(flops=16 * work, bytes_accessed=24 * work, transcendentals=work),
    )(place, shifts, floor, *operands)


def local(images, variance, spread_kernel, shifts, epoch_owner, valid_rows):
    exposure, noise_var = images[0], variance[0]
    height, columns = exposure.shape
    ksize = spread_kernel.shape[0]
    epochs = epoch_owner.shape[0]
    blocks = lax.axis_size("vel")
    width = columns // blocks
    me, lower = lax.axis_index("vel"), lax.axis_index("rows")
    swap = [(0, 1), (1, 0)]

    order = list(range(0, blocks, 2)) + list(range(1, blocks, 2))[::-1]
    right = [(order[i], order[(i + 1) % blocks]) for i in range(blocks)]
    left = [(b, a) for a, b in right]

    def position(index):
        return jnp.where(index % 2 == 0, index // 2, blocks - 1 - index // 2)

    mine = position(me)
    kernel_norm = spread_kernel / jnp.sum(spread_kernel)
    kernel_sq = kernel_norm * kernel_norm
    floor = (0.5 * jnp.sum(kernel_sq)).reshape(1)
    taps = jnp.stack([kernel_norm, kernel_sq]).reshape(-1)

    chunks = []
    for step in range(blocks):
        start = position(me ^ step) * width
        chunk = jnp.stack(
            [
                lax.dynamic_slice_in_dim(exposure, start, width, 1),
                lax.dynamic_slice_in_dim(noise_var, start, width, 1),
            ]
        )
        if step:
            chunk = lax.ppermute(chunk, "vel", [(i, i ^ step) for i in range(blocks)])
        if step == 1:
            chunk, taps = lax.optimization_barrier((chunk, taps))
        chunks.append(chunk)
    high, both = bands(taps, ksize)
    chunks[-1], high, both = lax.optimization_barrier((chunks[-1], high, both))
    row_ids = lower * height + jnp.arange(height, dtype=jnp.int32)[:, None]
    fields = []
    for epoch in range(epochs):
        key = epoch_owner[epoch] ^ me
        chosen = chunks[0]
        for step in range(1, blocks):
            chosen = jnp.where(key == step, chunks[step], chosen)
        usable = (row_ids >= valid_rows[epoch, 0]) & (row_ids < valid_rows[epoch, 1])
        fields.append(
            jnp.stack([jnp.where(usable, chosen[0] / chosen[1], 0.0), jnp.where(usable, 1.0 / chosen[1], 0.0)])
        )
    field = jnp.stack(fields)
    before = lax.ppermute(field[..., width - LANES :], "vel", right)
    wide = jnp.concatenate([before, field], axis=3)
    border = lax.ppermute(jnp.where(lower == 0, wide[:, :, height - MAXS :], wide[:, :, :MAXS]), "rows", swap)
    place = jnp.stack([mine, lower]).astype(jnp.int32)
    payload = correlate(place, wide, border, high, both)

    flat_shifts = shifts.reshape(-1)
    out_shape = jax.ShapeDtypeStruct((shifts.shape[0], height, columns), jnp.float32)
    border = lax.ppermute(payload[:1], "rows", swap)
    have = {0: ((payload, 0), (payload, 1), (border, 0))}
    behind = ahead = payload
    half = blocks // 2
    out = None
    for step in range(1, half + 1):
        if step < half:
            behind, ahead = lax.ppermute(behind, "vel", right), lax.ppermute(ahead, "vel", left)
            if out is not None:
                behind, ahead, out = lax.optimization_barrier((behind, ahead, out))
            border = lax.ppermute(jnp.concatenate([behind[:1], ahead[:1]]), "rows", swap)
            have[-step] = ((behind, 0), (behind, 1), (border, 0))
            have[step] = ((ahead, 0), (ahead, 1), (border, 1))
        else:
            edge, inner = lax.ppermute(behind[:1], "vel", right), lax.ppermute(ahead[1:], "vel", left)
            if out is not None:
                edge, inner, out = lax.optimization_barrier((edge, inner, out))
            border = lax.ppermute(edge, "rows", swap)
            have[step] = have[-step] = ((edge, 0), (inner, 0), (border, 0))
        now = [step - 1, -step]
        sources = []
        for offset in now:
            sources += list(have[offset]) + list(have[offset + 1])
        place = jnp.stack([(mine + offset) % blocks for offset in now] + [lower]).astype(jnp.int32)
        out = stack_blocks(place, flat_shifts, floor, sources, out, out_shape, len(now), blocks)
    return out


def solution(mesh):
    in_specs = (
        P(("fields", "vel"), "rows", None),
        P(("fields", "vel"), "rows", None),
        P(),
        P(("fields", "vel"), None, None),
        P("fields"),
        P("fields", None),
    )
    out_specs = P(("fields", "vel"), "rows", None)
    return jax.shard_map(local, mesh=mesh, in_specs=in_specs, out_specs=out_specs, check_vma=False)
```

```python
import functools
import jax
import jax.numpy as jnp
from jax import lax
from jax.experimental import pallas as pl
from jax.experimental.pallas import tpu as pltpu
from jax.sharding import PartitionSpec as P

LANES = 128
MAXS = 16
VMEM = 24 << 20


def band_kernel(taps, kernel, bands_ref, floor_ref):
    ksize = kernel.shape[0]
    skip = LANES - MAXS - ksize // 2
    top = skip // 8 * 8
    shape = (2 * LANES - top, LANES)
    offset = lax.broadcasted_iota(jnp.int32, shape, 0) - lax.broadcasted_iota(jnp.int32, shape, 1) + (top - skip)
    total = jnp.full((8, LANES), jnp.sum(kernel[...]), jnp.float32)
    norm = kernel[...] / total[:1, :1]
    floor_ref[...] = jnp.full(floor_ref.shape, 0.5 * jnp.sum(norm * norm), jnp.float32)
    bands_ref[:, :, :top] = jnp.zeros(bands_ref.shape[:2] + (top, 2 * LANES), jnp.bfloat16)

    def one(row, _):
        band = jnp.zeros(shape, jnp.float32)
        for col in range(ksize):
            band = jnp.where(offset == col, taps[row * ksize + col], band)
        band = band / total[:1]
        for kind, value in enumerate((band, band * band)):
            high = value.astype(jnp.bfloat16)
            bands_ref[kind, row, top:, :LANES] = high
            bands_ref[kind, row, top:, LANES:] = (value - high.astype(jnp.float32)).astype(jnp.bfloat16)
        return 0

    lax.fori_loop(0, ksize, one, 0)


def make_bands(spread_kernel):
    ksize = spread_kernel.shape[0]
    return pl.pallas_call(
        band_kernel,
        in_specs=[pl.BlockSpec(memory_space=pltpu.SMEM), pl.BlockSpec(memory_space=pltpu.VMEM)],
        out_specs=[pl.BlockSpec(memory_space=pltpu.VMEM)] * 2,
        out_shape=[
            jax.ShapeDtypeStruct((2, ksize, 2 * LANES, 2 * LANES), jnp.bfloat16),
            jax.ShapeDtypeStruct((8, LANES), jnp.float32),
        ],
        compiler_params=pltpu.CompilerParams(vmem_limit_bytes=VMEM),
        cost_estimate=pl.CostEstimate(flops=0, bytes_accessed=20 << 20, transcendentals=0),
    )(spread_kernel.reshape(-1), spread_kernel)


def cut_kernel(starts, exposure, noise_var, *chunk_refs):
    for index, ref in enumerate(chunk_refs):
        columns = pl.ds(pl.multiple_of(starts[index], LANES), ref.shape[2])
        ref[0] = exposure[:, columns]
        ref[1] = noise_var[:, columns]


def cut(starts, exposure, noise_var, blocks):
    height, columns = exposure.shape
    return pl.pallas_call(
        cut_kernel,
        in_specs=[pl.BlockSpec(memory_space=pltpu.SMEM)] + [pl.BlockSpec(memory_space=pltpu.VMEM)] * 2,
        out_specs=[pl.BlockSpec(memory_space=pltpu.VMEM)] * blocks,
        out_shape=[jax.ShapeDtypeStruct((2, height, columns // blocks), jnp.float32)] * blocks,
        compiler_params=pltpu.CompilerParams(vmem_limit_bytes=VMEM),
        cost_estimate=pl.CostEstimate(flops=0, bytes_accessed=16 * height * columns, transcendentals=0),
    )(starts, exposure, noise_var)


def pick_kernel(place, owner, valid, *refs):
    chunks, (own, last, edges, corner, chosen) = refs[:-5], refs[-5:]
    epochs, _, tiles, height, _ = own.shape
    me, lower = place[0], place[1]
    for epoch in range(epochs):
        for step, chunk in enumerate(chunks):

            @pl.when(owner[epoch] ^ me == step)
            def _():
                chosen[epoch] = chunk[...]

    row_ids = lower * height + lax.broadcasted_iota(jnp.int32, (height, LANES), 0)
    for epoch in range(epochs):
        usable = jnp.logical_and(row_ids >= valid[2 * epoch], row_ids < valid[2 * epoch + 1])
        for tile in range(tiles):
            columns = slice(tile * LANES, (tile + 1) * LANES)
            inverse = jnp.where(usable, 1.0 / chosen[epoch, 1, :, columns], 0.0)
            weighted = jnp.where(usable, chosen[epoch, 0, :, columns] / chosen[epoch, 1, :, columns], 0.0)
            own[epoch, 0, tile] = weighted
            own[epoch, 1, tile] = inverse
    rows = pl.ds(pl.multiple_of((1 - lower) * (height - MAXS), MAXS), MAXS)
    edges[...] = own[:, :, :, rows]
    last[...] = own[:, :, tiles - 1]
    corner[...] = own[:, :, tiles - 1, rows]


def pick(place, owner, valid, chunks):
    _, height, width = chunks[0].shape
    epochs, tiles = owner.shape[0], width // LANES
    shapes = [(tiles, height), (height,), (tiles, MAXS), (MAXS,)]
    return pl.pallas_call(
        pick_kernel,
        in_specs=[pl.BlockSpec(memory_space=pltpu.SMEM)] * 3 + [pl.BlockSpec(memory_space=pltpu.VMEM)] * len(chunks),
        out_specs=[pl.BlockSpec(memory_space=pltpu.VMEM)] * 4,
        out_shape=[jax.ShapeDtypeStruct((epochs, 2) + shape + (LANES,), jnp.float32) for shape in shapes],
        scratch_shapes=[pltpu.VMEM((epochs, 2, height, width), jnp.float32)],
        compiler_params=pltpu.CompilerParams(vmem_limit_bytes=VMEM),
        cost_estimate=pl.CostEstimate(flops=0, bytes_accessed=4 << 20, transcendentals=0),
    )(place, owner, valid.reshape(-1), *chunks)


def correlate_kernel(place, own, before, border, corner, bands_ref, rows_ref, ext, high, low, summed):
    epochs, kinds, tiles, height, _ = own.shape
    ksize = bands_ref.shape[1]
    members = high.shape[2] // (height + 2 * MAXS)
    first, lower = place[0] == 0, place[1]
    at_border = (1 - lower) * (MAXS + height)
    summed_rows = height * members
    blank = pl.ds(pl.multiple_of(lower * (MAXS + height) * members, 8), MAXS * members)
    ext[:, :, blank] = jnp.zeros((kinds, 2, MAXS * members, LANES), jnp.float32)
    nothing = jnp.zeros((height, LANES), jnp.float32)
    keep = jnp.where(first, 0.0, 1.0)

    def put(kind, half, member, value, beyond):
        ext[kind, half, pl.ds(MAXS * members + member, height, stride=members)] = value
        ext[kind, half, pl.ds(at_border * members + member, MAXS, stride=members)] = beyond

    for epoch in range(epochs):
        base = epoch * (tiles + 1)
        for kind in range(kinds):
            for tile in range(tiles):
                put(kind, 1, base + tile, own[epoch, kind, tile], border[epoch, kind, tile])
                if tile + 1 < tiles:
                    put(kind, 0, base + tile + 1, own[epoch, kind, tile], border[epoch, kind, tile])
            put(kind, 0, base, before[epoch, kind] * keep, corner[epoch, kind] * keep)
            put(kind, 0, base + tiles, before[epoch, kind], corner[epoch, kind])
            put(kind, 1, base + tiles, nothing, nothing[:MAXS])

    def split(index, _):
        rows = pl.ds(pl.multiple_of(index * 128, 128), 128)
        for kind in range(kinds):
            for half in range(2):
                value = ext[kind, half, rows]
                part = value.astype(jnp.bfloat16)
                high[kind, half, rows] = part
                low[kind, half, rows] = (value - part.astype(jnp.float32)).astype(jnp.bfloat16)
        return 0

    lax.fori_loop(0, ext.shape[2] // 128, split, 0)

    lane = lax.broadcasted_iota(jnp.int32, (MAXS, LANES), 1)
    wrapped = jnp.logical_and(first, lane < MAXS)
    for kind in range(kinds):
        offsets = [pl.ds((row + MAXS - ksize // 2) * members, summed_rows) for row in range(ksize)]
        upper = jnp.concatenate([high[kind, half, rows] for rows in offsets for half in range(2)], axis=1)
        rest = jnp.concatenate([low[kind, half, rows] for rows in offsets for half in range(2)], axis=1)
        weights = bands_ref[kind].reshape(ksize * 2 * LANES, 2 * LANES)
        pair = jnp.dot(upper, weights, preferred_element_type=jnp.float32)
        more = jnp.dot(rest, weights[:, :LANES], preferred_element_type=jnp.float32)
        summed[...] = pair[:, :LANES] + (pair[:, LANES:] + more)
        for half in range(2):
            start = (1 - lower if half == 0 else lower) * (height - MAXS)
            for epoch in range(epochs):
                base = epoch * (tiles + 1)

                def rows_of(tile):
                    return summed[pl.ds(start * members + base + tile, MAXS, stride=members)]

                rows_ref[half, epoch, kind, 0] = jnp.where(wrapped, rows_of(tiles), rows_of(0))
                for tile in range(1, tiles):
                    rows_ref[half, epoch, kind, tile] = rows_of(tile)


def correlate(place, own, before, border, corner, bands):
    epochs, kinds, tiles, height, _ = own.shape
    members = -(-epochs * (tiles + 1) // 16) * 16
    depth = (height + 2 * MAXS) * members
    flops = 2 * 2 * kinds * members * height * bands.shape[1] * 4 * LANES * LANES
    return pl.pallas_call(
        correlate_kernel,
        in_specs=[pl.BlockSpec(memory_space=pltpu.SMEM)] + [pl.BlockSpec(memory_space=pltpu.VMEM)] * 5,
        out_specs=pl.BlockSpec(memory_space=pltpu.VMEM),
        out_shape=jax.ShapeDtypeStruct((2, epochs, kinds, tiles, MAXS, LANES), jnp.float32),
        scratch_shapes=[
            pltpu.VMEM((kinds, 2, depth, LANES), jnp.float32),
            pltpu.VMEM((kinds, 2, depth, LANES), jnp.bfloat16),
            pltpu.VMEM((kinds, 2, depth, LANES), jnp.bfloat16),
            pltpu.VMEM((height * members, LANES), jnp.float32),
        ],
        compiler_params=pltpu.CompilerParams(vmem_limit_bytes=VMEM),
        cost_estimate=pl.CostEstimate(flops=flops, bytes_accessed=12 << 20, transcendentals=0),
    )(place, own, before, border, corner, bands)


def stack_kernel(place, shifts, floor, *refs, group, parts, blocks):
    sources, out_ref = refs[: 6 * parts], refs[-6]
    raw, whole, packed, near_packed, scale = refs[-5:]
    part, base = pl.program_id(0), pl.program_id(1) * group
    epochs, count, reach = whole.shape[:3]
    tiles = count - 1
    lower = place[parts]
    lane = lax.broadcasted_iota(jnp.int32, (1, LANES), 1)
    at = [pl.multiple_of(row, MAXS) for row in (32 - 16 * lower, 16 + 16 * lower, 48 - 48 * lower)]
    blank = pl.multiple_of(48 * lower, MAXS)
    most_psi = ((1 << 23) - 1) // epochs
    most_high = 255 // epochs
    most_phi = most_high * 64 + 63

    for index in range(parts):

        @pl.when(jnp.logical_and(part == index, pl.program_id(1) == 0))
        def _():
            block = place[index]
            keep_first = jnp.where(jnp.logical_and(block == 0, lane < MAXS), 0.0, 1.0) > 0.5
            keep_last = jnp.where(jnp.logical_and(block == blocks - 1, lane >= MAXS), 0.0, 1.0) > 0.5
            for epoch in range(epochs):
                for kind in range(2):
                    for tile in range(count):
                        raw[epoch, kind, tile, pl.ds(blank, MAXS)] = jnp.zeros((MAXS, LANES), jnp.float32)
            tops = [jnp.zeros((MAXS, LANES), jnp.float32) for _ in range(2)]
            for piece in range(3):
                own, nearby = sources[6 * index + piece], sources[6 * index + 3 + piece]
                rows = pl.ds(at[piece], MAXS)
                for epoch in range(epochs):
                    for kind in range(2):
                        for tile in range(count):
                            if tile == tiles:
                                value = jnp.where(keep_last, nearby[0, epoch, kind, 0], 0.0)
                            elif tile == 0:
                                value = jnp.where(keep_first, own[0, epoch, kind, 0], 0.0)
                            else:
                                value = own[0, epoch, kind, tile]
                            tops[kind] = jnp.maximum(tops[kind], jnp.abs(value))
                            raw[epoch, kind, tile, rows] = value
            tops = [jnp.full((8, LANES), jnp.maximum(jnp.max(top), 1e-30), jnp.float32) for top in tops]
            per_psi, per_phi = most_psi / tops[0], most_phi / tops[1]
            scale[0] = floor[0] * per_phi
            scale[1] = jnp.sqrt(per_phi) / per_psi

            def quantize(index, _):
                rows = pl.ds(pl.multiple_of(index * 8, 8), 8)
                for epoch in range(epochs):
                    lows = []
                    for tile in range(count):
                        psi = jnp.floor(raw[epoch, 0, tile, rows] * per_psi + 0.5).astype(jnp.int32)
                        phi = jnp.floor(jnp.maximum(raw[epoch, 1, tile, rows], 0.0) * per_phi + 0.5).astype(jnp.int32)
                        psi = jnp.clip(psi, -most_psi, most_psi)
                        phi = jnp.minimum(phi, most_phi)
                        whole[epoch, tile, rows] = psi * 256 + (phi >> 6)
                        lows.append(phi & 63)
                    here, nearby = lows[0], lows[1]
                    for tile in range(1, tiles):
                        here = here + (lows[tile] << (8 * tile))
                        nearby = nearby + (lows[tile + 1] << (8 * tile))
                    packed[epoch, rows] = here
                    near_packed[epoch, rows] = nearby
                return 0

            lax.fori_loop(0, reach // 8, quantize, 0)

    height = out_ref.shape[1]
    across = lax.broadcasted_iota(jnp.int32, (8, LANES), 1)
    least, unit = scale[0], scale[1]

    def one_velocity(local_index, _):
        start = (base + local_index) * epochs * 2
        rows = [shifts[start + 2 * epoch] + MAXS for epoch in range(epochs)]
        cols = [shifts[start + 2 * epoch + 1] + MAXS for epoch in range(epochs)]
        beyond = [across < col for col in cols]
        turn = [jnp.where(col == 0, 0, LANES - col) for col in cols]
        for top in range(0, height, 8):
            totals, low_total = [None] * tiles, None
            for epoch in range(epochs):
                here = pl.ds(rows[epoch] + top, 8)
                loaded = [whole[epoch, tile, here] for tile in range(count)]
                for tile in range(tiles):
                    moved = pltpu.roll(jnp.where(beyond[epoch], loaded[tile + 1], loaded[tile]), turn[epoch], 1)
                    totals[tile] = moved if epoch == 0 else totals[tile] + moved
                moved = pltpu.roll(jnp.where(beyond[epoch], near_packed[epoch, here], packed[epoch, here]), turn[epoch], 1)
                low_total = moved if epoch == 0 else low_total + moved
            for tile in range(tiles):
                psi = (totals[tile] >> 8).astype(jnp.float32)
                phi = (((totals[tile] & 255) << 6) + ((low_total >> (8 * tile)) & 255)).astype(jnp.float32)
                out_ref[local_index, top : top + 8, tile * LANES : (tile + 1) * LANES] = (
                    psi * unit * lax.rsqrt(jnp.maximum(phi, least))
                )
        return 0

    lax.fori_loop(0, group, one_velocity, 0, unroll=True)


def stack_blocks(place, shifts, floor, sources, out, out_shape, parts, blocks):
    epochs, kinds, tiles = sources[0][0].shape[1:4]
    velocities, height, columns = out_shape.shape
    group = next(size for size in (12, 9, 8, 6, 4, 3, 2, 1) if velocities % size == 0)
    width, reach = tiles * LANES, height + 2 * MAXS
    in_specs, operands = [], []
    for index, (array, slot) in enumerate(sources):
        depth = tiles if index % 6 < 3 else 1
        in_specs.append(
            pl.BlockSpec((1, epochs, kinds, depth, MAXS, LANES), functools.partial(lambda at, *_: (at, 0, 0, 0, 0, 0), slot))
        )
        operands.append(array)
    aliases = {}
    if out is not None:
        in_specs.append(pl.BlockSpec(memory_space=pl.ANY))
        operands.append(out)
        aliases = {3 + len(sources): 0}
    work = parts * velocities * height * width
    return pl.pallas_call(
        functools.partial(stack_kernel, group=group, parts=parts, blocks=blocks),
        grid_spec=pltpu.PrefetchScalarGridSpec(
            num_scalar_prefetch=3,
            grid=(parts, velocities // group),
            in_specs=in_specs,
            out_specs=pl.BlockSpec((group, height, width), lambda part, chunk, place, *_: (chunk, 0, place[part])),
            scratch_shapes=[
                pltpu.VMEM((epochs, kinds, tiles + 1, reach, LANES), jnp.float32),
                pltpu.VMEM((epochs, tiles + 1, reach, LANES), jnp.int32),
                pltpu.VMEM((epochs, reach, LANES), jnp.int32),
                pltpu.VMEM((epochs, reach, LANES), jnp.int32),
                pltpu.VMEM((2, 8, LANES), jnp.float32),
            ],
        ),
        out_shape=out_shape,
        input_output_aliases=aliases,
        compiler_params=pltpu.CompilerParams(vmem_limit_bytes=VMEM),
        cost_estimate=pl.CostEstimate(flops=16 * work, bytes_accessed=24 * work, transcendentals=work),
    )(place, shifts, floor, *operands)


def local(images, variance, spread_kernel, shifts, epoch_owner, valid_rows):
    exposure, noise_var = images[0], variance[0]
    height, columns = exposure.shape
    blocks = lax.axis_size("vel")
    width = columns // blocks
    me, lower = lax.axis_index("vel"), lax.axis_index("rows")
    swap = [(0, 1), (1, 0)]

    order = list(range(0, blocks, 2)) + list(range(1, blocks, 2))[::-1]
    right = [(order[i], order[(i + 1) % blocks]) for i in range(blocks)]
    left = [(b, a) for a, b in right]

    def position(index):
        return jnp.where(index % 2 == 0, index // 2, blocks - 1 - index // 2)

    mine = position(me)
    place = jnp.stack([mine, lower]).astype(jnp.int32)

    starts = position(me ^ jnp.arange(blocks, dtype=jnp.int32)) * width
    chunks = list(cut(starts, exposure, noise_var, blocks))
    for step in range(1, blocks):
        chunks[step] = lax.ppermute(chunks[step], "vel", [(i, i ^ step) for i in range(blocks)])
    chunks[1], spread_kernel = lax.optimization_barrier((chunks[1], spread_kernel))
    bands, floor = make_bands(spread_kernel)
    chunks[-1], bands = lax.optimization_barrier((chunks[-1], bands))
    spot = jnp.stack([me, lower]).astype(jnp.int32)
    own, last, edges, corner = pick(spot, epoch_owner, valid_rows, chunks)
    pairs = lax.axis_size("rows")
    diagonal = [(a * pairs + r, b * pairs + 1 - r) for a, b in right for r in range(pairs)]
    before = lax.ppermute(last, "vel", right)
    corner = lax.ppermute(corner, ("vel", "rows"), diagonal)
    border = lax.ppermute(edges, "rows", swap)
    payload = correlate(place, own, before, border, corner, bands)

    flat_shifts, floor = shifts.reshape(-1), floor[0, :1]
    out_shape = jax.ShapeDtypeStruct((shifts.shape[0], height, columns), jnp.float32)
    border = lax.ppermute(payload[:1], "rows", swap)
    have = {0: ((payload, 0), (payload, 1), (border, 0))}
    behind = ahead = payload
    half = blocks // 2
    out = None
    for step in range(1, half + 1):
        if step < half:
            behind, ahead = lax.ppermute(behind, "vel", right), lax.ppermute(ahead, "vel", left)
            if out is not None:
                behind, ahead, out = lax.optimization_barrier((behind, ahead, out))
            border = lax.ppermute(jnp.concatenate([behind[:1], ahead[:1]]), "rows", swap)
            have[-step] = ((behind, 0), (behind, 1), (border, 0))
            have[step] = ((ahead, 0), (ahead, 1), (border, 1))
        else:
            edge, inner = lax.ppermute(behind[:1], "vel", right), lax.ppermute(ahead[1:], "vel", left)
            if out is not None:
                edge, inner, out = lax.optimization_barrier((edge, inner, out))
            border = lax.ppermute(edge, "rows", swap)
            have[step] = have[-step] = ((edge, 0), (inner, 0), (border, 0))
        now = [step - 1, -step]
        sources = []
        for offset in now:
            sources += list(have[offset]) + list(have[offset + 1])
        place = jnp.stack([(mine + offset) % blocks for offset in now] + [lower]).astype(jnp.int32)
        out = stack_blocks(place, flat_shifts, floor, sources, out, out_shape, len(now), blocks)
    return out


def solution(mesh):
    in_specs = (
        P(("fields", "vel"), "rows", None),
        P(("fields", "vel"), "rows", None),
        P(),
        P(("fields", "vel"), None, None),
        P("fields"),
        P("fields", None),
    )
    out_specs = P(("fields", "vel"), "rows", None)
    return jax.shard_map(local, mesh=mesh, in_specs=in_specs, out_specs=out_specs, check_vma=False)
```

```python
import functools
import jax
import jax.numpy as jnp
from jax import lax
from jax.experimental import pallas as pl
from jax.experimental.pallas import tpu as pltpu
from jax.sharding import PartitionSpec as P

LANES = 128
MAXS = 16
HALO = 32
VMEM = 24 << 20


def band_kernel(taps, kernel, bands_ref, floor_ref):
    ksize = kernel.shape[0]
    skip = LANES - MAXS - ksize // 2
    top = skip // 8 * 8
    shape = (2 * LANES - top, LANES)
    offset = lax.broadcasted_iota(jnp.int32, shape, 0) - lax.broadcasted_iota(jnp.int32, shape, 1) + (top - skip)
    total = jnp.full((8, LANES), jnp.sum(kernel[...]), jnp.float32)
    norm = kernel[...] / total[:1, :1]
    floor_ref[...] = jnp.full(floor_ref.shape, 0.5 * jnp.sum(norm * norm), jnp.float32)
    bands_ref[:, :, :top] = jnp.zeros(bands_ref.shape[:2] + (top, 2 * LANES), jnp.bfloat16)

    def one(row, _):
        band = jnp.zeros(shape, jnp.float32)
        for col in range(ksize):
            band = jnp.where(offset == col, taps[row * ksize + col], band)
        band = band / total[:1]
        for kind, value in enumerate((band, band * band)):
            high = value.astype(jnp.bfloat16)
            bands_ref[kind, row, top:, :LANES] = high
            bands_ref[kind, row, top:, LANES:] = (value - high.astype(jnp.float32)).astype(jnp.bfloat16)
        return 0

    lax.fori_loop(0, ksize, one, 0)


def make_bands(spread_kernel):
    ksize = spread_kernel.shape[0]
    return pl.pallas_call(
        band_kernel,
        in_specs=[pl.BlockSpec(memory_space=pltpu.SMEM), pl.BlockSpec(memory_space=pltpu.VMEM)],
        out_specs=[pl.BlockSpec(memory_space=pltpu.VMEM)] * 2,
        out_shape=[
            jax.ShapeDtypeStruct((2, ksize, 2 * LANES, 2 * LANES), jnp.bfloat16),
            jax.ShapeDtypeStruct((8, LANES), jnp.float32),
        ],
        compiler_params=pltpu.CompilerParams(vmem_limit_bytes=VMEM),
        cost_estimate=pl.CostEstimate(flops=0, bytes_accessed=20 << 20, transcendentals=0),
    )(spread_kernel.reshape(-1), spread_kernel)


def cut_kernel(starts, exposure, noise_var, *refs):
    chunk_refs, (held, arrived) = refs[:-2], refs[-2:]
    _, height, columns = held.shape
    tiles = columns // len(chunk_refs) // LANES
    copies = []
    for kind, source in enumerate((exposure, noise_var)):
        for top in range(0, height, 8):
            copies.append(
                pltpu.make_async_copy(
                    source.at[pl.ds(top, 8)], held.at[kind, pl.ds(top, 8)], arrived.at[kind, top // 8]
                )
            )
            copies[-1].start()
    for copy in copies:
        copy.wait()
    lane = lax.broadcasted_iota(jnp.int32, (8, LANES), 1)
    for index, ref in enumerate(chunk_refs):
        start = starts[index]
        ahead = jnp.where(start == 0, columns, start) - LANES
        for kind in range(2):
            for tile in range(tiles):
                at = pl.multiple_of(start + tile * LANES, LANES)
                ref[kind, tile * height : (tile + 1) * height] = held[kind, :, pl.ds(at, LANES)]
            halo = jnp.zeros((8, LANES), jnp.float32)
            for group in range(LANES // HALO):
                rows = held[kind, 8 * group : 8 * group + 8, pl.ds(pl.multiple_of(ahead, LANES), LANES)]
                moved = pltpu.roll(rows, (group + 1) * HALO % LANES, 1)
                halo = jnp.where(lane // HALO == group, moved, halo)
            ref[kind, tiles * height :] = halo


def cut(starts, exposure, noise_var, blocks):
    height, columns = exposure.shape
    rows = columns // blocks // LANES * height + height * HALO // LANES
    return pl.pallas_call(
        cut_kernel,
        in_specs=[pl.BlockSpec(memory_space=pltpu.SMEM)] + [pl.BlockSpec(memory_space=pltpu.HBM)] * 2,
        out_specs=[pl.BlockSpec(memory_space=pltpu.VMEM)] * blocks,
        out_shape=[jax.ShapeDtypeStruct((2, rows, LANES), jnp.float32)] * blocks,
        scratch_shapes=[pltpu.VMEM((2, height, columns), jnp.float32), pltpu.SemaphoreType.DMA((2, height // 8))],
        compiler_params=pltpu.CompilerParams(vmem_limit_bytes=VMEM),
        cost_estimate=pl.CostEstimate(flops=0, bytes_accessed=16 * height * columns, transcendentals=0),
    )(starts, exposure, noise_var)


def pick_kernel(place, owner, valid, *refs):
    chunks, (own, edges, chosen) = refs[:-3], refs[-3:]
    epochs, _, count, height, _ = own.shape
    tiles = count - 1
    me, lower = place[0], place[1]
    for epoch in range(epochs):
        for step, chunk in enumerate(chunks):

            @pl.when(owner[epoch] ^ me == step)
            def _():
                chosen[epoch] = chunk[...]

    row_ids = lower * height + lax.broadcasted_iota(jnp.int32, (height, LANES), 0)
    behind = lax.broadcasted_iota(jnp.int32, (8, LANES), 1) >= LANES - HALO
    for epoch in range(epochs):
        usable = jnp.logical_and(row_ids >= valid[2 * epoch], row_ids < valid[2 * epoch + 1])
        for tile in range(count):
            if tile:
                value, noise = (chosen[epoch, kind, (tile - 1) * height : tile * height] for kind in range(2))
            else:
                packed = [chosen[epoch, kind, tiles * height :] for kind in range(2)]
                spread = [
                    jnp.concatenate(
                        [
                            jnp.where(behind, pltpu.roll(rows, (LANES - (group + 1) * HALO) % LANES, 1), fill)
                            for group in range(LANES // HALO)
                        ],
                        axis=0,
                    )
                    for rows, fill in zip(packed, (0.0, 1.0))
                ]
                value, noise = spread
            own[epoch, 0, tile] = jnp.where(usable, value / noise, 0.0)
            own[epoch, 1, tile] = jnp.where(usable, 1.0 / noise, 0.0)
    edges[...] = own[:, :, :, pl.ds(pl.multiple_of((1 - lower) * (height - MAXS), MAXS), MAXS)]


def pick(place, owner, valid, chunks, height):
    rows = chunks[0].shape[1]
    epochs, tiles = owner.shape[0], (rows - height * HALO // LANES) // height
    return pl.pallas_call(
        pick_kernel,
        in_specs=[pl.BlockSpec(memory_space=pltpu.SMEM)] * 3 + [pl.BlockSpec(memory_space=pltpu.VMEM)] * len(chunks),
        out_specs=[pl.BlockSpec(memory_space=pltpu.VMEM)] * 2,
        out_shape=[
            jax.ShapeDtypeStruct((epochs, 2, tiles + 1, depth, LANES), jnp.float32) for depth in (height, MAXS)
        ],
        scratch_shapes=[pltpu.VMEM((epochs, 2, rows, LANES), jnp.float32)],
        compiler_params=pltpu.CompilerParams(vmem_limit_bytes=VMEM),
        cost_estimate=pl.CostEstimate(flops=0, bytes_accessed=4 << 20, transcendentals=0),
    )(place, owner, valid.reshape(-1), *chunks)


def correlate_kernel(place, own, border, bands_ref, rows_ref, ext, high, low, summed):
    epochs, kinds, count, height, _ = own.shape
    tiles = count - 1
    ksize = bands_ref.shape[1]
    members = high.shape[2] // (height + 2 * MAXS)
    first, lower = place[0] == 0, place[1]
    at_border = (1 - lower) * (MAXS + height)
    summed_rows = height * members
    blank = pl.ds(pl.multiple_of(lower * (MAXS + height) * members, 8), MAXS * members)
    ext[:, :, blank] = jnp.zeros((kinds, 2, MAXS * members, LANES), jnp.float32)
    nothing = jnp.zeros((height, LANES), jnp.float32)
    keep = jnp.where(first, 0.0, 1.0)

    def put(kind, half, member, value, beyond):
        ext[kind, half, pl.ds(MAXS * members + member, height, stride=members)] = value
        ext[kind, half, pl.ds(at_border * members + member, MAXS, stride=members)] = beyond

    for epoch in range(epochs):
        base = epoch * (tiles + 1)
        for kind in range(kinds):
            for tile in range(1, count):
                put(kind, 1, base + tile - 1, own[epoch, kind, tile], border[epoch, kind, tile])
                if tile < tiles:
                    put(kind, 0, base + tile, own[epoch, kind, tile], border[epoch, kind, tile])
            put(kind, 0, base, own[epoch, kind, 0] * keep, border[epoch, kind, 0] * keep)
            put(kind, 0, base + tiles, own[epoch, kind, 0], border[epoch, kind, 0])
            put(kind, 1, base + tiles, nothing, nothing[:MAXS])

    def split(index, _):
        rows = pl.ds(pl.multiple_of(index * 128, 128), 128)
        for kind in range(kinds):
            for half in range(2):
                value = ext[kind, half, rows]
                part = value.astype(jnp.bfloat16)
                high[kind, half, rows] = part
                low[kind, half, rows] = (value - part.astype(jnp.float32)).astype(jnp.bfloat16)
        return 0

    lax.fori_loop(0, ext.shape[2] // 128, split, 0)

    lane = lax.broadcasted_iota(jnp.int32, (MAXS, LANES), 1)
    wrapped = jnp.logical_and(first, lane < MAXS)
    for kind in range(kinds):
        offsets = [pl.ds((row + MAXS - ksize // 2) * members, summed_rows) for row in range(ksize)]
        upper = jnp.concatenate([high[kind, half, rows] for rows in offsets for half in range(2)], axis=1)
        rest = jnp.concatenate([low[kind, half, rows] for rows in offsets for half in range(2)], axis=1)
        weights = bands_ref[kind].reshape(ksize * 2 * LANES, 2 * LANES)
        pair = jnp.dot(upper, weights, preferred_element_type=jnp.float32)
        more = jnp.dot(rest, weights[:, :LANES], preferred_element_type=jnp.float32)
        summed[...] = pair[:, :LANES] + (pair[:, LANES:] + more)
        for half in range(2):
            start = (1 - lower if half == 0 else lower) * (height - MAXS)
            for epoch in range(epochs):
                base = epoch * (tiles + 1)

                def rows_of(tile):
                    return summed[pl.ds(start * members + base + tile, MAXS, stride=members)]

                rows_ref[half, epoch, kind, 0] = jnp.where(wrapped, rows_of(tiles), rows_of(0))
                for tile in range(1, tiles):
                    rows_ref[half, epoch, kind, tile] = rows_of(tile)


def correlate(place, own, border, bands):
    epochs, kinds, count, height, _ = own.shape
    tiles = count - 1
    members = -(-epochs * (tiles + 1) // 16) * 16
    depth = (height + 2 * MAXS) * members
    flops = 2 * 2 * kinds * members * height * bands.shape[1] * 4 * LANES * LANES
    return pl.pallas_call(
        correlate_kernel,
        in_specs=[pl.BlockSpec(memory_space=pltpu.SMEM)] + [pl.BlockSpec(memory_space=pltpu.VMEM)] * 3,
        out_specs=pl.BlockSpec(memory_space=pltpu.VMEM),
        out_shape=jax.ShapeDtypeStruct((2, epochs, kinds, tiles, MAXS, LANES), jnp.float32),
        scratch_shapes=[
            pltpu.VMEM((kinds, 2, depth, LANES), jnp.float32),
            pltpu.VMEM((kinds, 2, depth, LANES), jnp.bfloat16),
            pltpu.VMEM((kinds, 2, depth, LANES), jnp.bfloat16),
            pltpu.VMEM((height * members, LANES), jnp.float32),
        ],
        compiler_params=pltpu.CompilerParams(vmem_limit_bytes=VMEM),
        cost_estimate=pl.CostEstimate(flops=flops, bytes_accessed=12 << 20, transcendentals=0),
    )(place, own, border, bands)


def stack_kernel(place, shifts, floor, *refs, group, parts, blocks):
    sources, out_ref = refs[: 6 * parts], refs[-6]
    raw, whole, packed, near_packed, scale = refs[-5:]
    part, base = pl.program_id(0), pl.program_id(1) * group
    epochs, count, reach = whole.shape[:3]
    tiles = count - 1
    lower = place[parts]
    lane = lax.broadcasted_iota(jnp.int32, (1, LANES), 1)
    at = [pl.multiple_of(row, MAXS) for row in (32 - 16 * lower, 16 + 16 * lower, 48 - 48 * lower)]
    blank = pl.multiple_of(48 * lower, MAXS)
    most_psi = ((1 << 23) - 1) // epochs
    most_high = 255 // epochs
    most_phi = most_high * 64 + 63

    for index in range(parts):

        @pl.when(jnp.logical_and(part == index, pl.program_id(1) == 0))
        def _():
            block = place[index]
            keep_first = jnp.where(jnp.logical_and(block == 0, lane < MAXS), 0.0, 1.0) > 0.5
            keep_last = jnp.where(jnp.logical_and(block == blocks - 1, lane >= MAXS), 0.0, 1.0) > 0.5
            for epoch in range(epochs):
                for kind in range(2):
                    for tile in range(count):
                        raw[epoch, kind, tile, pl.ds(blank, MAXS)] = jnp.zeros((MAXS, LANES), jnp.float32)
            tops = [jnp.zeros((MAXS, LANES), jnp.float32) for _ in range(2)]
            for piece in range(3):
                own, nearby = sources[6 * index + piece], sources[6 * index + 3 + piece]
                rows = pl.ds(at[piece], MAXS)
                for epoch in range(epochs):
                    for kind in range(2):
                        for tile in range(count):
                            if tile == tiles:
                                value = jnp.where(keep_last, nearby[0, epoch, kind, 0], 0.0)
                            elif tile == 0:
                                value = jnp.where(keep_first, own[0, epoch, kind, 0], 0.0)
                            else:
                                value = own[0, epoch, kind, tile]
                            tops[kind] = jnp.maximum(tops[kind], jnp.abs(value))
                            raw[epoch, kind, tile, rows] = value
            tops = [jnp.full((8, LANES), jnp.maximum(jnp.max(top), 1e-30), jnp.float32) for top in tops]
            per_psi, per_phi = most_psi / tops[0], most_phi / tops[1]
            scale[0] = floor[0] * per_phi
            scale[1] = jnp.sqrt(per_phi) / per_psi

            def quantize(index, _):
                rows = pl.ds(pl.multiple_of(index * 8, 8), 8)
                for epoch in range(epochs):
                    lows = []
                    for tile in range(count):
                        psi = jnp.floor(raw[epoch, 0, tile, rows] * per_psi + 0.5).astype(jnp.int32)
                        phi = jnp.floor(jnp.maximum(raw[epoch, 1, tile, rows], 0.0) * per_phi + 0.5).astype(jnp.int32)
                        psi = jnp.clip(psi, -most_psi, most_psi)
                        phi = jnp.minimum(phi, most_phi)
                        whole[epoch, tile, rows] = psi * 256 + (phi >> 6)
                        lows.append(phi & 63)
                    here, nearby = lows[0], lows[1]
                    for tile in range(1, tiles):
                        here = here + (lows[tile] << (8 * tile))
                        nearby = nearby + (lows[tile + 1] << (8 * tile))
                    packed[epoch, rows] = here
                    near_packed[epoch, rows] = nearby
                return 0

            lax.fori_loop(0, reach // 8, quantize, 0, unroll=4)

    height = out_ref.shape[1]
    across = lax.broadcasted_iota(jnp.int32, (8, LANES), 1)
    least, unit = scale[0], scale[1]

    def one_velocity(local_index, _):
        start = (base + local_index) * epochs * 2
        rows = [shifts[start + 2 * epoch] + MAXS for epoch in range(epochs)]
        cols = [shifts[start + 2 * epoch + 1] + MAXS for epoch in range(epochs)]
        beyond = [across < col for col in cols]
        turn = [jnp.where(col == 0, 0, LANES - col) for col in cols]
        for top in range(0, height, 8):
            totals, low_total = [None] * tiles, None
            for epoch in range(epochs):
                here = pl.ds(rows[epoch] + top, 8)
                loaded = [whole[epoch, tile, here] for tile in range(count)]
                for tile in range(tiles):
                    moved = pltpu.roll(jnp.where(beyond[epoch], loaded[tile + 1], loaded[tile]), turn[epoch], 1)
                    totals[tile] = moved if epoch == 0 else totals[tile] + moved
                moved = pltpu.roll(jnp.where(beyond[epoch], near_packed[epoch, here], packed[epoch, here]), turn[epoch], 1)
                low_total = moved if epoch == 0 else low_total + moved
            for tile in range(tiles):
                psi = (totals[tile] >> 8).astype(jnp.float32)
                phi = (((totals[tile] & 255) << 6) + ((low_total >> (8 * tile)) & 255)).astype(jnp.float32)
                out_ref[local_index, top : top + 8, tile * LANES : (tile + 1) * LANES] = (
                    psi * unit * lax.rsqrt(jnp.maximum(phi, least))
                )
        return 0

    lax.fori_loop(0, group, one_velocity, 0, unroll=True)


def stack_blocks(place, shifts, floor, sources, out, out_shape, parts, blocks):
    epochs, kinds, tiles = sources[0][0].shape[1:4]
    velocities, height, columns = out_shape.shape
    group = next(size for size in (18, 12, 9, 8, 6, 4, 3, 2, 1) if velocities % size == 0)
    width, reach = tiles * LANES, height + 2 * MAXS
    in_specs, operands = [], []
    for index, (array, slot, tile) in enumerate(sources):
        depth = tiles if index % 6 < 3 else 1
        in_specs.append(
            pl.BlockSpec(
                (1, epochs, kinds, depth, MAXS, LANES),
                functools.partial(lambda slot, tile, *_: (slot, 0, 0, tile, 0, 0), slot, tile),
            )
        )
        operands.append(array)
    aliases = {}
    if out is not None:
        in_specs.append(pl.BlockSpec(memory_space=pl.ANY))
        operands.append(out)
        aliases = {3 + len(sources): 0}
    work = parts * velocities * height * width
    return pl.pallas_call(
        functools.partial(stack_kernel, group=group, parts=parts, blocks=blocks),
        grid_spec=pltpu.PrefetchScalarGridSpec(
            num_scalar_prefetch=3,
            grid=(parts, velocities // group),
            in_specs=in_specs,
            out_specs=pl.BlockSpec((group, height, width), lambda part, chunk, place, *_: (chunk, 0, place[part])),
            scratch_shapes=[
                pltpu.VMEM((epochs, kinds, tiles + 1, reach, LANES), jnp.float32),
                pltpu.VMEM((epochs, tiles + 1, reach, LANES), jnp.int32),
                pltpu.VMEM((epochs, reach, LANES), jnp.int32),
                pltpu.VMEM((epochs, reach, LANES), jnp.int32),
                pltpu.VMEM((2, 8, LANES), jnp.float32),
            ],
        ),
        out_shape=out_shape,
        input_output_aliases=aliases,
        compiler_params=pltpu.CompilerParams(vmem_limit_bytes=VMEM),
        cost_estimate=pl.CostEstimate(flops=16 * work, bytes_accessed=24 * work, transcendentals=work),
    )(place, shifts, floor, *operands)


def local(images, variance, spread_kernel, shifts, epoch_owner, valid_rows):
    exposure, noise_var = images[0], variance[0]
    height, columns = exposure.shape
    blocks = lax.axis_size("vel")
    width = columns // blocks
    me, lower = lax.axis_index("vel"), lax.axis_index("rows")
    swap = [(0, 1), (1, 0)]

    order = list(range(0, blocks, 2)) + list(range(1, blocks, 2))[::-1]
    right = [(order[i], order[(i + 1) % blocks]) for i in range(blocks)]
    left = [(b, a) for a, b in right]

    def position(index):
        return jnp.where(index % 2 == 0, index // 2, blocks - 1 - index // 2)

    mine = position(me)
    place = jnp.stack([mine, lower]).astype(jnp.int32)

    starts = position(me ^ jnp.arange(blocks, dtype=jnp.int32)) * width
    chunks = list(cut(starts, exposure, noise_var, blocks))
    for step in range(1, blocks):
        chunks[step] = lax.ppermute(chunks[step], "vel", [(i, i ^ step) for i in range(blocks)])
    chunks[1], spread_kernel = lax.optimization_barrier((chunks[1], spread_kernel))
    bands, floor = make_bands(spread_kernel)
    chunks[-1], floor = lax.optimization_barrier((chunks[-1], floor))
    spot = jnp.stack([me, lower]).astype(jnp.int32)
    own, edges = pick(spot, epoch_owner, valid_rows, chunks, height)
    payload = correlate(place, own, lax.ppermute(edges, "rows", swap), bands)

    flat_shifts, floor = shifts.reshape(-1), floor[0, :1]
    out_shape = jax.ShapeDtypeStruct((shifts.shape[0], height, columns), jnp.float32)

    def stack_now(offsets, out):
        sources = []
        for offset in offsets:
            sources += list(have[offset]) + list(front if offset == 0 else have[offset + 1])
        spots = jnp.stack([(mine + offset) % blocks for offset in offsets] + [lower]).astype(jnp.int32)
        return stack_blocks(spots, flat_shifts, floor, sources, out, out_shape, len(offsets), blocks)

    tiles = payload.shape[3]
    front = lax.ppermute(payload[:, :, :, :1], "vel", left)
    behind, ahead = lax.ppermute(payload, "vel", right), lax.ppermute(payload, "vel", left)
    border = lax.ppermute(jnp.concatenate([payload[:1], front[:1]], axis=3), "rows", swap)
    front = ((front, 0, 0), (front, 1, 0), (border, 0, tiles))
    have = {0: ((payload, 0, 0), (payload, 1, 0), (border, 0, 0))}
    out = stack_now([0], None)
    half = blocks // 2
    for step in range(1, half + 1):
        if step < half:
            if step > 1:
                behind, ahead = lax.ppermute(behind, "vel", right), lax.ppermute(ahead, "vel", left)
            behind, ahead, out = lax.optimization_barrier((behind, ahead, out))
            border = lax.ppermute(jnp.concatenate([behind[:1], ahead[:1]]), "rows", swap)
            have[-step] = ((behind, 0, 0), (behind, 1, 0), (border, 0, 0))
            have[step] = ((ahead, 0, 0), (ahead, 1, 0), (border, 1, 0))
        else:
            edge, inner = lax.ppermute(behind[:1], "vel", right), lax.ppermute(ahead[1:], "vel", left)
            edge, inner, out = lax.optimization_barrier((edge, inner, out))
            border = lax.ppermute(edge, "rows", swap)
            have[step] = have[-step] = ((edge, 0, 0), (inner, 0, 0), (border, 0, 0))
        out = stack_now([step - 1, -step] if step > 1 else [-step], out)
    return out


def solution(mesh):
    in_specs = (
        P(("fields", "vel"), "rows", None),
        P(("fields", "vel"), "rows", None),
        P(),
        P(("fields", "vel"), None, None),
        P("fields"),
        P("fields", None),
    )
    out_specs = P(("fields", "vel"), "rows", None)
    return jax.shard_map(local, mesh=mesh, in_specs=in_specs, out_specs=out_specs, check_vma=False)
```

```python
import functools
import jax
import jax.numpy as jnp
from jax import lax
from jax.experimental import pallas as pl
from jax.experimental.pallas import tpu as pltpu
from jax.sharding import PartitionSpec as P

LANES = 128
MAXS = 16
HALO = 32
VMEM = 24 << 20
LARGE = 56 << 20


def band_kernel(taps, kernel, bands_ref, floor_ref):
    ksize = kernel.shape[0]
    skip = LANES - MAXS - ksize // 2
    top = skip // 8 * 8
    shape = (2 * LANES - top, LANES)
    offset = lax.broadcasted_iota(jnp.int32, shape, 0) - lax.broadcasted_iota(jnp.int32, shape, 1) + (top - skip)
    total = jnp.full((8, LANES), jnp.sum(kernel[...]), jnp.float32)
    norm = kernel[...] / total[:1, :1]
    floor_ref[...] = jnp.full(floor_ref.shape, 0.5 * jnp.sum(norm * norm), jnp.float32)
    bands_ref[:, :, :top] = jnp.zeros(bands_ref.shape[:2] + (top, 2 * LANES), jnp.bfloat16)

    def one(row, _):
        band = jnp.zeros(shape, jnp.float32)
        for col in range(ksize):
            band = jnp.where(offset == col, taps[row * ksize + col], band)
        band = band / total[:1]
        for kind, value in enumerate((band, band * band)):
            high = value.astype(jnp.bfloat16)
            bands_ref[kind, row, top:, :LANES] = high
            bands_ref[kind, row, top:, LANES:] = (value - high.astype(jnp.float32)).astype(jnp.bfloat16)
        return 0

    lax.fori_loop(0, ksize, one, 0)


def make_bands(spread_kernel):
    ksize = spread_kernel.shape[0]
    return pl.pallas_call(
        band_kernel,
        in_specs=[pl.BlockSpec(memory_space=pltpu.SMEM), pl.BlockSpec(memory_space=pltpu.VMEM)],
        out_specs=[pl.BlockSpec(memory_space=pltpu.VMEM)] * 2,
        out_shape=[
            jax.ShapeDtypeStruct((2, ksize, 2 * LANES, 2 * LANES), jnp.bfloat16),
            jax.ShapeDtypeStruct((8, LANES), jnp.float32),
        ],
        compiler_params=pltpu.CompilerParams(vmem_limit_bytes=LARGE),
        cost_estimate=pl.CostEstimate(flops=0, bytes_accessed=20 << 20, transcendentals=0),
    )(spread_kernel.reshape(-1), spread_kernel)


def cut_kernel(starts, exposure, noise_var, *refs):
    chunk_refs, (held, arrived) = refs[:-2], refs[-2:]
    _, height, columns = held.shape
    tiles = columns // len(chunk_refs) // LANES
    copies = []
    for kind, source in enumerate((exposure, noise_var)):
        for top in range(0, height, 8):
            copies.append(
                pltpu.make_async_copy(
                    source.at[pl.ds(top, 8)], held.at[kind, pl.ds(top, 8)], arrived.at[kind, top // 8]
                )
            )
            copies[-1].start()
    for copy in copies:
        copy.wait()
    lane = lax.broadcasted_iota(jnp.int32, (8, LANES), 1)
    for index, ref in enumerate(chunk_refs):
        start = starts[index]
        ahead = jnp.where(start == 0, columns, start) - LANES
        for kind in range(2):
            for tile in range(tiles):
                at = pl.multiple_of(start + tile * LANES, LANES)
                ref[kind, tile * height : (tile + 1) * height] = held[kind, :, pl.ds(at, LANES)]
            halo = jnp.zeros((8, LANES), jnp.float32)
            for group in range(LANES // HALO):
                rows = held[kind, 8 * group : 8 * group + 8, pl.ds(pl.multiple_of(ahead, LANES), LANES)]
                moved = pltpu.roll(rows, (group + 1) * HALO % LANES, 1)
                halo = jnp.where(lane // HALO == group, moved, halo)
            ref[kind, tiles * height :] = halo


def cut(starts, exposure, noise_var, blocks):
    height, columns = exposure.shape
    rows = columns // blocks // LANES * height + height * HALO // LANES
    return pl.pallas_call(
        cut_kernel,
        in_specs=[pl.BlockSpec(memory_space=pltpu.SMEM)] + [pl.BlockSpec(memory_space=pltpu.HBM)] * 2,
        out_specs=[pl.BlockSpec(memory_space=pltpu.VMEM)] * blocks,
        out_shape=[jax.ShapeDtypeStruct((2, rows, LANES), jnp.float32)] * blocks,
        scratch_shapes=[pltpu.VMEM((2, height, columns), jnp.float32), pltpu.SemaphoreType.DMA((2, height // 8))],
        compiler_params=pltpu.CompilerParams(vmem_limit_bytes=LARGE),
        cost_estimate=pl.CostEstimate(flops=0, bytes_accessed=16 * height * columns, transcendentals=0),
    )(starts, exposure, noise_var)


def pick_kernel(place, owner, valid, *refs):
    chunks, (own, edges, chosen) = refs[:-3], refs[-3:]
    epochs, _, count, height, _ = own.shape
    tiles = count - 1
    me, lower = place[0], place[1]
    for epoch in range(epochs):
        for step, chunk in enumerate(chunks):

            @pl.when(owner[epoch] ^ me == step)
            def _():
                chosen[epoch] = chunk[...]

    row_ids = lower * height + lax.broadcasted_iota(jnp.int32, (height, LANES), 0)
    behind = lax.broadcasted_iota(jnp.int32, (8, LANES), 1) >= LANES - HALO
    for epoch in range(epochs):
        usable = jnp.logical_and(row_ids >= valid[2 * epoch], row_ids < valid[2 * epoch + 1])
        for tile in range(count):
            if tile:
                value, noise = (chosen[epoch, kind, (tile - 1) * height : tile * height] for kind in range(2))
            else:
                packed = [chosen[epoch, kind, tiles * height :] for kind in range(2)]
                spread = [
                    jnp.concatenate(
                        [
                            jnp.where(behind, pltpu.roll(rows, (LANES - (group + 1) * HALO) % LANES, 1), fill)
                            for group in range(LANES // HALO)
                        ],
                        axis=0,
                    )
                    for rows, fill in zip(packed, (0.0, 1.0))
                ]
                value, noise = spread
            own[epoch, 0, tile] = jnp.where(usable, value / noise, 0.0)
            own[epoch, 1, tile] = jnp.where(usable, 1.0 / noise, 0.0)
    edges[...] = own[:, :, :, pl.ds(pl.multiple_of((1 - lower) * (height - MAXS), MAXS), MAXS)]


def pick(place, owner, valid, chunks, height):
    rows = chunks[0].shape[1]
    epochs, tiles = owner.shape[0], (rows - height * HALO // LANES) // height
    return pl.pallas_call(
        pick_kernel,
        in_specs=[pl.BlockSpec(memory_space=pltpu.SMEM)] * 3 + [pl.BlockSpec(memory_space=pltpu.VMEM)] * len(chunks),
        out_specs=[pl.BlockSpec(memory_space=pltpu.VMEM)] * 2,
        out_shape=[
            jax.ShapeDtypeStruct((epochs, 2, tiles + 1, depth, LANES), jnp.float32) for depth in (height, MAXS)
        ],
        scratch_shapes=[pltpu.VMEM((epochs, 2, rows, LANES), jnp.float32)],
        compiler_params=pltpu.CompilerParams(vmem_limit_bytes=VMEM),
        cost_estimate=pl.CostEstimate(flops=0, bytes_accessed=4 << 20, transcendentals=0),
    )(place, owner, valid.reshape(-1), *chunks)


def correlate_kernel(place, own, border, bands_hbm, rows_ref, ext, high, low, summed, bands_ref, arrived):
    epochs, kinds, count, height, _ = own.shape
    tiles = count - 1
    ksize = bands_ref.shape[1]
    members = high.shape[2] // (height + 2 * MAXS)
    copies = [pltpu.make_async_copy(bands_hbm.at[kind], bands_ref.at[kind], arrived.at[kind]) for kind in range(kinds)]
    for copy in copies:
        copy.start()
    first, lower = place[0] == 0, place[1]
    at_border = (1 - lower) * (MAXS + height)
    summed_rows = height * members
    blank = pl.ds(pl.multiple_of(lower * (MAXS + height) * members, 8), MAXS * members)
    ext[:, :, blank] = jnp.zeros((kinds, 2, MAXS * members, LANES), jnp.float32)
    nothing = jnp.zeros((height, LANES), jnp.float32)
    keep = jnp.where(first, 0.0, 1.0)

    def put(kind, half, member, value, beyond):
        ext[kind, half, pl.ds(MAXS * members + member, height, stride=members)] = value
        ext[kind, half, pl.ds(at_border * members + member, MAXS, stride=members)] = beyond

    for epoch in range(epochs):
        base = epoch * (tiles + 1)
        for kind in range(kinds):
            for tile in range(1, count):
                put(kind, 1, base + tile - 1, own[epoch, kind, tile], border[epoch, kind, tile])
                if tile < tiles:
                    put(kind, 0, base + tile, own[epoch, kind, tile], border[epoch, kind, tile])
            put(kind, 0, base, own[epoch, kind, 0] * keep, border[epoch, kind, 0] * keep)
            put(kind, 0, base + tiles, own[epoch, kind, 0], border[epoch, kind, 0])
            put(kind, 1, base + tiles, nothing, nothing[:MAXS])

    def split(index, _):
        rows = pl.ds(pl.multiple_of(index * 128, 128), 128)
        for kind in range(kinds):
            for half in range(2):
                value = ext[kind, half, rows]
                part = value.astype(jnp.bfloat16)
                high[kind, half, rows] = part
                low[kind, half, rows] = (value - part.astype(jnp.float32)).astype(jnp.bfloat16)
        return 0

    lax.fori_loop(0, ext.shape[2] // 128, split, 0)

    lane = lax.broadcasted_iota(jnp.int32, (MAXS, LANES), 1)
    wrapped = jnp.logical_and(first, lane < MAXS)
    for kind in range(kinds):
        offsets = [pl.ds((row + MAXS - ksize // 2) * members, summed_rows) for row in range(ksize)]
        upper = jnp.concatenate([high[kind, half, rows] for rows in offsets for half in range(2)], axis=1)
        rest = jnp.concatenate([low[kind, half, rows] for rows in offsets for half in range(2)], axis=1)
        copies[kind].wait()
        weights = bands_ref[kind].reshape(ksize * 2 * LANES, 2 * LANES)
        pair = jnp.dot(upper, weights, preferred_element_type=jnp.float32)
        more = jnp.dot(rest, weights[:, :LANES], preferred_element_type=jnp.float32)
        summed[...] = pair[:, :LANES] + (pair[:, LANES:] + more)
        for half in range(2):
            start = (1 - lower if half == 0 else lower) * (height - MAXS)
            for epoch in range(epochs):
                base = epoch * (tiles + 1)

                def rows_of(tile):
                    return summed[pl.ds(start * members + base + tile, MAXS, stride=members)]

                rows_ref[half, epoch, kind, 0] = jnp.where(wrapped, rows_of(tiles), rows_of(0))
                for tile in range(1, tiles):
                    rows_ref[half, epoch, kind, tile] = rows_of(tile)


def correlate(place, own, border, bands):
    epochs, kinds, count, height, _ = own.shape
    tiles = count - 1
    members = -(-epochs * (tiles + 1) // 16) * 16
    depth = (height + 2 * MAXS) * members
    flops = 2 * 2 * kinds * members * height * bands.shape[1] * 4 * LANES * LANES
    return pl.pallas_call(
        correlate_kernel,
        in_specs=[pl.BlockSpec(memory_space=pltpu.SMEM)] + [pl.BlockSpec(memory_space=pltpu.VMEM)] * 2
        + [pl.BlockSpec(memory_space=pltpu.HBM)],
        out_specs=pl.BlockSpec(memory_space=pltpu.VMEM),
        out_shape=jax.ShapeDtypeStruct((2, epochs, kinds, tiles, MAXS, LANES), jnp.float32),
        scratch_shapes=[
            pltpu.VMEM((kinds, 2, depth, LANES), jnp.float32),
            pltpu.VMEM((kinds, 2, depth, LANES), jnp.bfloat16),
            pltpu.VMEM((kinds, 2, depth, LANES), jnp.bfloat16),
            pltpu.VMEM((height * members, LANES), jnp.float32),
            pltpu.VMEM(bands.shape, bands.dtype),
            pltpu.SemaphoreType.DMA((kinds,)),
        ],
        compiler_params=pltpu.CompilerParams(vmem_limit_bytes=LARGE),
        cost_estimate=pl.CostEstimate(flops=flops, bytes_accessed=12 << 20, transcendentals=0),
    )(place, own, border, bands)


def stack_kernel(place, shifts, floor, *refs, group, parts, blocks):
    sources, out_ref = refs[: 6 * parts], refs[-6]
    raw, whole, packed, near_packed, scale = refs[-5:]
    part, base = pl.program_id(0), pl.program_id(1) * group
    epochs, count, reach = whole.shape[:3]
    tiles = count - 1
    lower = place[parts]
    lane = lax.broadcasted_iota(jnp.int32, (1, LANES), 1)
    at = [pl.multiple_of(row, MAXS) for row in (32 - 16 * lower, 16 + 16 * lower, 48 - 48 * lower)]
    blank = pl.multiple_of(48 * lower, MAXS)
    most_psi = ((1 << 23) - 1) // epochs
    most_high = 255 // epochs
    most_phi = most_high * 64 + 63

    for index in range(parts):

        @pl.when(jnp.logical_and(part == index, pl.program_id(1) == 0))
        def _():
            block = place[index]
            keep_first = jnp.where(jnp.logical_and(block == 0, lane < MAXS), 0.0, 1.0) > 0.5
            keep_last = jnp.where(jnp.logical_and(block == blocks - 1, lane >= MAXS), 0.0, 1.0) > 0.5
            for epoch in range(epochs):
                for kind in range(2):
                    for tile in range(count):
                        raw[epoch, kind, tile, pl.ds(blank, MAXS)] = jnp.zeros((MAXS, LANES), jnp.float32)
            tops = [jnp.zeros((MAXS, LANES), jnp.float32) for _ in range(2)]
            for piece in range(3):
                own, nearby = sources[6 * index + piece], sources[6 * index + 3 + piece]
                rows = pl.ds(at[piece], MAXS)
                for epoch in range(epochs):
                    for kind in range(2):
                        for tile in range(count):
                            if tile == tiles:
                                value = jnp.where(keep_last, nearby[0, epoch, kind, 0], 0.0)
                            elif tile == 0:
                                value = jnp.where(keep_first, own[0, epoch, kind, 0], 0.0)
                            else:
                                value = own[0, epoch, kind, tile]
                            tops[kind] = jnp.maximum(tops[kind], jnp.abs(value))
                            raw[epoch, kind, tile, rows] = value
            tops = [jnp.full((8, LANES), jnp.maximum(jnp.max(top), 1e-30), jnp.float32) for top in tops]
            per_psi, per_phi = most_psi / tops[0], most_phi / tops[1]
            scale[0] = floor[0] * per_phi
            scale[1] = jnp.sqrt(per_phi) / per_psi

            def quantize(index, _):
                rows = pl.ds(pl.multiple_of(index * 8, 8), 8)
                for epoch in range(epochs):
                    lows = []
                    for tile in range(count):
                        psi = jnp.floor(raw[epoch, 0, tile, rows] * per_psi + 0.5).astype(jnp.int32)
                        phi = jnp.floor(jnp.maximum(raw[epoch, 1, tile, rows], 0.0) * per_phi + 0.5).astype(jnp.int32)
                        psi = jnp.clip(psi, -most_psi, most_psi)
                        phi = jnp.minimum(phi, most_phi)
                        whole[epoch, tile, rows] = psi * 256 + (phi >> 6)
                        lows.append(phi & 63)
                    here, nearby = lows[0], lows[1]
                    for tile in range(1, tiles):
                        here = here + (lows[tile] << (8 * tile))
                        nearby = nearby + (lows[tile + 1] << (8 * tile))
                    packed[epoch, rows] = here
                    near_packed[epoch, rows] = nearby
                return 0

            lax.fori_loop(0, reach // 8, quantize, 0, unroll=4)

    height = out_ref.shape[1]
    across = lax.broadcasted_iota(jnp.int32, (8, LANES), 1)
    least, unit = scale[0], scale[1]

    def one_velocity(local_index, _):
        start = (base + local_index) * epochs * 2
        rows = [shifts[start + 2 * epoch] + MAXS for epoch in range(epochs)]
        cols = [shifts[start + 2 * epoch + 1] + MAXS for epoch in range(epochs)]
        beyond = [across < col for col in cols]
        turn = [jnp.where(col == 0, 0, LANES - col) for col in cols]
        for top in range(0, height, 8):
            totals, low_total = [None] * tiles, None
            for epoch in range(epochs):
                here = pl.ds(rows[epoch] + top, 8)
                loaded = [whole[epoch, tile, here] for tile in range(count)]
                for tile in range(tiles):
                    moved = pltpu.roll(jnp.where(beyond[epoch], loaded[tile + 1], loaded[tile]), turn[epoch], 1)
                    totals[tile] = moved if epoch == 0 else totals[tile] + moved
                moved = pltpu.roll(jnp.where(beyond[epoch], near_packed[epoch, here], packed[epoch, here]), turn[epoch], 1)
                low_total = moved if epoch == 0 else low_total + moved
            for tile in range(tiles):
                psi = (totals[tile] >> 8).astype(jnp.float32)
                phi = (((totals[tile] & 255) << 6) + ((low_total >> (8 * tile)) & 255)).astype(jnp.float32)
                out_ref[local_index, top : top + 8, tile * LANES : (tile + 1) * LANES] = (
                    psi * unit * lax.rsqrt(jnp.maximum(phi, least))
                )
        return 0

    lax.fori_loop(0, group, one_velocity, 0, unroll=True)


def stack_blocks(place, shifts, floor, sources, out, out_shape, parts, blocks):
    epochs, kinds, tiles = sources[0][0].shape[1:4]
    velocities, height, columns = out_shape.shape
    group = next(size for size in (18, 12, 9, 8, 6, 4, 3, 2, 1) if velocities % size == 0)
    width, reach = tiles * LANES, height + 2 * MAXS
    in_specs, operands = [], []
    for index, (array, slot, tile) in enumerate(sources):
        depth = tiles if index % 6 < 3 else 1
        in_specs.append(
            pl.BlockSpec(
                (1, epochs, kinds, depth, MAXS, LANES),
                functools.partial(lambda slot, tile, *_: (slot, 0, 0, tile, 0, 0), slot, tile),
            )
        )
        operands.append(array)
    aliases = {}
    if out is not None:
        in_specs.append(pl.BlockSpec(memory_space=pl.ANY))
        operands.append(out)
        aliases = {3 + len(sources): 0}
    work = parts * velocities * height * width
    return pl.pallas_call(
        functools.partial(stack_kernel, group=group, parts=parts, blocks=blocks),
        grid_spec=pltpu.PrefetchScalarGridSpec(
            num_scalar_prefetch=3,
            grid=(parts, velocities // group),
            in_specs=in_specs,
            out_specs=pl.BlockSpec((group, height, width), lambda part, chunk, place, *_: (chunk, 0, place[part])),
            scratch_shapes=[
                pltpu.VMEM((epochs, kinds, tiles + 1, reach, LANES), jnp.float32),
                pltpu.VMEM((epochs, tiles + 1, reach, LANES), jnp.int32),
                pltpu.VMEM((epochs, reach, LANES), jnp.int32),
                pltpu.VMEM((epochs, reach, LANES), jnp.int32),
                pltpu.VMEM((2, 8, LANES), jnp.float32),
            ],
        ),
        out_shape=out_shape,
        input_output_aliases=aliases,
        compiler_params=pltpu.CompilerParams(vmem_limit_bytes=VMEM),
        cost_estimate=pl.CostEstimate(flops=16 * work, bytes_accessed=24 * work, transcendentals=work),
    )(place, shifts, floor, *operands)


def local(images, variance, spread_kernel, shifts, epoch_owner, valid_rows):
    exposure, noise_var = images[0], variance[0]
    height, columns = exposure.shape
    blocks = lax.axis_size("vel")
    width = columns // blocks
    me, lower = lax.axis_index("vel"), lax.axis_index("rows")
    swap = [(0, 1), (1, 0)]

    order = list(range(0, blocks, 2)) + list(range(1, blocks, 2))[::-1]
    right = [(order[i], order[(i + 1) % blocks]) for i in range(blocks)]
    left = [(b, a) for a, b in right]

    def position(index):
        return jnp.where(index % 2 == 0, index // 2, blocks - 1 - index // 2)

    mine = position(me)
    place = jnp.stack([mine, lower]).astype(jnp.int32)

    starts = position(me ^ jnp.arange(blocks, dtype=jnp.int32)) * width
    chunks = list(cut(starts, exposure, noise_var, blocks))
    for step in range(blocks - 1, 0, -1):
        chunks[step] = lax.ppermute(chunks[step], "vel", [(i, i ^ step) for i in range(blocks)])
    chunks[-1], spread_kernel = lax.optimization_barrier((chunks[-1], spread_kernel))
    bands, floor = make_bands(spread_kernel)
    chunks[1], floor = lax.optimization_barrier((chunks[1], floor))
    spot = jnp.stack([me, lower]).astype(jnp.int32)
    own, edges = pick(spot, epoch_owner, valid_rows, chunks, height)
    payload = correlate(place, own, lax.ppermute(edges, "rows", swap), bands)

    flat_shifts, floor = shifts.reshape(-1), floor[0, :1]
    out_shape = jax.ShapeDtypeStruct((shifts.shape[0], height, columns), jnp.float32)

    def stack_now(offsets, out):
        sources = []
        for offset in offsets:
            sources += list(have[offset]) + list(front if offset == 0 else have[offset + 1])
        spots = jnp.stack([(mine + offset) % blocks for offset in offsets] + [lower]).astype(jnp.int32)
        return stack_blocks(spots, flat_shifts, floor, sources, out, out_shape, len(offsets), blocks)

    tiles = payload.shape[3]
    front = lax.ppermute(payload[:, :, :, :1], "vel", left)
    behind, ahead = lax.ppermute(payload, "vel", right), lax.ppermute(payload, "vel", left)
    border = lax.ppermute(jnp.concatenate([payload[:1], front[:1]], axis=3), "rows", swap)
    front = ((front, 0, 0), (front, 1, 0), (border, 0, tiles))
    have = {0: ((payload, 0, 0), (payload, 1, 0), (border, 0, 0))}
    out = stack_now([0], None)
    half = blocks // 2
    for step in range(1, half + 1):
        if step < half:
            if step > 1:
                behind, ahead = lax.ppermute(behind, "vel", right), lax.ppermute(ahead, "vel", left)
            behind, ahead, out = lax.optimization_barrier((behind, ahead, out))
            border = lax.ppermute(jnp.concatenate([behind[:1], ahead[:1]]), "rows", swap)
            have[-step] = ((behind, 0, 0), (behind, 1, 0), (border, 0, 0))
            have[step] = ((ahead, 0, 0), (ahead, 1, 0), (border, 1, 0))
        else:
            edge, inner = lax.ppermute(behind[:1], "vel", right), lax.ppermute(ahead[1:], "vel", left)
            edge, inner, out = lax.optimization_barrier((edge, inner, out))
            border = lax.ppermute(edge, "rows", swap)
            have[step] = have[-step] = ((edge, 0, 0), (inner, 0, 0), (border, 0, 0))
        out = stack_now([step - 1, -step] if step > 1 else [-step], out)
    return out


def solution(mesh):
    in_specs = (
        P(("fields", "vel"), "rows", None),
        P(("fields", "vel"), "rows", None),
        P(),
        P(("fields", "vel"), None, None),
        P("fields"),
        P("fields", None),
    )
    out_specs = P(("fields", "vel"), "rows", None)
    return jax.shard_map(local, mesh=mesh, in_specs=in_specs, out_specs=out_specs, check_vma=False)
```

```python
import functools
import jax
import jax.numpy as jnp
from jax import lax
from jax.experimental import pallas as pl
from jax.experimental.pallas import tpu as pltpu
from jax.sharding import PartitionSpec as P

LANES = 128
MAXS = 16
HALO = 32
VMEM = 24 << 20


def band_kernel(taps, kernel, bands_ref, floor_ref):
    ksize = kernel.shape[0]
    skip = LANES - MAXS - ksize // 2
    top = skip // 8 * 8
    shape = (2 * LANES - top, LANES)
    offset = lax.broadcasted_iota(jnp.int32, shape, 0) - lax.broadcasted_iota(jnp.int32, shape, 1) + (top - skip)
    total = jnp.full((8, LANES), jnp.sum(kernel[...]), jnp.float32)
    norm = kernel[...] / total[:1, :1]
    floor_ref[...] = jnp.full(floor_ref.shape, 0.5 * jnp.sum(norm * norm), jnp.float32)
    bands_ref[:, :, :top] = jnp.zeros(bands_ref.shape[:2] + (top, 2 * LANES), jnp.bfloat16)

    def one(row, _):
        band = jnp.zeros(shape, jnp.float32)
        for col in range(ksize):
            band = jnp.where(offset == col, taps[row * ksize + col], band)
        band = band / total[:1]
        for kind, value in enumerate((band, band * band)):
            high = value.astype(jnp.bfloat16)
            bands_ref[kind, row, top:, :LANES] = high
            bands_ref[kind, row, top:, LANES:] = (value - high.astype(jnp.float32)).astype(jnp.bfloat16)
        return 0

    lax.fori_loop(0, ksize, one, 0)


def make_bands(spread_kernel):
    ksize = spread_kernel.shape[0]
    return pl.pallas_call(
        band_kernel,
        in_specs=[pl.BlockSpec(memory_space=pltpu.SMEM), pl.BlockSpec(memory_space=pltpu.VMEM)],
        out_specs=[pl.BlockSpec(memory_space=pltpu.VMEM)] * 2,
        out_shape=[
            jax.ShapeDtypeStruct((2, ksize, 2 * LANES, 2 * LANES), jnp.bfloat16),
            jax.ShapeDtypeStruct((8, LANES), jnp.float32),
        ],
        compiler_params=pltpu.CompilerParams(vmem_limit_bytes=VMEM),
        cost_estimate=pl.CostEstimate(flops=0, bytes_accessed=20 << 20, transcendentals=0),
    )(spread_kernel.reshape(-1), spread_kernel)


def cut_kernel(starts, exposure, noise_var, *chunk_refs):
    height, columns = exposure.shape
    tiles = columns // len(chunk_refs) // LANES
    lane = lax.broadcasted_iota(jnp.int32, (8, LANES), 1)
    for index, ref in enumerate(chunk_refs):
        start = starts[index]
        ahead = jnp.where(start == 0, columns, start) - LANES
        for kind, held in enumerate((exposure, noise_var)):
            for tile in range(tiles):
                at = pl.multiple_of(start + tile * LANES, LANES)
                ref[kind, tile * height : (tile + 1) * height] = held[:, pl.ds(at, LANES)]
            halo = jnp.zeros((8, LANES), jnp.float32)
            for group in range(LANES // HALO):
                rows = held[8 * group : 8 * group + 8, pl.ds(pl.multiple_of(ahead, LANES), LANES)]
                moved = pltpu.roll(rows, (group + 1) * HALO % LANES, 1)
                halo = jnp.where(lane // HALO == group, moved, halo)
            ref[kind, tiles * height :] = halo


def cut(starts, exposure, noise_var, blocks):
    height, columns = exposure.shape
    rows = columns // blocks // LANES * height + height * HALO // LANES
    return pl.pallas_call(
        cut_kernel,
        in_specs=[pl.BlockSpec(memory_space=pltpu.SMEM)] + [pl.BlockSpec(memory_space=pltpu.VMEM)] * 2,
        out_specs=[pl.BlockSpec(memory_space=pltpu.VMEM)] * blocks,
        out_shape=[jax.ShapeDtypeStruct((2, rows, LANES), jnp.float32)] * blocks,
        compiler_params=pltpu.CompilerParams(vmem_limit_bytes=VMEM),
        cost_estimate=pl.CostEstimate(flops=0, bytes_accessed=16 * height * columns, transcendentals=0),
    )(starts, exposure, noise_var)


def pick_kernel(place, owner, valid, *refs):
    chunks, (own, edges, chosen) = refs[:-3], refs[-3:]
    epochs, _, count, height, _ = own.shape
    tiles = count - 1
    me, lower = place[0], place[1]
    for epoch in range(epochs):
        for step, chunk in enumerate(chunks):

            @pl.when(owner[epoch] ^ me == step)
            def _():
                chosen[epoch] = chunk[...]

    row_ids = lower * height + lax.broadcasted_iota(jnp.int32, (height, LANES), 0)
    behind = lax.broadcasted_iota(jnp.int32, (8, LANES), 1) >= LANES - HALO
    for epoch in range(epochs):
        usable = jnp.logical_and(row_ids >= valid[2 * epoch], row_ids < valid[2 * epoch + 1])
        for tile in range(count):
            if tile:
                value, noise = (chosen[epoch, kind, (tile - 1) * height : tile * height] for kind in range(2))
            else:
                packed = [chosen[epoch, kind, tiles * height :] for kind in range(2)]
                spread = [
                    jnp.concatenate(
                        [
                            jnp.where(behind, pltpu.roll(rows, (LANES - (group + 1) * HALO) % LANES, 1), fill)
                            for group in range(LANES // HALO)
                        ],
                        axis=0,
                    )
                    for rows, fill in zip(packed, (0.0, 1.0))
                ]
                value, noise = spread
            own[epoch, 0, tile] = jnp.where(usable, value / noise, 0.0)
            own[epoch, 1, tile] = jnp.where(usable, 1.0 / noise, 0.0)
    edges[...] = own[:, :, :, pl.ds(pl.multiple_of((1 - lower) * (height - MAXS), MAXS), MAXS)]


def pick(place, owner, valid, chunks, height):
    rows = chunks[0].shape[1]
    epochs, tiles = owner.shape[0], (rows - height * HALO // LANES) // height
    return pl.pallas_call(
        pick_kernel,
        in_specs=[pl.BlockSpec(memory_space=pltpu.SMEM)] * 3 + [pl.BlockSpec(memory_space=pltpu.VMEM)] * len(chunks),
        out_specs=[pl.BlockSpec(memory_space=pltpu.VMEM)] * 2,
        out_shape=[
            jax.ShapeDtypeStruct((epochs, 2, tiles + 1, depth, LANES), jnp.float32) for depth in (height, MAXS)
        ],
        scratch_shapes=[pltpu.VMEM((epochs, 2, rows, LANES), jnp.float32)],
        compiler_params=pltpu.CompilerParams(vmem_limit_bytes=VMEM),
        cost_estimate=pl.CostEstimate(flops=0, bytes_accessed=4 << 20, transcendentals=0),
    )(place, owner, valid.reshape(-1), *chunks)


def correlate_kernel(place, own, border, bands_ref, rows_ref, ext, high, low, summed):
    epochs, kinds, count, height, _ = own.shape
    tiles = count - 1
    ksize = bands_ref.shape[1]
    members = high.shape[2] // (height + 2 * MAXS)
    first, lower = place[0] == 0, place[1]
    at_border = (1 - lower) * (MAXS + height)
    summed_rows = height * members
    blank = pl.ds(pl.multiple_of(lower * (MAXS + height) * members, 8), MAXS * members)
    ext[:, :, blank] = jnp.zeros((kinds, 2, MAXS * members, LANES), jnp.float32)
    nothing = jnp.zeros((height, LANES), jnp.float32)
    keep = jnp.where(first, 0.0, 1.0)

    def put(kind, half, member, value, beyond):
        ext[kind, half, pl.ds(MAXS * members + member, height, stride=members)] = value
        ext[kind, half, pl.ds(at_border * members + member, MAXS, stride=members)] = beyond

    for epoch in range(epochs):
        base = epoch * (tiles + 1)
        for kind in range(kinds):
            for tile in range(1, count):
                put(kind, 1, base + tile - 1, own[epoch, kind, tile], border[epoch, kind, tile])
                if tile < tiles:
                    put(kind, 0, base + tile, own[epoch, kind, tile], border[epoch, kind, tile])
            put(kind, 0, base, own[epoch, kind, 0] * keep, border[epoch, kind, 0] * keep)
            put(kind, 0, base + tiles, own[epoch, kind, 0], border[epoch, kind, 0])
            put(kind, 1, base + tiles, nothing, nothing[:MAXS])

    def split(index, _):
        rows = pl.ds(pl.multiple_of(index * 128, 128), 128)
        for kind in range(kinds):
            for half in range(2):
                value = ext[kind, half, rows]
                part = value.astype(jnp.bfloat16)
                high[kind, half, rows] = part
                low[kind, half, rows] = (value - part.astype(jnp.float32)).astype(jnp.bfloat16)
        return 0

    lax.fori_loop(0, ext.shape[2] // 128, split, 0)

    lane = lax.broadcasted_iota(jnp.int32, (MAXS, LANES), 1)
    wrapped = jnp.logical_and(first, lane < MAXS)
    for kind in range(kinds):
        offsets = [pl.ds((row + MAXS - ksize // 2) * members, summed_rows) for row in range(ksize)]
        upper = jnp.concatenate([high[kind, half, rows] for rows in offsets for half in range(2)], axis=1)
        rest = jnp.concatenate([low[kind, half, rows] for rows in offsets for half in range(2)], axis=1)
        weights = bands_ref[kind].reshape(ksize * 2 * LANES, 2 * LANES)
        pair = jnp.dot(upper, weights, preferred_element_type=jnp.float32)
        more = jnp.dot(rest, weights[:, :LANES], preferred_element_type=jnp.float32)
        summed[...] = pair[:, :LANES] + (pair[:, LANES:] + more)
        for half in range(2):
            start = (1 - lower if half == 0 else lower) * (height - MAXS)
            for epoch in range(epochs):
                base = epoch * (tiles + 1)

                def rows_of(tile):
                    return summed[pl.ds(start * members + base + tile, MAXS, stride=members)]

                rows_ref[half, epoch, kind, 0] = jnp.where(wrapped, rows_of(tiles), rows_of(0))
                for tile in range(1, tiles):
                    rows_ref[half, epoch, kind, tile] = rows_of(tile)


def correlate(place, own, border, bands):
    epochs, kinds, count, height, _ = own.shape
    tiles = count - 1
    members = -(-epochs * (tiles + 1) // 16) * 16
    depth = (height + 2 * MAXS) * members
    flops = 2 * 2 * kinds * members * height * bands.shape[1] * 4 * LANES * LANES
    return pl.pallas_call(
        correlate_kernel,
        in_specs=[pl.BlockSpec(memory_space=pltpu.SMEM)] + [pl.BlockSpec(memory_space=pltpu.VMEM)] * 3,
        out_specs=pl.BlockSpec(memory_space=pltpu.VMEM),
        out_shape=jax.ShapeDtypeStruct((2, epochs, kinds, tiles, MAXS, LANES), jnp.float32),
        scratch_shapes=[
            pltpu.VMEM((kinds, 2, depth, LANES), jnp.float32),
            pltpu.VMEM((kinds, 2, depth, LANES), jnp.bfloat16),
            pltpu.VMEM((kinds, 2, depth, LANES), jnp.bfloat16),
            pltpu.VMEM((height * members, LANES), jnp.float32),
        ],
        compiler_params=pltpu.CompilerParams(vmem_limit_bytes=VMEM),
        cost_estimate=pl.CostEstimate(flops=flops, bytes_accessed=12 << 20, transcendentals=0),
    )(place, own, border, bands)


def stack_kernel(place, shifts, floor, *refs, segments, sources, total, together):
    operands, out_ref = refs[:sources], refs[-6]
    raw, whole, lows, packed, scale = refs[-5:]
    step = pl.program_id(0)
    epochs, slots, reach = whole.shape[:3]
    velocities, height = out_ref.shape[:2]
    fold = height // 8
    steps = sum(len(held) - 1 for held in segments)
    lower = place[steps]
    at = [pl.multiple_of(row, MAXS) for row in (32 - 16 * lower, 16 + 16 * lower, 48 - 48 * lower)]
    blank = pl.multiple_of(48 * lower, MAXS)
    most_psi = ((1 << 23) - 1) // epochs
    most_phi = 255 // epochs * 64 + 63
    lane = lax.broadcasted_iota(jnp.int32, (8, LANES), 1)

    def assemble(first, held):
        tops = [jnp.zeros((MAXS, LANES), jnp.float32) for _ in range(2)]
        for slot, pieces in enumerate(held):
            for epoch in range(epochs):
                for kind in range(2):
                    raw[epoch, kind, slot, pl.ds(blank, MAXS)] = jnp.zeros((MAXS, LANES), jnp.float32)
                    for start, (source, index, tile) in zip(at, pieces):
                        value = operands[source][index, epoch, kind, tile]
                        tops[kind] = jnp.maximum(tops[kind], jnp.abs(value))
                        raw[epoch, kind, slot, pl.ds(start, MAXS)] = value
        tops = [jnp.full((8, LANES), jnp.maximum(jnp.max(top), 1e-30), jnp.float32) for top in tops]
        per_psi, per_phi = most_psi / tops[0], most_phi / tops[1]
        scale[0] = floor[0] * per_phi
        scale[1] = jnp.sqrt(per_phi) / per_psi

        def quantize(index, _):
            rows = pl.ds(pl.multiple_of(index * 8, 8), 8)
            for epoch in range(epochs):
                for slot in range(len(held)):
                    psi = jnp.floor(raw[epoch, 0, slot, rows] * per_psi + 0.5).astype(jnp.int32)
                    phi = jnp.floor(jnp.maximum(raw[epoch, 1, slot, rows], 0.0) * per_phi + 0.5).astype(jnp.int32)
                    psi = jnp.clip(psi, -most_psi, most_psi)
                    phi = jnp.minimum(phi, most_phi)
                    whole[epoch, slot, rows] = psi * 256 + (phi >> 6)
                    lows[epoch, slot, rows] = phi & 63
            return 0

        lax.fori_loop(0, reach // 8, quantize, 0, unroll=4)
        for epoch in range(epochs):
            for slot in range(len(held)):
                for top in range(0, reach - 8 * (fold - 1), 8):
                    word = lows[epoch, slot, top : top + 8]
                    for part in range(1, fold):
                        word = word + (lows[epoch, slot, top + 8 * part : top + 8 * part + 8] << (8 * part))
                    packed[epoch, slot, top : top + 8] = word
        for slot in range(len(held)):
            number = place[first + slot] if slot < len(held) - 1 else (place[first + slot - 1] + 1) % total
            for spot, keep in ((slots - 2, lane >= MAXS), (slots - 1, lane < MAXS)):

                @pl.when(number == 0)
                def _():
                    for epoch in range(epochs):
                        for ref in (whole, packed):
                            for top in range(0, ref.shape[2], 8):
                                rows = slice(top, top + 8)
                                ref[epoch, spot, rows] = jnp.where(keep, ref[epoch, slot, rows], 0)

    first, begin = 0, 0
    for held in segments:
        pl.when(step == first)(functools.partial(assemble, first, held))
        begin = jnp.where(step >= first, first, begin)
        first += len(held) - 1

    number = place[step]
    left = jnp.where(number == 0, slots - 2, step - begin)
    right = jnp.where(number == total - 1, slots - 1, step - begin + 1)
    least, unit = scale[0], scale[1]

    def one_velocity(velocity, _):
        start = velocity * epochs * 2
        totals, low_total = [None] * fold, None
        for epoch in range(epochs):
            row, col = shifts[start + 2 * epoch] + MAXS, shifts[start + 2 * epoch + 1] + MAXS
            beyond, turn = lane < col, jnp.where(col == 0, 0, LANES - col)

            def moved(ref, top):
                rows = pl.ds(row + top, 8)
                return pltpu.roll(jnp.where(beyond, ref[epoch, right, rows], ref[epoch, left, rows]), turn, 1)

            for part in range(fold):
                word = moved(whole, 8 * part)
                totals[part] = word if epoch == 0 else totals[part] + word
            word = moved(packed, 0)
            low_total = word if epoch == 0 else low_total + word
        for part in range(fold):
            psi = (totals[part] >> 8).astype(jnp.float32)
            phi = (((totals[part] & 255) << 6) + ((low_total >> (8 * part)) & 255)).astype(jnp.float32)
            out_ref[velocity, 8 * part : 8 * part + 8] = psi * unit * lax.rsqrt(jnp.maximum(phi, least))
        return 0

    lax.fori_loop(0, velocities, one_velocity, 0, unroll=together)


def stack_tiles(numbers, lower, shifts, floor, segments, out, out_shape):
    velocities, height, columns = out_shape.shape
    operands, described = [], []
    for held in segments:
        tiles = []
        for pieces, tile in held:
            spots = []
            for array, index in pieces:
                source = next((i for i, other in enumerate(operands) if other is array), len(operands))
                operands += [array] if source == len(operands) else []
                spots.append((source, index, tile))
            tiles.append(spots)
        described.append(tiles)
    sources, epochs = len(operands), operands[0].shape[1]
    in_specs = [pl.BlockSpec(memory_space=pltpu.VMEM)] * sources
    aliases = {}
    if out is not None:
        in_specs.append(pl.BlockSpec(memory_space=pl.ANY))
        operands.append(out)
        aliases = {3 + sources: 0}
    steps, longest, reach = len(numbers), max(len(held) for held in segments), height + 2 * MAXS
    work = steps * velocities * height * LANES
    return pl.pallas_call(
        functools.partial(
            stack_kernel,
            segments=described,
            sources=sources,
            total=columns // LANES,
            together=next(size for size in (36, 18, 12, 9, 8, 6, 4, 3, 2, 1) if velocities % size == 0),
        ),
        grid_spec=pltpu.PrefetchScalarGridSpec(
            num_scalar_prefetch=3,
            grid=(steps,),
            in_specs=in_specs,
            out_specs=pl.BlockSpec((velocities, height, LANES), lambda step, place, *_: (0, 0, place[step])),
            scratch_shapes=[
                pltpu.VMEM((epochs, 2, longest, reach, LANES), jnp.float32),
                pltpu.VMEM((epochs, longest + 2, reach, LANES), jnp.int32),
                pltpu.VMEM((epochs, longest, reach, LANES), jnp.int32),
                pltpu.VMEM((epochs, longest + 2, reach - height + 8, LANES), jnp.int32),
                pltpu.VMEM((2, 8, LANES), jnp.float32),
            ],
        ),
        out_shape=out_shape,
        input_output_aliases=aliases,
        compiler_params=pltpu.CompilerParams(vmem_limit_bytes=VMEM),
        cost_estimate=pl.CostEstimate(flops=16 * work, bytes_accessed=24 * work, transcendentals=work),
    )(jnp.stack(numbers + [lower]).astype(jnp.int32), shifts, floor, *operands)


def local(images, variance, spread_kernel, shifts, epoch_owner, valid_rows):
    exposure, noise_var = images[0], variance[0]
    height, columns = exposure.shape
    blocks = lax.axis_size("vel")
    width = columns // blocks
    me, lower = lax.axis_index("vel"), lax.axis_index("rows")
    swap = [(0, 1), (1, 0)]

    order = list(range(0, blocks, 2)) + list(range(1, blocks, 2))[::-1]
    right = [(order[i], order[(i + 1) % blocks]) for i in range(blocks)]
    left = [(b, a) for a, b in right]

    def position(index):
        return jnp.where(index % 2 == 0, index // 2, blocks - 1 - index // 2)

    mine = position(me)
    place = jnp.stack([mine, lower]).astype(jnp.int32)

    starts = position(me ^ jnp.arange(blocks, dtype=jnp.int32)) * width
    chunks = list(cut(starts, exposure, noise_var, blocks))
    for step in range(1, blocks):
        chunks[step] = lax.ppermute(chunks[step], "vel", [(i, i ^ step) for i in range(blocks)])
    chunks[1], spread_kernel = lax.optimization_barrier((chunks[1], spread_kernel))
    bands, floor = make_bands(spread_kernel)
    chunks[-1], floor = lax.optimization_barrier((chunks[-1], floor))
    spot = jnp.stack([me, lower]).astype(jnp.int32)
    own, edges = pick(spot, epoch_owner, valid_rows, chunks, height)
    payload = correlate(place, own, lax.ppermute(edges, "rows", swap), bands)

    flat_shifts, floor = shifts.reshape(-1), floor[0, :1]
    out_shape = jax.ShapeDtypeStruct((shifts.shape[0], height, columns), jnp.float32)

    tiles, half = payload.shape[3], blocks // 2

    def stack_now(segments, out):
        numbers = [
            (mine + offset) % blocks * tiles + tile for held in segments for offset, tile in held[:-1]
        ]
        held = [[(have[offset], tile) for offset, tile in segment] for segment in segments]
        return stack_tiles(numbers, lower, flat_shifts, floor, held, out, out_shape)

    def block(offset):
        return [(offset, tile) for tile in range(tiles)]

    behind, ahead = lax.ppermute(payload, "vel", right), lax.ppermute(payload, "vel", left)
    border = lax.ppermute(payload[:1], "rows", swap)
    have = {0: ((payload, 0), (payload, 1), (border, 0))}
    out = stack_now([block(0)], None)
    for step in range(1, half + 1):
        if step < half:
            if step > 1:
                behind, ahead = lax.ppermute(behind, "vel", right), lax.ppermute(ahead, "vel", left)
            behind, ahead, out = lax.optimization_barrier((behind, ahead, out))
            border = lax.ppermute(jnp.concatenate([behind[:1], ahead[:1]]), "rows", swap)
            have[-step] = ((behind, 0), (behind, 1), (border, 0))
            have[step] = ((ahead, 0), (ahead, 1), (border, 1))
            segments = [block(-step) + [(1 - step, 0)], [(step - 1, tiles - 1)] + block(step)]
        else:
            edge, inner = lax.ppermute(behind[:1], "vel", right), lax.ppermute(ahead[1:], "vel", left)
            edge, inner, out = lax.optimization_barrier((edge, inner, out))
            border = lax.ppermute(edge, "rows", swap)
            have[step] = ((edge, 0), (inner, 0), (border, 0))
            segments = [[(step - 1, tiles - 1)] + block(step) + [(1 - step, 0)]]
        out = stack_now(segments, out)
    return out


def solution(mesh):
    in_specs = (
        P(("fields", "vel"), "rows", None),
        P(("fields", "vel"), "rows", None),
        P(),
        P(("fields", "vel"), None, None),
        P("fields"),
        P("fields", None),
    )
    out_specs = P(("fields", "vel"), "rows", None)
    return jax.shard_map(local, mesh=mesh, in_specs=in_specs, out_specs=out_specs, check_vma=False)
```

```python
import functools
import jax
import jax.numpy as jnp
from jax import lax
from jax.experimental import pallas as pl
from jax.experimental.pallas import tpu as pltpu
from jax.sharding import PartitionSpec as P

LANES = 128
MAXS = 16
HALO = 32
VMEM = 24 << 20


def band_kernel(taps, kernel, bands_ref, floor_ref):
    ksize = kernel.shape[0]
    skip = LANES - MAXS - ksize // 2
    top = skip // 8 * 8
    shape = (2 * LANES - top, LANES)
    offset = lax.broadcasted_iota(jnp.int32, shape, 0) - lax.broadcasted_iota(jnp.int32, shape, 1) + (top - skip)
    total = jnp.full((8, LANES), jnp.sum(kernel[...]), jnp.float32)
    norm = kernel[...] / total[:1, :1]
    floor_ref[...] = jnp.full(floor_ref.shape, 0.5 * jnp.sum(norm * norm), jnp.float32)
    bands_ref[:, :, :top] = jnp.zeros(bands_ref.shape[:2] + (top, 2 * LANES), jnp.bfloat16)

    def one(row, _):
        band = jnp.zeros(shape, jnp.float32)
        for col in range(ksize):
            band = jnp.where(offset == col, taps[row * ksize + col], band)
        band = band / total[:1]
        for kind, value in enumerate((band, band * band)):
            high = value.astype(jnp.bfloat16)
            bands_ref[kind, row, top:, :LANES] = high
            bands_ref[kind, row, top:, LANES:] = (value - high.astype(jnp.float32)).astype(jnp.bfloat16)
        return 0

    lax.fori_loop(0, ksize, one, 0)


def make_bands(spread_kernel):
    ksize = spread_kernel.shape[0]
    return pl.pallas_call(
        band_kernel,
        in_specs=[pl.BlockSpec(memory_space=pltpu.SMEM), pl.BlockSpec(memory_space=pltpu.VMEM)],
        out_specs=[pl.BlockSpec(memory_space=pltpu.VMEM)] * 2,
        out_shape=[
            jax.ShapeDtypeStruct((2, ksize, 2 * LANES, 2 * LANES), jnp.bfloat16),
            jax.ShapeDtypeStruct((8, LANES), jnp.float32),
        ],
        compiler_params=pltpu.CompilerParams(vmem_limit_bytes=VMEM),
        cost_estimate=pl.CostEstimate(flops=0, bytes_accessed=20 << 20, transcendentals=0),
    )(spread_kernel.reshape(-1), spread_kernel)


def cut_kernel(starts, exposure, noise_var, *chunk_refs):
    height, columns = exposure.shape
    tiles = columns // len(chunk_refs) // LANES
    lane = lax.broadcasted_iota(jnp.int32, (8, LANES), 1)
    for index, ref in enumerate(chunk_refs):
        start = starts[index]
        ahead = jnp.where(start == 0, columns, start) - LANES
        for kind, held in enumerate((exposure, noise_var)):
            for tile in range(tiles):
                at = pl.multiple_of(start + tile * LANES, LANES)
                ref[kind, tile * height : (tile + 1) * height] = held[:, pl.ds(at, LANES)]
            halo = jnp.zeros((8, LANES), jnp.float32)
            for group in range(LANES // HALO):
                rows = held[8 * group : 8 * group + 8, pl.ds(pl.multiple_of(ahead, LANES), LANES)]
                moved = pltpu.roll(rows, (group + 1) * HALO % LANES, 1)
                halo = jnp.where(lane // HALO == group, moved, halo)
            ref[kind, tiles * height :] = halo


def cut(starts, exposure, noise_var, blocks):
    height, columns = exposure.shape
    rows = columns // blocks // LANES * height + height * HALO // LANES
    return pl.pallas_call(
        cut_kernel,
        in_specs=[pl.BlockSpec(memory_space=pltpu.SMEM)] + [pl.BlockSpec(memory_space=pltpu.VMEM)] * 2,
        out_specs=[pl.BlockSpec(memory_space=pltpu.VMEM)] * blocks,
        out_shape=[jax.ShapeDtypeStruct((2, rows, LANES), jnp.float32)] * blocks,
        compiler_params=pltpu.CompilerParams(vmem_limit_bytes=VMEM),
        cost_estimate=pl.CostEstimate(flops=0, bytes_accessed=16 * height * columns, transcendentals=0),
    )(starts, exposure, noise_var)


def pick_kernel(numbers, *refs):
    chunks, (own, edges, chosen) = refs[:-3], refs[-3:]
    epochs, _, count, height, _ = own.shape
    tiles = count - 1
    me, lower, valid = numbers[0], numbers[1], 2 + epochs
    for epoch in range(epochs):
        for step, chunk in enumerate(chunks):

            @pl.when(numbers[2 + epoch] ^ me == step)
            def _():
                chosen[epoch] = chunk[...]

    row_ids = lower * height + lax.broadcasted_iota(jnp.int32, (height, LANES), 0)
    behind = lax.broadcasted_iota(jnp.int32, (8, LANES), 1) >= LANES - HALO
    for epoch in range(epochs):
        first, last = numbers[valid + 2 * epoch], numbers[valid + 2 * epoch + 1]
        usable = jnp.logical_and(row_ids >= first, row_ids < last)
        for tile in range(count):
            if tile:
                value, noise = (chosen[epoch, kind, (tile - 1) * height : tile * height] for kind in range(2))
            else:
                packed = [chosen[epoch, kind, tiles * height :] for kind in range(2)]
                spread = [
                    jnp.concatenate(
                        [
                            jnp.where(behind, pltpu.roll(rows, (LANES - (group + 1) * HALO) % LANES, 1), fill)
                            for group in range(LANES // HALO)
                        ],
                        axis=0,
                    )
                    for rows, fill in zip(packed, (0.0, 1.0))
                ]
                value, noise = spread
            own[epoch, 0, tile] = jnp.where(usable, value / noise, 0.0)
            own[epoch, 1, tile] = jnp.where(usable, 1.0 / noise, 0.0)
    edges[...] = own[:, :, :, pl.ds(pl.multiple_of((1 - lower) * (height - MAXS), MAXS), MAXS)]


def pick(numbers, epochs, chunks, height):
    rows = chunks[0].shape[1]
    tiles = (rows - height * HALO // LANES) // height
    return pl.pallas_call(
        pick_kernel,
        in_specs=[pl.BlockSpec(memory_space=pltpu.SMEM)] + [pl.BlockSpec(memory_space=pltpu.VMEM)] * len(chunks),
        out_specs=[pl.BlockSpec(memory_space=pltpu.VMEM)] * 2,
        out_shape=[
            jax.ShapeDtypeStruct((epochs, 2, tiles + 1, depth, LANES), jnp.float32) for depth in (height, MAXS)
        ],
        scratch_shapes=[pltpu.VMEM((epochs, 2, rows, LANES), jnp.float32)],
        compiler_params=pltpu.CompilerParams(vmem_limit_bytes=VMEM),
        cost_estimate=pl.CostEstimate(flops=0, bytes_accessed=4 << 20, transcendentals=0),
    )(numbers, *chunks)


def correlate_kernel(place, own, border, bands_ref, rows_ref, ext, high, low, summed):
    epochs, kinds, count, height, _ = own.shape
    tiles = count - 1
    ksize = bands_ref.shape[1]
    members = high.shape[2] // (height + 2 * MAXS)
    first, lower = place[0] == 0, place[1]
    at_border = (1 - lower) * (MAXS + height)
    summed_rows = height * members
    blank = pl.ds(pl.multiple_of(lower * (MAXS + height) * members, 8), MAXS * members)
    ext[:, :, blank] = jnp.zeros((kinds, 2, MAXS * members, LANES), jnp.float32)
    nothing = jnp.zeros((height, LANES), jnp.float32)
    keep = jnp.where(first, 0.0, 1.0)

    def put(kind, half, member, value, beyond):
        ext[kind, half, pl.ds(MAXS * members + member, height, stride=members)] = value
        ext[kind, half, pl.ds(at_border * members + member, MAXS, stride=members)] = beyond

    for epoch in range(epochs):
        base = epoch * (tiles + 1)
        for kind in range(kinds):
            for tile in range(1, count):
                put(kind, 1, base + tile - 1, own[epoch, kind, tile], border[epoch, kind, tile])
                if tile < tiles:
                    put(kind, 0, base + tile, own[epoch, kind, tile], border[epoch, kind, tile])
            put(kind, 0, base, own[epoch, kind, 0] * keep, border[epoch, kind, 0] * keep)
            put(kind, 0, base + tiles, own[epoch, kind, 0], border[epoch, kind, 0])
            put(kind, 1, base + tiles, nothing, nothing[:MAXS])

    def split(index, _):
        rows = pl.ds(pl.multiple_of(index * 128, 128), 128)
        for kind in range(kinds):
            for half in range(2):
                value = ext[kind, half, rows]
                part = value.astype(jnp.bfloat16)
                high[kind, half, rows] = part
                low[kind, half, rows] = (value - part.astype(jnp.float32)).astype(jnp.bfloat16)
        return 0

    lax.fori_loop(0, ext.shape[2] // 128, split, 0)

    lane = lax.broadcasted_iota(jnp.int32, (MAXS, LANES), 1)
    wrapped = jnp.logical_and(first, lane < MAXS)
    for kind in range(kinds):
        offsets = [pl.ds((row + MAXS - ksize // 2) * members, summed_rows) for row in range(ksize)]
        upper = jnp.concatenate([high[kind, half, rows] for rows in offsets for half in range(2)], axis=1)
        rest = jnp.concatenate([low[kind, half, rows] for rows in offsets for half in range(2)], axis=1)
        weights = bands_ref[kind].reshape(ksize * 2 * LANES, 2 * LANES)
        pair = jnp.dot(upper, weights, preferred_element_type=jnp.float32)
        more = jnp.dot(rest, weights[:, :LANES], preferred_element_type=jnp.float32)
        summed[...] = pair[:, :LANES] + (pair[:, LANES:] + more)
        for half in range(2):
            start = (1 - lower if half == 0 else lower) * (height - MAXS)
            for epoch in range(epochs):
                base = epoch * (tiles + 1)

                def rows_of(tile):
                    return summed[pl.ds(start * members + base + tile, MAXS, stride=members)]

                rows_ref[half, epoch, kind, 0] = jnp.where(wrapped, rows_of(tiles), rows_of(0))
                for tile in range(1, tiles):
                    rows_ref[half, epoch, kind, tile] = rows_of(tile)


def correlate(place, own, border, bands):
    epochs, kinds, count, height, _ = own.shape
    tiles = count - 1
    members = -(-epochs * (tiles + 1) // 16) * 16
    depth = (height + 2 * MAXS) * members
    flops = 2 * 2 * kinds * members * height * bands.shape[1] * 4 * LANES * LANES
    return pl.pallas_call(
        correlate_kernel,
        in_specs=[pl.BlockSpec(memory_space=pltpu.SMEM)] + [pl.BlockSpec(memory_space=pltpu.VMEM)] * 3,
        out_specs=pl.BlockSpec(memory_space=pltpu.VMEM),
        out_shape=jax.ShapeDtypeStruct((2, epochs, kinds, tiles, MAXS, LANES), jnp.float32),
        scratch_shapes=[
            pltpu.VMEM((kinds, 2, depth, LANES), jnp.float32),
            pltpu.VMEM((kinds, 2, depth, LANES), jnp.bfloat16),
            pltpu.VMEM((kinds, 2, depth, LANES), jnp.bfloat16),
            pltpu.VMEM((height * members, LANES), jnp.float32),
        ],
        compiler_params=pltpu.CompilerParams(vmem_limit_bytes=VMEM),
        cost_estimate=pl.CostEstimate(flops=flops, bytes_accessed=12 << 20, transcendentals=0),
    )(place, own, border, bands)


def stack_kernel(place, shifts, floor, *refs, segments, sources, total, together):
    operands, out_ref = refs[:sources], refs[-6]
    raw, whole, lows, packed, scale = refs[-5:]
    step = pl.program_id(0)
    epochs, slots, reach = whole.shape[:3]
    velocities, height = out_ref.shape[:2]
    fold = height // 8
    steps = sum(len(held) - 1 for held in segments)
    lower = place[steps]
    at = [pl.multiple_of(row, MAXS) for row in (32 - 16 * lower, 16 + 16 * lower, 48 - 48 * lower)]
    blank = pl.multiple_of(48 * lower, MAXS)
    most_psi = ((1 << 23) - 1) // epochs
    most_phi = 255 // epochs * 64 + 63
    lane = lax.broadcasted_iota(jnp.int32, (8, LANES), 1)

    def assemble(first, held):
        tops = [jnp.zeros((MAXS, LANES), jnp.float32) for _ in range(2)]
        for slot, pieces in enumerate(held):
            for epoch in range(epochs):
                for kind in range(2):
                    raw[epoch, kind, slot, pl.ds(blank, MAXS)] = jnp.zeros((MAXS, LANES), jnp.float32)
                    for start, (source, index, tile) in zip(at, pieces):
                        value = operands[source][index, epoch, kind, tile]
                        tops[kind] = jnp.maximum(tops[kind], value if kind else jnp.abs(value))
                        raw[epoch, kind, slot, pl.ds(start, MAXS)] = value
        tops = [jnp.full((8, LANES), jnp.maximum(jnp.max(top), 1e-30), jnp.float32) for top in tops]
        per_psi, per_phi = (most_psi - 1) / tops[0], (most_phi - 1) / tops[1]
        scale[0] = floor[0] * per_phi
        scale[1] = jnp.sqrt(per_phi) / (per_psi * 256.0)

        def quantize(index, _):
            rows = pl.ds(pl.multiple_of(index * 8, 8), 8)
            for epoch in range(epochs):
                for slot in range(len(held)):
                    psi = jnp.floor(raw[epoch, 0, slot, rows] * per_psi + 0.5).astype(jnp.int32)
                    phi = (raw[epoch, 1, slot, rows] * per_phi + 0.5).astype(jnp.int32)
                    whole[epoch, slot, rows] = psi * 256 + (phi >> 6)
                    lows[epoch, slot, rows] = phi & 63
            return 0

        lax.fori_loop(0, reach // 8, quantize, 0, unroll=8)
        for epoch in range(epochs):
            for slot in range(len(held)):
                for top in range(0, reach - 8 * (fold - 1), 8):
                    word = lows[epoch, slot, top : top + 8]
                    for part in range(1, fold):
                        word = word + (lows[epoch, slot, top + 8 * part : top + 8 * part + 8] << (8 * part))
                    packed[epoch, slot, top : top + 8] = word
        for slot in range(len(held)):
            number = place[first + slot] if slot < len(held) - 1 else (place[first + slot - 1] + 1) % total
            for spot, keep in ((slots - 2, lane >= MAXS), (slots - 1, lane < MAXS)):

                @pl.when(number == 0)
                def _():
                    for epoch in range(epochs):
                        for ref in (whole, packed):
                            for top in range(0, ref.shape[2], 8):
                                rows = slice(top, top + 8)
                                ref[epoch, spot, rows] = jnp.where(keep, ref[epoch, slot, rows], 0)

    first, begin = 0, 0
    for held in segments:
        pl.when(step == first)(functools.partial(assemble, first, held))
        begin = jnp.where(step >= first, first, begin)
        first += len(held) - 1

    number = place[step]
    left = jnp.where(number == 0, slots - 2, step - begin)
    right = jnp.where(number == total - 1, slots - 1, step - begin + 1)
    least, unit = scale[0], scale[1]

    def one_velocity(velocity, _):
        start = velocity * epochs * 2
        totals, low_total = [None] * fold, None
        for epoch in range(epochs):
            row, col = shifts[start + 2 * epoch], shifts[start + 2 * epoch + 1]
            beyond, turn = lane < col, (LANES - col) & (LANES - 1)

            def moved(ref, top):
                rows = pl.ds(row + top, 8)
                return pltpu.roll(jnp.where(beyond, ref[epoch, right, rows], ref[epoch, left, rows]), turn, 1)

            for part in range(fold):
                word = moved(whole, 8 * part)
                totals[part] = word if epoch == 0 else totals[part] + word
            word = moved(packed, 0)
            low_total = word if epoch == 0 else low_total + word
        for part in range(fold):
            psi = totals[part].astype(jnp.float32)
            phi = (((totals[part] & 255) << 6) + ((low_total >> (8 * part)) & 255)).astype(jnp.float32)
            out_ref[velocity, 8 * part : 8 * part + 8] = psi * unit * lax.rsqrt(jnp.maximum(phi, least))
        return 0

    lax.fori_loop(0, velocities, one_velocity, 0, unroll=together)


def stack_tiles(numbers, lower, shifts, floor, segments, out, out_shape):
    velocities, height, columns = out_shape.shape
    operands, described = [], []
    for held in segments:
        tiles = []
        for pieces, tile in held:
            spots = []
            for array, index in pieces:
                source = next((i for i, other in enumerate(operands) if other is array), len(operands))
                operands += [array] if source == len(operands) else []
                spots.append((source, index, tile))
            tiles.append(spots)
        described.append(tiles)
    sources, epochs = len(operands), operands[0].shape[1]
    in_specs = [pl.BlockSpec(memory_space=pltpu.VMEM)] * sources
    aliases = {}
    if out is not None:
        in_specs.append(pl.BlockSpec(memory_space=pl.ANY))
        operands.append(out)
        aliases = {3 + sources: 0}
    steps, longest, reach = len(numbers), max(len(held) for held in segments), height + 2 * MAXS
    work = steps * velocities * height * LANES
    return pl.pallas_call(
        functools.partial(
            stack_kernel,
            segments=described,
            sources=sources,
            total=columns // LANES,
            together=next(size for size in (36, 18, 12, 9, 8, 6, 4, 3, 2, 1) if velocities % size == 0),
        ),
        grid_spec=pltpu.PrefetchScalarGridSpec(
            num_scalar_prefetch=3,
            grid=(steps,),
            in_specs=in_specs,
            out_specs=pl.BlockSpec((velocities, height, LANES), lambda step, place, *_: (0, 0, place[step])),
            scratch_shapes=[
                pltpu.VMEM((epochs, 2, longest, reach, LANES), jnp.float32),
                pltpu.VMEM((epochs, longest + 2, reach, LANES), jnp.int32),
                pltpu.VMEM((epochs, longest, reach, LANES), jnp.int32),
                pltpu.VMEM((epochs, longest + 2, reach - height + 8, LANES), jnp.int32),
                pltpu.VMEM((2, 8, LANES), jnp.float32),
            ],
        ),
        out_shape=out_shape,
        input_output_aliases=aliases,
        compiler_params=pltpu.CompilerParams(vmem_limit_bytes=VMEM),
        cost_estimate=pl.CostEstimate(flops=16 * work, bytes_accessed=24 * work, transcendentals=work),
    )(jnp.stack(numbers + [lower]).astype(jnp.int32), shifts + MAXS, floor, *operands)


def local(images, variance, spread_kernel, shifts, epoch_owner, valid_rows):
    exposure, noise_var = images[0], variance[0]
    height, columns = exposure.shape
    blocks = lax.axis_size("vel")
    width = columns // blocks
    me, lower = lax.axis_index("vel"), lax.axis_index("rows")
    swap = [(0, 1), (1, 0)]

    order = list(range(0, blocks, 2)) + list(range(1, blocks, 2))[::-1]
    right = [(order[i], order[(i + 1) % blocks]) for i in range(blocks)]
    left = [(b, a) for a, b in right]

    def position(index):
        return jnp.where(index % 2 == 0, index // 2, blocks - 1 - index // 2)

    mine = position(me)
    place = jnp.stack([mine, lower]).astype(jnp.int32)

    numbers = jnp.concatenate([jnp.stack([me, lower]).astype(jnp.int32), epoch_owner, valid_rows.reshape(-1)])
    starts = position(me ^ jnp.arange(blocks, dtype=jnp.int32)) * width
    chunks = list(cut(starts, exposure, noise_var, blocks))
    for step in range(1, blocks):
        chunks[step] = lax.ppermute(chunks[step], "vel", [(i, i ^ step) for i in range(blocks)])
    chunks[1], spread_kernel, numbers = lax.optimization_barrier((chunks[1], spread_kernel, numbers))
    bands, floor = make_bands(spread_kernel)
    chunks[-1], floor = lax.optimization_barrier((chunks[-1], floor))
    own, edges = pick(numbers, epoch_owner.shape[0], chunks, height)
    payload = correlate(place, own, lax.ppermute(edges, "rows", swap), bands)

    flat_shifts, floor = shifts.reshape(-1), floor[0, :1]
    out_shape = jax.ShapeDtypeStruct((shifts.shape[0], height, columns), jnp.float32)

    tiles, half = payload.shape[3], blocks // 2

    def stack_now(segments, out):
        numbers = [
            (mine + offset) % blocks * tiles + tile for held in segments for offset, tile in held[:-1]
        ]
        held = [[(have[offset], tile) for offset, tile in segment] for segment in segments]
        return stack_tiles(numbers, lower, flat_shifts, floor, held, out, out_shape)

    def block(offset):
        return [(offset, tile) for tile in range(tiles)]

    behind, ahead = lax.ppermute(payload, "vel", right), lax.ppermute(payload, "vel", left)
    border = lax.ppermute(payload[:1], "rows", swap)
    have = {0: ((payload, 0), (payload, 1), (border, 0))}
    out = stack_now([block(0)], None)
    for step in range(1, half + 1):
        if step < half:
            if step > 1:
                behind, ahead = lax.ppermute(behind, "vel", right), lax.ppermute(ahead, "vel", left)
            behind, ahead, out = lax.optimization_barrier((behind, ahead, out))
            border = lax.ppermute(jnp.concatenate([behind[:1], ahead[:1]]), "rows", swap)
            have[-step] = ((behind, 0), (behind, 1), (border, 0))
            have[step] = ((ahead, 0), (ahead, 1), (border, 1))
            segments = [block(-step) + [(1 - step, 0)], [(step - 1, tiles - 1)] + block(step)]
        else:
            behind = lax.ppermute(behind, "vel", right)
            behind, out = lax.optimization_barrier((behind, out))
            border = lax.ppermute(behind[:1], "rows", swap)
            have[step] = ((behind, 0), (behind, 1), (border, 0))
            segments = [[(step - 1, tiles - 1)] + block(step) + [(1 - step, 0)]]
        out = stack_now(segments, out)
    return out


def solution(mesh):
    in_specs = (
        P(("fields", "vel"), "rows", None),
        P(("fields", "vel"), "rows", None),
        P(),
        P(("fields", "vel"), None, None),
        P("fields"),
        P("fields", None),
    )
    out_specs = P(("fields", "vel"), "rows", None)
    return jax.shard_map(local, mesh=mesh, in_specs=in_specs, out_specs=out_specs, check_vma=False)
```

```python
import functools
import jax
import jax.numpy as jnp
from jax import lax
from jax.experimental import pallas as pl
from jax.experimental.pallas import tpu as pltpu
from jax.sharding import PartitionSpec as P

LANES = 128
MAXS = 16
HALO = 32
VMEM = 24 << 20
LARGE = 50 << 20


def band_kernel(taps, kernel, bands_ref, floor_ref):
    ksize = kernel.shape[0]
    skip = LANES - MAXS - ksize // 2
    top = skip // 8 * 8
    shape = (2 * LANES - top, LANES)
    offset = lax.broadcasted_iota(jnp.int32, shape, 0) - lax.broadcasted_iota(jnp.int32, shape, 1) + (top - skip)
    total = jnp.full((8, LANES), jnp.sum(kernel[...]), jnp.float32)
    norm = kernel[...] / total[:1, :1]
    floor_ref[...] = jnp.full(floor_ref.shape, 0.5 * jnp.sum(norm * norm), jnp.float32)
    bands_ref[:, :, :top] = jnp.zeros(bands_ref.shape[:2] + (top, 2 * LANES), jnp.bfloat16)

    def one(row, _):
        band = jnp.zeros(shape, jnp.float32)
        for col in range(ksize):
            band = jnp.where(offset == col, taps[row * ksize + col], band)
        band = band / total[:1]
        for kind, value in enumerate((band, band * band)):
            high = value.astype(jnp.bfloat16)
            bands_ref[kind, row, top:, :LANES] = high
            bands_ref[kind, row, top:, LANES:] = (value - high.astype(jnp.float32)).astype(jnp.bfloat16)
        return 0

    lax.fori_loop(0, ksize, one, 0)


def make_bands(spread_kernel):
    ksize = spread_kernel.shape[0]
    return pl.pallas_call(
        band_kernel,
        in_specs=[pl.BlockSpec(memory_space=pltpu.SMEM), pl.BlockSpec(memory_space=pltpu.VMEM)],
        out_specs=[pl.BlockSpec(memory_space=pltpu.VMEM)] * 2,
        out_shape=[
            jax.ShapeDtypeStruct((2, ksize, 2 * LANES, 2 * LANES), jnp.bfloat16),
            jax.ShapeDtypeStruct((8, LANES), jnp.float32),
        ],
        compiler_params=pltpu.CompilerParams(vmem_limit_bytes=VMEM),
        cost_estimate=pl.CostEstimate(flops=0, bytes_accessed=20 << 20, transcendentals=0),
    )(spread_kernel.reshape(-1), spread_kernel)


def cut_kernel(starts, exposure, noise_var, *chunk_refs):
    height, columns = exposure.shape
    tiles = columns // len(chunk_refs) // LANES
    lane = lax.broadcasted_iota(jnp.int32, (8, LANES), 1)
    for index, ref in enumerate(chunk_refs):
        start = starts[index]
        ahead = jnp.where(start == 0, columns, start) - LANES
        for kind, held in enumerate((exposure, noise_var)):
            for tile in range(tiles):
                at = pl.multiple_of(start + tile * LANES, LANES)
                ref[kind, tile * height : (tile + 1) * height] = held[:, pl.ds(at, LANES)]
            halo = jnp.zeros((8, LANES), jnp.float32)
            for group in range(LANES // HALO):
                rows = held[8 * group : 8 * group + 8, pl.ds(pl.multiple_of(ahead, LANES), LANES)]
                moved = pltpu.roll(rows, (group + 1) * HALO % LANES, 1)
                halo = jnp.where(lane // HALO == group, moved, halo)
            ref[kind, tiles * height :] = halo


def cut(starts, exposure, noise_var, blocks):
    height, columns = exposure.shape
    rows = columns // blocks // LANES * height + height * HALO // LANES
    return pl.pallas_call(
        cut_kernel,
        in_specs=[pl.BlockSpec(memory_space=pltpu.SMEM)] + [pl.BlockSpec(memory_space=pltpu.VMEM)] * 2,
        out_specs=[pl.BlockSpec(memory_space=pltpu.VMEM)] * blocks,
        out_shape=[jax.ShapeDtypeStruct((2, rows, LANES), jnp.float32)] * blocks,
        compiler_params=pltpu.CompilerParams(vmem_limit_bytes=VMEM),
        cost_estimate=pl.CostEstimate(flops=0, bytes_accessed=16 * height * columns, transcendentals=0),
    )(starts, exposure, noise_var)


def pick_kernel(numbers, *refs):
    chunks, (own, edges, chosen) = refs[:-3], refs[-3:]
    epochs, _, count, height, _ = own.shape
    tiles = count - 1
    me, lower, valid = numbers[0], numbers[1], 2 + epochs
    for epoch in range(epochs):
        for step, chunk in enumerate(chunks):

            @pl.when(numbers[2 + epoch] ^ me == step)
            def _():
                chosen[epoch] = chunk[...]

    row_ids = lower * height + lax.broadcasted_iota(jnp.int32, (height, LANES), 0)
    behind = lax.broadcasted_iota(jnp.int32, (8, LANES), 1) >= LANES - HALO
    for epoch in range(epochs):
        first, last = numbers[valid + 2 * epoch], numbers[valid + 2 * epoch + 1]
        usable = jnp.logical_and(row_ids >= first, row_ids < last)
        for tile in range(count):
            if tile:
                value, noise = (chosen[epoch, kind, (tile - 1) * height : tile * height] for kind in range(2))
            else:
                packed = [chosen[epoch, kind, tiles * height :] for kind in range(2)]
                spread = [
                    jnp.concatenate(
                        [
                            jnp.where(behind, pltpu.roll(rows, (LANES - (group + 1) * HALO) % LANES, 1), fill)
                            for group in range(LANES // HALO)
                        ],
                        axis=0,
                    )
                    for rows, fill in zip(packed, (0.0, 1.0))
                ]
                value, noise = spread
            own[epoch, 0, tile] = jnp.where(usable, value / noise, 0.0)
            own[epoch, 1, tile] = jnp.where(usable, 1.0 / noise, 0.0)
    edges[...] = own[:, :, :, pl.ds(pl.multiple_of((1 - lower) * (height - MAXS), MAXS), MAXS)]


def pick(numbers, epochs, chunks, height):
    rows = chunks[0].shape[1]
    tiles = (rows - height * HALO // LANES) // height
    return pl.pallas_call(
        pick_kernel,
        in_specs=[pl.BlockSpec(memory_space=pltpu.SMEM)] + [pl.BlockSpec(memory_space=pltpu.VMEM)] * len(chunks),
        out_specs=[pl.BlockSpec(memory_space=pltpu.VMEM)] * 2,
        out_shape=[
            jax.ShapeDtypeStruct((epochs, 2, tiles + 1, depth, LANES), jnp.float32) for depth in (height, MAXS)
        ],
        scratch_shapes=[pltpu.VMEM((epochs, 2, rows, LANES), jnp.float32)],
        compiler_params=pltpu.CompilerParams(vmem_limit_bytes=VMEM),
        cost_estimate=pl.CostEstimate(flops=0, bytes_accessed=4 << 20, transcendentals=0),
    )(numbers, *chunks)


def correlate_kernel(place, own, border, bands_hbm, rows_ref, ext, high, low, summed, bands_ref, arrived):
    epochs, kinds, count, height, _ = own.shape
    tiles = count - 1
    ksize = bands_ref.shape[1]
    members = high.shape[2] // (height + 2 * MAXS)
    copies = [pltpu.make_async_copy(bands_hbm.at[kind], bands_ref.at[kind], arrived.at[kind]) for kind in range(kinds)]
    for copy in copies:
        copy.start()
    first, lower = place[0] == 0, place[1]
    at_border = (1 - lower) * (MAXS + height)
    summed_rows = height * members
    blank = pl.ds(pl.multiple_of(lower * (MAXS + height) * members, 8), MAXS * members)
    ext[:, :, blank] = jnp.zeros((kinds, 2, MAXS * members, LANES), jnp.float32)
    nothing = jnp.zeros((height, LANES), jnp.float32)
    keep = jnp.where(first, 0.0, 1.0)

    def put(kind, half, member, value, beyond):
        ext[kind, half, pl.ds(MAXS * members + member, height, stride=members)] = value
        ext[kind, half, pl.ds(at_border * members + member, MAXS, stride=members)] = beyond

    for epoch in range(epochs):
        base = epoch * (tiles + 1)
        for kind in range(kinds):
            for tile in range(1, count):
                put(kind, 1, base + tile - 1, own[epoch, kind, tile], border[epoch, kind, tile])
                if tile < tiles:
                    put(kind, 0, base + tile, own[epoch, kind, tile], border[epoch, kind, tile])
            put(kind, 0, base, own[epoch, kind, 0] * keep, border[epoch, kind, 0] * keep)
            put(kind, 0, base + tiles, own[epoch, kind, 0], border[epoch, kind, 0])
            put(kind, 1, base + tiles, nothing, nothing[:MAXS])

    def split(index, _):
        rows = pl.ds(pl.multiple_of(index * 128, 128), 128)
        for kind in range(kinds):
            for half in range(2):
                value = ext[kind, half, rows]
                part = value.astype(jnp.bfloat16)
                high[kind, half, rows] = part
                low[kind, half, rows] = (value - part.astype(jnp.float32)).astype(jnp.bfloat16)
        return 0

    lax.fori_loop(0, ext.shape[2] // 128, split, 0)

    lane = lax.broadcasted_iota(jnp.int32, (MAXS, LANES), 1)
    wrapped = jnp.logical_and(first, lane < MAXS)
    for kind in range(kinds):
        offsets = [pl.ds((row + MAXS - ksize // 2) * members, summed_rows) for row in range(ksize)]
        upper = jnp.concatenate([high[kind, half, rows] for rows in offsets for half in range(2)], axis=1)
        rest = jnp.concatenate([low[kind, half, rows] for rows in offsets for half in range(2)], axis=1)
        copies[kind].wait()
        weights = bands_ref[kind].reshape(ksize * 2 * LANES, 2 * LANES)
        pair = jnp.dot(upper, weights, preferred_element_type=jnp.float32)
        more = jnp.dot(rest, weights[:, :LANES], preferred_element_type=jnp.float32)
        summed[...] = pair[:, :LANES] + (pair[:, LANES:] + more)
        for half in range(2):
            start = (1 - lower if half == 0 else lower) * (height - MAXS)
            for epoch in range(epochs):
                base = epoch * (tiles + 1)

                def rows_of(tile):
                    return summed[pl.ds(start * members + base + tile, MAXS, stride=members)]

                rows_ref[half, epoch, kind, 0] = jnp.where(wrapped, rows_of(tiles), rows_of(0))
                for tile in range(1, tiles):
                    rows_ref[half, epoch, kind, tile] = rows_of(tile)


def correlate(place, own, border, bands):
    epochs, kinds, count, height, _ = own.shape
    tiles = count - 1
    members = -(-epochs * (tiles + 1) // 16) * 16
    depth = (height + 2 * MAXS) * members
    flops = 2 * 2 * kinds * members * height * bands.shape[1] * 4 * LANES * LANES
    return pl.pallas_call(
        correlate_kernel,
        in_specs=[pl.BlockSpec(memory_space=pltpu.SMEM)] + [pl.BlockSpec(memory_space=pltpu.VMEM)] * 2
        + [pl.BlockSpec(memory_space=pltpu.HBM)],
        out_specs=pl.BlockSpec(memory_space=pltpu.VMEM),
        out_shape=jax.ShapeDtypeStruct((2, epochs, kinds, tiles, MAXS, LANES), jnp.float32),
        scratch_shapes=[
            pltpu.VMEM((kinds, 2, depth, LANES), jnp.float32),
            pltpu.VMEM((kinds, 2, depth, LANES), jnp.bfloat16),
            pltpu.VMEM((kinds, 2, depth, LANES), jnp.bfloat16),
            pltpu.VMEM((height * members, LANES), jnp.float32),
            pltpu.VMEM(bands.shape, bands.dtype),
            pltpu.SemaphoreType.DMA((kinds,)),
        ],
        compiler_params=pltpu.CompilerParams(vmem_limit_bytes=LARGE),
        cost_estimate=pl.CostEstimate(flops=flops, bytes_accessed=12 << 20, transcendentals=0),
    )(place, own, border, bands)


def stack_kernel(place, shifts, floor, *refs, segments, sources, total, together):
    operands, out_ref = refs[:sources], refs[-6]
    raw, whole, lows, packed, scale = refs[-5:]
    step = pl.program_id(0)
    epochs, slots, reach = whole.shape[:3]
    velocities, height = out_ref.shape[:2]
    fold = height // 8
    steps = sum(len(held) - 1 for held in segments)
    lower = place[steps]
    at = [pl.multiple_of(row, MAXS) for row in (32 - 16 * lower, 16 + 16 * lower, 48 - 48 * lower)]
    blank = pl.multiple_of(48 * lower, MAXS)
    most_psi = ((1 << 23) - 1) // epochs
    most_phi = 255 // epochs * 64 + 63
    lane = lax.broadcasted_iota(jnp.int32, (8, LANES), 1)

    def assemble(first, held):
        tops = [jnp.zeros((MAXS, LANES), jnp.float32) for _ in range(2)]
        for slot, pieces in enumerate(held):
            for epoch in range(epochs):
                for kind in range(2):
                    raw[epoch, kind, slot, pl.ds(blank, MAXS)] = jnp.zeros((MAXS, LANES), jnp.float32)
                    for start, (source, index, tile) in zip(at, pieces):
                        value = operands[source][index, epoch, kind, tile]
                        tops[kind] = jnp.maximum(tops[kind], value if kind else jnp.abs(value))
                        raw[epoch, kind, slot, pl.ds(start, MAXS)] = value
        tops = [jnp.full((8, LANES), jnp.maximum(jnp.max(top), 1e-30), jnp.float32) for top in tops]
        per_psi, per_phi = (most_psi - 1) / tops[0], (most_phi - 1) / tops[1]
        scale[0] = floor[0] * per_phi
        scale[1] = jnp.sqrt(per_phi) / (per_psi * 256.0)

        def quantize(index, _):
            rows = pl.ds(pl.multiple_of(index * 8, 8), 8)
            for epoch in range(epochs):
                for slot in range(len(held)):
                    psi = jnp.floor(raw[epoch, 0, slot, rows] * per_psi + 0.5).astype(jnp.int32)
                    phi = (raw[epoch, 1, slot, rows] * per_phi + 0.5).astype(jnp.int32)
                    whole[epoch, slot, rows] = psi * 256 + (phi >> 6)
                    lows[epoch, slot, rows] = phi & 63
            return 0

        lax.fori_loop(0, reach // 8, quantize, 0, unroll=8)
        for epoch in range(epochs):
            for slot in range(len(held)):
                for top in range(0, reach - 8 * (fold - 1), 8):
                    word = lows[epoch, slot, top : top + 8]
                    for part in range(1, fold):
                        word = word + (lows[epoch, slot, top + 8 * part : top + 8 * part + 8] << (8 * part))
                    packed[epoch, slot, top : top + 8] = word
        for slot in range(len(held)):
            number = place[first + slot] if slot < len(held) - 1 else (place[first + slot - 1] + 1) % total
            for spot, keep in ((slots - 2, lane >= MAXS), (slots - 1, lane < MAXS)):

                @pl.when(number == 0)
                def _():
                    for epoch in range(epochs):
                        for ref in (whole, packed):
                            for top in range(0, ref.shape[2], 8):
                                rows = slice(top, top + 8)
                                ref[epoch, spot, rows] = jnp.where(keep, ref[epoch, slot, rows], 0)

    first, begin = 0, 0
    for held in segments:
        pl.when(step == first)(functools.partial(assemble, first, held))
        begin = jnp.where(step >= first, first, begin)
        first += len(held) - 1

    number = place[step]
    left = jnp.where(number == 0, slots - 2, step - begin)
    right = jnp.where(number == total - 1, slots - 1, step - begin + 1)
    least, unit = scale[0], scale[1]

    def one_velocity(velocity, _):
        start = velocity * epochs * 2
        totals, low_total = [None] * fold, None
        for epoch in range(epochs):
            row, col = shifts[start + 2 * epoch], shifts[start + 2 * epoch + 1]
            beyond, turn = lane < col, (LANES - col) & (LANES - 1)

            def moved(ref, top):
                rows = pl.ds(row + top, 8)
                return pltpu.roll(jnp.where(beyond, ref[epoch, right, rows], ref[epoch, left, rows]), turn, 1)

            for part in range(fold):
                word = moved(whole, 8 * part)
                totals[part] = word if epoch == 0 else totals[part] + word
            word = moved(packed, 0)
            low_total = word if epoch == 0 else low_total + word
        for part in range(fold):
            psi = totals[part].astype(jnp.float32)
            phi = (((totals[part] & 255) << 6) + ((low_total >> (8 * part)) & 255)).astype(jnp.float32)
            out_ref[velocity, 8 * part : 8 * part + 8] = psi * unit * lax.rsqrt(jnp.maximum(phi, least))
        return 0

    lax.fori_loop(0, velocities, one_velocity, 0, unroll=together)


def stack_tiles(numbers, lower, shifts, floor, segments, out, out_shape):
    velocities, height, columns = out_shape.shape
    operands, described = [], []
    for held in segments:
        tiles = []
        for pieces, tile in held:
            spots = []
            for array, index in pieces:
                source = next((i for i, other in enumerate(operands) if other is array), len(operands))
                operands += [array] if source == len(operands) else []
                spots.append((source, index, tile))
            tiles.append(spots)
        described.append(tiles)
    sources, epochs = len(operands), operands[0].shape[1]
    in_specs = [pl.BlockSpec(memory_space=pltpu.VMEM)] * sources
    aliases = {}
    if out is not None:
        in_specs.append(pl.BlockSpec(memory_space=pl.ANY))
        operands.append(out)
        aliases = {3 + sources: 0}
    steps, longest, reach = len(numbers), max(len(held) for held in segments), height + 2 * MAXS
    work = steps * velocities * height * LANES
    return pl.pallas_call(
        functools.partial(
            stack_kernel,
            segments=described,
            sources=sources,
            total=columns // LANES,
            together=next(size for size in (36, 18, 12, 9, 8, 6, 4, 3, 2, 1) if velocities % size == 0),
        ),
        grid_spec=pltpu.PrefetchScalarGridSpec(
            num_scalar_prefetch=3,
            grid=(steps,),
            in_specs=in_specs,
            out_specs=pl.BlockSpec((velocities, height, LANES), lambda step, place, *_: (0, 0, place[step])),
            scratch_shapes=[
                pltpu.VMEM((epochs, 2, longest, reach, LANES), jnp.float32),
                pltpu.VMEM((epochs, longest + 2, reach, LANES), jnp.int32),
                pltpu.VMEM((epochs, longest, reach, LANES), jnp.int32),
                pltpu.VMEM((epochs, longest + 2, reach - height + 8, LANES), jnp.int32),
                pltpu.VMEM((2, 8, LANES), jnp.float32),
            ],
        ),
        out_shape=out_shape,
        input_output_aliases=aliases,
        compiler_params=pltpu.CompilerParams(vmem_limit_bytes=VMEM),
        cost_estimate=pl.CostEstimate(flops=16 * work, bytes_accessed=24 * work, transcendentals=work),
    )(jnp.stack(numbers + [lower]).astype(jnp.int32), shifts + MAXS, floor, *operands)


def local(images, variance, spread_kernel, shifts, epoch_owner, valid_rows):
    exposure, noise_var = images[0], variance[0]
    height, columns = exposure.shape
    blocks = lax.axis_size("vel")
    width = columns // blocks
    me, lower = lax.axis_index("vel"), lax.axis_index("rows")
    swap = [(0, 1), (1, 0)]

    order = list(range(0, blocks, 2)) + list(range(1, blocks, 2))[::-1]
    right = [(order[i], order[(i + 1) % blocks]) for i in range(blocks)]
    left = [(b, a) for a, b in right]

    def position(index):
        return jnp.where(index % 2 == 0, index // 2, blocks - 1 - index // 2)

    mine = position(me)
    place = jnp.stack([mine, lower]).astype(jnp.int32)

    numbers = jnp.concatenate([jnp.stack([me, lower]).astype(jnp.int32), epoch_owner, valid_rows.reshape(-1)])
    starts = position(me ^ jnp.arange(blocks, dtype=jnp.int32)) * width
    chunks = list(cut(starts, exposure, noise_var, blocks))
    for step in range(1, blocks):
        chunks[step] = lax.ppermute(chunks[step], "vel", [(i, i ^ step) for i in range(blocks)])
    chunks[1], spread_kernel, numbers = lax.optimization_barrier((chunks[1], spread_kernel, numbers))
    bands, floor = make_bands(spread_kernel)
    chunks[-1], floor = lax.optimization_barrier((chunks[-1], floor))
    own, edges = pick(numbers, epoch_owner.shape[0], chunks, height)
    payload = correlate(place, own, lax.ppermute(edges, "rows", swap), bands)

    flat_shifts, floor = shifts.reshape(-1), floor[0, :1]
    out_shape = jax.ShapeDtypeStruct((shifts.shape[0], height, columns), jnp.float32)

    tiles, half = payload.shape[3], blocks // 2

    def stack_now(segments, out):
        numbers = [
            (mine + offset) % blocks * tiles + tile for held in segments for offset, tile in held[:-1]
        ]
        held = [[(have[offset], tile) for offset, tile in segment] for segment in segments]
        return stack_tiles(numbers, lower, flat_shifts, floor, held, out, out_shape)

    def block(offset):
        return [(offset, tile) for tile in range(tiles)]

    behind, ahead = lax.ppermute(payload, "vel", right), lax.ppermute(payload, "vel", left)
    border = lax.ppermute(payload[:1], "rows", swap)
    have = {0: ((payload, 0), (payload, 1), (border, 0))}
    out = stack_now([block(0)], None)
    for step in range(1, half + 1):
        if step < half:
            if step > 1:
                behind, ahead = lax.ppermute(behind, "vel", right), lax.ppermute(ahead, "vel", left)
            behind, ahead, out = lax.optimization_barrier((behind, ahead, out))
            border = lax.ppermute(jnp.concatenate([behind[:1], ahead[:1]]), "rows", swap)
            have[-step] = ((behind, 0), (behind, 1), (border, 0))
            have[step] = ((ahead, 0), (ahead, 1), (border, 1))
            segments = [block(-step) + [(1 - step, 0)], [(step - 1, tiles - 1)] + block(step)]
        else:
            behind = lax.ppermute(behind, "vel", right)
            behind, out = lax.optimization_barrier((behind, out))
            border = lax.ppermute(behind[:1], "rows", swap)
            have[step] = ((behind, 0), (behind, 1), (border, 0))
            segments = [[(step - 1, tiles - 1)] + block(step) + [(1 - step, 0)]]
        out = stack_now(segments, out)
    return out


def solution(mesh):
    in_specs = (
        P(("fields", "vel"), "rows", None),
        P(("fields", "vel"), "rows", None),
        P(),
        P(("fields", "vel"), None, None),
        P("fields"),
        P("fields", None),
    )
    out_specs = P(("fields", "vel"), "rows", None)
    return jax.shard_map(local, mesh=mesh, in_specs=in_specs, out_specs=out_specs, check_vma=False)
```

```python
import functools
import jax
import jax.numpy as jnp
from jax import lax
from jax.experimental import pallas as pl
from jax.experimental.pallas import tpu as pltpu
from jax.sharding import PartitionSpec as P

LANES = 128
MAXS = 16
HALO = 32
VMEM = 24 << 20
LARGE = 50 << 20


FOLD = LANES // HALO


def band_row(row, ksize):
    group, place = row // FOLD, row % FOLD
    base = group * (FOLD + 1) * LANES
    count = min(FOLD, ksize - group * FOLD) if isinstance(row, int) else jnp.minimum(FOLD, ksize - group * FOLD)
    return base + place * LANES, base + count * LANES + place * HALO


def band_kernel(taps, kernel, bands_ref, floor_ref):
    ksize = kernel.shape[0]
    skip = HALO - MAXS - ksize // 2
    shape = (HALO + LANES, LANES)
    offset = lax.broadcasted_iota(jnp.int32, shape, 0) - lax.broadcasted_iota(jnp.int32, shape, 1) - skip
    total = jnp.full((8, LANES), jnp.sum(kernel[...]), jnp.float32)
    norm = kernel[...] / total[:1, :1]
    floor_ref[...] = jnp.full(floor_ref.shape, 0.5 * jnp.sum(norm * norm), jnp.float32)
    bands_ref[:, -LANES:] = jnp.zeros((2, LANES, 2 * LANES), jnp.bfloat16)

    def one(row, _):
        band = jnp.zeros(shape, jnp.float32)
        for col in range(ksize):
            band = jnp.where(offset == col, taps[row * ksize + col], band)
        band = band / total[:1]
        for kind, value in enumerate((band, band * band)):
            high = value.astype(jnp.bfloat16)
            both = jnp.concatenate([high, (value - high.astype(jnp.float32)).astype(jnp.bfloat16)], axis=1)
            main, halo = (pl.multiple_of(at, HALO) for at in band_row(row, ksize))
            bands_ref[kind, pl.ds(main, LANES)] = both[HALO:]
            bands_ref[kind, pl.ds(halo, HALO)] = both[:HALO]
        return 0

    lax.fori_loop(0, ksize, one, 0)


def make_bands(spread_kernel):
    ksize = spread_kernel.shape[0]
    return pl.pallas_call(
        band_kernel,
        in_specs=[pl.BlockSpec(memory_space=pltpu.SMEM), pl.BlockSpec(memory_space=pltpu.VMEM)],
        out_specs=[pl.BlockSpec(memory_space=pltpu.VMEM)] * 2,
        out_shape=[
            jax.ShapeDtypeStruct((2, (ksize - (-ksize // FOLD)) * LANES, 2 * LANES), jnp.bfloat16),
            jax.ShapeDtypeStruct((8, LANES), jnp.float32),
        ],
        compiler_params=pltpu.CompilerParams(vmem_limit_bytes=VMEM),
        cost_estimate=pl.CostEstimate(flops=0, bytes_accessed=20 << 20, transcendentals=0),
    )(spread_kernel.reshape(-1), spread_kernel)


def cut_kernel(starts, exposure, noise_var, *chunk_refs):
    height, columns = exposure.shape
    tiles = columns // len(chunk_refs) // LANES
    lane = lax.broadcasted_iota(jnp.int32, (8, LANES), 1)
    for index, ref in enumerate(chunk_refs):
        start = starts[index]
        ahead = jnp.where(start == 0, columns, start) - LANES
        for kind, held in enumerate((exposure, noise_var)):
            for tile in range(tiles):
                at = pl.multiple_of(start + tile * LANES, LANES)
                ref[kind, tile * height : (tile + 1) * height] = held[:, pl.ds(at, LANES)]
            halo = jnp.zeros((8, LANES), jnp.float32)
            for group in range(LANES // HALO):
                rows = held[8 * group : 8 * group + 8, pl.ds(pl.multiple_of(ahead, LANES), LANES)]
                moved = pltpu.roll(rows, (group + 1) * HALO % LANES, 1)
                halo = jnp.where(lane // HALO == group, moved, halo)
            ref[kind, tiles * height :] = halo


def cut(starts, exposure, noise_var, blocks):
    height, columns = exposure.shape
    rows = columns // blocks // LANES * height + height * HALO // LANES
    return pl.pallas_call(
        cut_kernel,
        in_specs=[pl.BlockSpec(memory_space=pltpu.SMEM)] + [pl.BlockSpec(memory_space=pltpu.VMEM)] * 2,
        out_specs=[pl.BlockSpec(memory_space=pltpu.VMEM)] * blocks,
        out_shape=[jax.ShapeDtypeStruct((2, rows, LANES), jnp.float32)] * blocks,
        compiler_params=pltpu.CompilerParams(vmem_limit_bytes=VMEM),
        cost_estimate=pl.CostEstimate(flops=0, bytes_accessed=16 * height * columns, transcendentals=0),
    )(starts, exposure, noise_var)


def pick_kernel(numbers, *refs):
    chunks, (own, edges, chosen) = refs[:-3], refs[-3:]
    epochs, _, count, height, _ = own.shape
    tiles = count - 1
    me, lower, valid = numbers[0], numbers[1], 2 + epochs
    for epoch in range(epochs):
        for step, chunk in enumerate(chunks):

            @pl.when(numbers[2 + epoch] ^ me == step)
            def _():
                chosen[epoch] = chunk[...]

    row_ids = lower * height + lax.broadcasted_iota(jnp.int32, (height, LANES), 0)
    behind = lax.broadcasted_iota(jnp.int32, (8, LANES), 1) >= LANES - HALO
    for epoch in range(epochs):
        first, last = numbers[valid + 2 * epoch], numbers[valid + 2 * epoch + 1]
        usable = jnp.logical_and(row_ids >= first, row_ids < last)
        for tile in range(count):
            if tile:
                value, noise = (chosen[epoch, kind, (tile - 1) * height : tile * height] for kind in range(2))
            else:
                packed = [chosen[epoch, kind, tiles * height :] for kind in range(2)]
                spread = [
                    jnp.concatenate(
                        [
                            jnp.where(behind, pltpu.roll(rows, (LANES - (group + 1) * HALO) % LANES, 1), fill)
                            for group in range(LANES // HALO)
                        ],
                        axis=0,
                    )
                    for rows, fill in zip(packed, (0.0, 1.0))
                ]
                value, noise = spread
            own[epoch, 0, tile] = jnp.where(usable, value / noise, 0.0)
            own[epoch, 1, tile] = jnp.where(usable, 1.0 / noise, 0.0)
    edges[...] = own[:, :, :, pl.ds(pl.multiple_of((1 - lower) * (height - MAXS), MAXS), MAXS)]


def pick(numbers, epochs, chunks, height):
    rows = chunks[0].shape[1]
    tiles = (rows - height * HALO // LANES) // height
    return pl.pallas_call(
        pick_kernel,
        in_specs=[pl.BlockSpec(memory_space=pltpu.SMEM)] + [pl.BlockSpec(memory_space=pltpu.VMEM)] * len(chunks),
        out_specs=[pl.BlockSpec(memory_space=pltpu.VMEM)] * 2,
        out_shape=[
            jax.ShapeDtypeStruct((epochs, 2, tiles + 1, depth, LANES), jnp.float32) for depth in (height, MAXS)
        ],
        scratch_shapes=[pltpu.VMEM((epochs, 2, rows, LANES), jnp.float32)],
        compiler_params=pltpu.CompilerParams(vmem_limit_bytes=VMEM),
        cost_estimate=pl.CostEstimate(flops=0, bytes_accessed=4 << 20, transcendentals=0),
    )(numbers, *chunks)


def correlate_kernel(place, own, border, bands_hbm, rows_ref, ext, high, low, summed, bands_ref, arrived, *, ksize):
    epochs, kinds, count, height, _ = own.shape
    tiles = count - 1
    members = high.shape[2] // (height + 2 * MAXS)
    copies = [pltpu.make_async_copy(bands_hbm.at[kind], bands_ref.at[kind], arrived.at[kind]) for kind in range(kinds)]
    for copy in copies:
        copy.start()
    first, lower = place[0] == 0, place[1]
    at_border = (1 - lower) * (MAXS + height)
    summed_rows = height * members
    blank = pl.ds(pl.multiple_of(lower * (MAXS + height) * members, 8), MAXS * members)
    ext[:, :, blank] = jnp.zeros((kinds, 2, MAXS * members, LANES), jnp.float32)
    nothing = jnp.zeros((height, LANES), jnp.float32)
    keep = jnp.where(first, 0.0, 1.0)

    def put(kind, half, member, value, beyond):
        ext[kind, half, pl.ds(MAXS * members + member, height, stride=members)] = value
        ext[kind, half, pl.ds(at_border * members + member, MAXS, stride=members)] = beyond

    for epoch in range(epochs):
        base = epoch * (tiles + 1)
        for kind in range(kinds):
            for tile in range(1, count):
                put(kind, 1, base + tile - 1, own[epoch, kind, tile], border[epoch, kind, tile])
                if tile < tiles:
                    put(kind, 0, base + tile, own[epoch, kind, tile], border[epoch, kind, tile])
            put(kind, 0, base, own[epoch, kind, 0] * keep, border[epoch, kind, 0] * keep)
            put(kind, 0, base + tiles, own[epoch, kind, 0], border[epoch, kind, 0])
            put(kind, 1, base + tiles, nothing, nothing[:MAXS])

    lanes = lax.broadcasted_iota(jnp.int32, (128, LANES), 1)

    def split(index, _):
        rows = pl.ds(pl.multiple_of(index * 128, 128), 128)
        for kind in range(kinds):
            halo = jnp.zeros((128, LANES), jnp.float32)
            for fold in range(FOLD):
                ahead = ext[kind, 0, pl.ds(pl.multiple_of(index * 128 + fold * members, 16), 128)]
                halo = jnp.where(lanes // HALO == fold, pltpu.roll(ahead, (fold + 1) * HALO % LANES, 1), halo)
            for half, value in enumerate((halo, ext[kind, 1, rows])):
                part = value.astype(jnp.bfloat16)
                high[kind, half, rows] = part
                low[kind, half, rows] = (value - part.astype(jnp.float32)).astype(jnp.bfloat16)
        return 0

    lax.fori_loop(0, high.shape[2] // 128, split, 0, unroll=4)

    lane = lax.broadcasted_iota(jnp.int32, (MAXS, LANES), 1)
    wrapped = jnp.logical_and(first, lane < MAXS)
    for kind in range(kinds):
        offsets = [pl.ds((row + MAXS - ksize // 2) * members, summed_rows) for row in range(ksize)]
        parts = []
        for base in range(0, ksize, FOLD):
            parts += [(1, rows) for rows in offsets[base : base + FOLD]] + [(0, offsets[base])]
        upper = jnp.concatenate([high[kind, half, rows] for half, rows in parts], axis=1)
        rest = jnp.concatenate([low[kind, half, rows] for half, rows in parts], axis=1)
        copies[kind].wait()
        weights = bands_ref[kind]
        pair = jnp.dot(upper, weights, preferred_element_type=jnp.float32)
        more = jnp.dot(rest, weights[:, :LANES], preferred_element_type=jnp.float32)
        summed[...] = pair[:, :LANES] + (pair[:, LANES:] + more)
        for half in range(2):
            start = (1 - lower if half == 0 else lower) * (height - MAXS)
            for epoch in range(epochs):
                base = epoch * (tiles + 1)

                def rows_of(tile):
                    return summed[pl.ds(start * members + base + tile, MAXS, stride=members)]

                rows_ref[half, epoch, kind, 0] = jnp.where(wrapped, rows_of(tiles), rows_of(0))
                for tile in range(1, tiles):
                    rows_ref[half, epoch, kind, tile] = rows_of(tile)


def correlate(place, own, border, bands, ksize):
    epochs, kinds, count, height, _ = own.shape
    tiles = count - 1
    members = -(-epochs * (tiles + 1) // 16) * 16
    depth = (height + 2 * MAXS) * members
    flops = 2 * 2 * kinds * members * height * bands.shape[1] * 2 * LANES
    return pl.pallas_call(
        functools.partial(correlate_kernel, ksize=ksize),
        in_specs=[pl.BlockSpec(memory_space=pltpu.SMEM)] + [pl.BlockSpec(memory_space=pltpu.VMEM)] * 2
        + [pl.BlockSpec(memory_space=pltpu.HBM)],
        out_specs=pl.BlockSpec(memory_space=pltpu.VMEM),
        out_shape=jax.ShapeDtypeStruct((2, epochs, kinds, tiles, MAXS, LANES), jnp.float32),
        scratch_shapes=[
            pltpu.VMEM((kinds, 2, depth + (FOLD - 1) * members, LANES), jnp.float32),
            pltpu.VMEM((kinds, 2, depth, LANES), jnp.bfloat16),
            pltpu.VMEM((kinds, 2, depth, LANES), jnp.bfloat16),
            pltpu.VMEM((height * members, LANES), jnp.float32),
            pltpu.VMEM(bands.shape, bands.dtype),
            pltpu.SemaphoreType.DMA((kinds,)),
        ],
        compiler_params=pltpu.CompilerParams(vmem_limit_bytes=LARGE),
        cost_estimate=pl.CostEstimate(flops=flops, bytes_accessed=12 << 20, transcendentals=0),
    )(place, own, border, bands)


def stack_kernel(place, shifts, floor, *refs, segments, sources, total, together):
    operands, out_ref = refs[:sources], refs[-6]
    raw, whole, lows, packed, scale = refs[-5:]
    step = pl.program_id(0)
    epochs, slots, reach = whole.shape[:3]
    velocities, height = out_ref.shape[:2]
    fold = height // 8
    steps = sum(len(held) - 1 for held in segments)
    lower = place[steps]
    at = [pl.multiple_of(row, MAXS) for row in (32 - 16 * lower, 16 + 16 * lower, 48 - 48 * lower)]
    blank = pl.multiple_of(48 * lower, MAXS)
    most_psi = ((1 << 23) - 1) // epochs
    most_phi = 255 // epochs * 64 + 63
    lane = lax.broadcasted_iota(jnp.int32, (8, LANES), 1)

    def assemble(first, held):
        tops = [jnp.zeros((MAXS, LANES), jnp.float32) for _ in range(2)]
        for slot, pieces in enumerate(held):
            for epoch in range(epochs):
                for kind in range(2):
                    raw[epoch, kind, slot, pl.ds(blank, MAXS)] = jnp.zeros((MAXS, LANES), jnp.float32)
                    for start, (source, index, tile) in zip(at, pieces):
                        value = operands[source][index, epoch, kind, tile]
                        tops[kind] = jnp.maximum(tops[kind], value if kind else jnp.abs(value))
                        raw[epoch, kind, slot, pl.ds(start, MAXS)] = value
        tops = [jnp.full((8, LANES), jnp.maximum(jnp.max(top), 1e-30), jnp.float32) for top in tops]
        per_psi, per_phi = (most_psi - 1) / tops[0], (most_phi - 1) / tops[1]
        scale[0] = floor[0] * per_phi
        scale[1] = jnp.sqrt(per_phi) / (per_psi * 256.0)

        def quantize(index, _):
            rows = pl.ds(pl.multiple_of(index * 8, 8), 8)
            for epoch in range(epochs):
                for slot in range(len(held)):
                    psi = jnp.floor(raw[epoch, 0, slot, rows] * per_psi + 0.5).astype(jnp.int32)
                    phi = (raw[epoch, 1, slot, rows] * per_phi + 0.5).astype(jnp.int32)
                    whole[epoch, slot, rows] = psi * 256 + (phi >> 6)
                    lows[epoch, slot, rows] = phi & 63
            return 0

        lax.fori_loop(0, reach // 8, quantize, 0, unroll=8)
        for epoch in range(epochs):
            for slot in range(len(held)):
                for top in range(0, reach - 8 * (fold - 1), 8):
                    word = lows[epoch, slot, top : top + 8]
                    for part in range(1, fold):
                        word = word + (lows[epoch, slot, top + 8 * part : top + 8 * part + 8] << (8 * part))
                    packed[epoch, slot, top : top + 8] = word
        for slot in range(len(held)):
            number = place[first + slot] if slot < len(held) - 1 else (place[first + slot - 1] + 1) % total
            for spot, keep in ((slots - 2, lane >= MAXS), (slots - 1, lane < MAXS)):

                @pl.when(number == 0)
                def _():
                    for epoch in range(epochs):
                        for ref in (whole, packed):
                            for top in range(0, ref.shape[2], 8):
                                rows = slice(top, top + 8)
                                ref[epoch, spot, rows] = jnp.where(keep, ref[epoch, slot, rows], 0)

    first, begin = 0, 0
    for held in segments:
        pl.when(step == first)(functools.partial(assemble, first, held))
        begin = jnp.where(step >= first, first, begin)
        first += len(held) - 1

    number = place[step]
    left = jnp.where(number == 0, slots - 2, step - begin)
    right = jnp.where(number == total - 1, slots - 1, step - begin + 1)
    least, unit = scale[0], scale[1]

    def one_velocity(velocity, _):
        start = velocity * epochs * 2
        totals, low_total = [None] * fold, None
        for epoch in range(epochs):
            row, col = shifts[start + 2 * epoch], shifts[start + 2 * epoch + 1]
            beyond, turn = lane < col, (LANES - col) & (LANES - 1)

            def moved(ref, top):
                rows = pl.ds(row + top, 8)
                return pltpu.roll(jnp.where(beyond, ref[epoch, right, rows], ref[epoch, left, rows]), turn, 1)

            for part in range(fold):
                word = moved(whole, 8 * part)
                totals[part] = word if epoch == 0 else totals[part] + word
            word = moved(packed, 0)
            low_total = word if epoch == 0 else low_total + word
        for part in range(fold):
            psi = totals[part].astype(jnp.float32)
            phi = (((totals[part] & 255) << 6) + ((low_total >> (8 * part)) & 255)).astype(jnp.float32)
            out_ref[velocity, 8 * part : 8 * part + 8] = psi * unit * lax.rsqrt(jnp.maximum(phi, least))
        return 0

    lax.fori_loop(0, velocities, one_velocity, 0, unroll=together)


def stack_tiles(numbers, lower, shifts, floor, segments, out, out_shape):
    velocities, height, columns = out_shape.shape
    operands, described = [], []
    for held in segments:
        tiles = []
        for pieces, tile in held:
            spots = []
            for array, index in pieces:
                source = next((i for i, other in enumerate(operands) if other is array), len(operands))
                operands += [array] if source == len(operands) else []
                spots.append((source, index, tile))
            tiles.append(spots)
        described.append(tiles)
    sources, epochs = len(operands), operands[0].shape[1]
    in_specs = [pl.BlockSpec(memory_space=pltpu.VMEM)] * sources
    aliases = {}
    if out is not None:
        in_specs.append(pl.BlockSpec(memory_space=pl.ANY))
        operands.append(out)
        aliases = {3 + sources: 0}
    steps, longest, reach = len(numbers), max(len(held) for held in segments), height + 2 * MAXS
    work = steps * velocities * height * LANES
    return pl.pallas_call(
        functools.partial(
            stack_kernel,
            segments=described,
            sources=sources,
            total=columns // LANES,
            together=next(size for size in (36, 18, 12, 9, 8, 6, 4, 3, 2, 1) if velocities % size == 0),
        ),
        grid_spec=pltpu.PrefetchScalarGridSpec(
            num_scalar_prefetch=3,
            grid=(steps,),
            in_specs=in_specs,
            out_specs=pl.BlockSpec((velocities, height, LANES), lambda step, place, *_: (0, 0, place[step])),
            scratch_shapes=[
                pltpu.VMEM((epochs, 2, longest, reach, LANES), jnp.float32),
                pltpu.VMEM((epochs, longest + 2, reach, LANES), jnp.int32),
                pltpu.VMEM((epochs, longest, reach, LANES), jnp.int32),
                pltpu.VMEM((epochs, longest + 2, reach - height + 8, LANES), jnp.int32),
                pltpu.VMEM((2, 8, LANES), jnp.float32),
            ],
        ),
        out_shape=out_shape,
        input_output_aliases=aliases,
        compiler_params=pltpu.CompilerParams(vmem_limit_bytes=VMEM),
        cost_estimate=pl.CostEstimate(flops=16 * work, bytes_accessed=24 * work, transcendentals=work),
    )(jnp.stack(numbers + [lower]).astype(jnp.int32), shifts + MAXS, floor, *operands)


def local(images, variance, spread_kernel, shifts, epoch_owner, valid_rows):
    exposure, noise_var = images[0], variance[0]
    height, columns = exposure.shape
    blocks = lax.axis_size("vel")
    width = columns // blocks
    me, lower = lax.axis_index("vel"), lax.axis_index("rows")
    swap = [(0, 1), (1, 0)]

    order = list(range(0, blocks, 2)) + list(range(1, blocks, 2))[::-1]
    right = [(order[i], order[(i + 1) % blocks]) for i in range(blocks)]
    left = [(b, a) for a, b in right]

    def position(index):
        return jnp.where(index % 2 == 0, index // 2, blocks - 1 - index // 2)

    mine = position(me)
    place = jnp.stack([mine, lower]).astype(jnp.int32)

    numbers = jnp.concatenate([jnp.stack([me, lower]).astype(jnp.int32), epoch_owner, valid_rows.reshape(-1)])
    starts = position(me ^ jnp.arange(blocks, dtype=jnp.int32)) * width
    chunks = list(cut(starts, exposure, noise_var, blocks))
    for step in range(1, blocks):
        chunks[step] = lax.ppermute(chunks[step], "vel", [(i, i ^ step) for i in range(blocks)])
    chunks[1], spread_kernel, numbers = lax.optimization_barrier((chunks[1], spread_kernel, numbers))
    bands, floor = make_bands(spread_kernel)
    chunks[-1], floor = lax.optimization_barrier((chunks[-1], floor))
    own, edges = pick(numbers, epoch_owner.shape[0], chunks, height)
    payload = correlate(place, own, lax.ppermute(edges, "rows", swap), bands, spread_kernel.shape[0])

    flat_shifts, floor = shifts.reshape(-1), floor[0, :1]
    out_shape = jax.ShapeDtypeStruct((shifts.shape[0], height, columns), jnp.float32)

    tiles, half = payload.shape[3], blocks // 2

    def stack_now(segments, out):
        numbers = [
            (mine + offset) % blocks * tiles + tile for held in segments for offset, tile in held[:-1]
        ]
        held = [[(have[offset], tile) for offset, tile in segment] for segment in segments]
        return stack_tiles(numbers, lower, flat_shifts, floor, held, out, out_shape)

    def block(offset):
        return [(offset, tile) for tile in range(tiles)]

    behind, ahead = lax.ppermute(payload, "vel", right), lax.ppermute(payload, "vel", left)
    border = lax.ppermute(payload[:1], "rows", swap)
    have = {0: ((payload, 0), (payload, 1), (border, 0))}
    out = stack_now([block(0)], None)
    for step in range(1, half + 1):
        if step < half:
            if step > 1:
                behind, ahead = lax.ppermute(behind, "vel", right), lax.ppermute(ahead, "vel", left)
            behind, ahead, out = lax.optimization_barrier((behind, ahead, out))
            border = lax.ppermute(jnp.concatenate([behind[:1], ahead[:1]]), "rows", swap)
            have[-step] = ((behind, 0), (behind, 1), (border, 0))
            have[step] = ((ahead, 0), (ahead, 1), (border, 1))
            segments = [block(-step) + [(1 - step, 0)], [(step - 1, tiles - 1)] + block(step)]
        else:
            behind = lax.ppermute(behind, "vel", right)
            behind, out = lax.optimization_barrier((behind, out))
            border = lax.ppermute(behind[:1], "rows", swap)
            have[step] = ((behind, 0), (behind, 1), (border, 0))
            segments = [[(step - 1, tiles - 1)] + block(step) + [(1 - step, 0)]]
        out = stack_now(segments, out)
    return out


def solution(mesh):
    in_specs = (
        P(("fields", "vel"), "rows", None),
        P(("fields", "vel"), "rows", None),
        P(),
        P(("fields", "vel"), None, None),
        P("fields"),
        P("fields", None),
    )
    out_specs = P(("fields", "vel"), "rows", None)
    return jax.shard_map(local, mesh=mesh, in_specs=in_specs, out_specs=out_specs, check_vma=False)
```

```python
import functools
import jax
import jax.numpy as jnp
from jax import lax
from jax.experimental import pallas as pl
from jax.experimental.pallas import tpu as pltpu
from jax.sharding import PartitionSpec as P

LANES = 128
MAXS = 16
HALO = 32
VMEM = 24 << 20
LARGE = 50 << 20


FOLD = LANES // HALO


def band_row(row, ksize):
    group, place = row // FOLD, row % FOLD
    base = group * (FOLD + 1) * LANES
    count = min(FOLD, ksize - group * FOLD) if isinstance(row, int) else jnp.minimum(FOLD, ksize - group * FOLD)
    return base + place * LANES, base + count * LANES + place * HALO


def band_kernel(taps, kernel, bands_ref, floor_ref):
    ksize = kernel.shape[0]
    skip = HALO - MAXS - ksize // 2
    shape = (HALO + LANES, LANES)
    offset = lax.broadcasted_iota(jnp.int32, shape, 0) - lax.broadcasted_iota(jnp.int32, shape, 1) - skip
    total = jnp.full((8, LANES), jnp.sum(kernel[...]), jnp.float32)
    norm = kernel[...] / total[:1, :1]
    floor_ref[...] = jnp.full(floor_ref.shape, 0.5 * jnp.sum(norm * norm), jnp.float32)
    bands_ref[:, -LANES:] = jnp.zeros((2, LANES, 2 * LANES), jnp.bfloat16)

    def one(row, _):
        band = jnp.zeros(shape, jnp.float32)
        for col in range(ksize):
            band = jnp.where(offset == col, taps[row * ksize + col], band)
        band = band / total[:1]
        for kind, value in enumerate((band, band * band)):
            high = value.astype(jnp.bfloat16)
            both = jnp.concatenate([high, (value - high.astype(jnp.float32)).astype(jnp.bfloat16)], axis=1)
            main, halo = (pl.multiple_of(at, HALO) for at in band_row(row, ksize))
            bands_ref[kind, pl.ds(main, LANES)] = both[HALO:]
            bands_ref[kind, pl.ds(halo, HALO)] = both[:HALO]
        return 0

    lax.fori_loop(0, ksize, one, 0)


def make_bands(spread_kernel):
    ksize = spread_kernel.shape[0]
    return pl.pallas_call(
        band_kernel,
        in_specs=[pl.BlockSpec(memory_space=pltpu.SMEM), pl.BlockSpec(memory_space=pltpu.VMEM)],
        out_specs=[pl.BlockSpec(memory_space=pltpu.VMEM)] * 2,
        out_shape=[
            jax.ShapeDtypeStruct((2, (ksize - (-ksize // FOLD)) * LANES, 2 * LANES), jnp.bfloat16),
            jax.ShapeDtypeStruct((8, LANES), jnp.float32),
        ],
        compiler_params=pltpu.CompilerParams(vmem_limit_bytes=VMEM),
        cost_estimate=pl.CostEstimate(flops=0, bytes_accessed=20 << 20, transcendentals=0),
    )(spread_kernel.reshape(-1), spread_kernel)


def cut_kernel(starts, pair, *chunk_refs):
    _, height, columns = pair.shape
    tiles = columns // len(chunk_refs) // LANES
    lane = lax.broadcasted_iota(jnp.int32, (8, LANES), 1)
    for index, ref in enumerate(chunk_refs):
        start = starts[index]
        ahead = jnp.where(start == 0, columns, start) - LANES
        for kind in range(2):
            for tile in range(tiles):
                at = pl.multiple_of(start + tile * LANES, LANES)
                ref[kind, tile * height : (tile + 1) * height] = pair[kind, :, pl.ds(at, LANES)]
            halo = jnp.zeros((8, LANES), jnp.float32)
            for group in range(LANES // HALO):
                rows = pair[kind, 8 * group : 8 * group + 8, pl.ds(pl.multiple_of(ahead, LANES), LANES)]
                moved = pltpu.roll(rows, (group + 1) * HALO % LANES, 1)
                halo = jnp.where(lane // HALO == group, moved, halo)
            ref[kind, tiles * height :] = halo


def cut(starts, pair, blocks):
    _, height, columns = pair.shape
    rows = columns // blocks // LANES * height + height * HALO // LANES
    return pl.pallas_call(
        cut_kernel,
        in_specs=[pl.BlockSpec(memory_space=pltpu.SMEM), pl.BlockSpec(memory_space=pltpu.VMEM)],
        out_specs=[pl.BlockSpec(memory_space=pltpu.VMEM)] * blocks,
        out_shape=[jax.ShapeDtypeStruct((2, rows, LANES), jnp.float32)] * blocks,
        compiler_params=pltpu.CompilerParams(vmem_limit_bytes=VMEM),
        cost_estimate=pl.CostEstimate(flops=0, bytes_accessed=16 * height * columns, transcendentals=0),
    )(starts, pair)


def pick_kernel(numbers, *refs):
    chunks, (own, edges, chosen) = refs[:-3], refs[-3:]
    epochs, _, count, height, _ = own.shape
    tiles = count - 1
    me, lower, valid = numbers[0], numbers[1], 2 + epochs
    for epoch in range(epochs):
        for step, chunk in enumerate(chunks):

            @pl.when(numbers[2 + epoch] ^ me == step)
            def _():
                chosen[epoch] = chunk[...]

    row_ids = lower * height + lax.broadcasted_iota(jnp.int32, (height, LANES), 0)
    behind = lax.broadcasted_iota(jnp.int32, (8, LANES), 1) >= LANES - HALO
    for epoch in range(epochs):
        first, last = numbers[valid + 2 * epoch], numbers[valid + 2 * epoch + 1]
        usable = jnp.logical_and(row_ids >= first, row_ids < last)
        for tile in range(count):
            if tile:
                value, noise = (chosen[epoch, kind, (tile - 1) * height : tile * height] for kind in range(2))
            else:
                packed = [chosen[epoch, kind, tiles * height :] for kind in range(2)]
                spread = [
                    jnp.concatenate(
                        [
                            jnp.where(behind, pltpu.roll(rows, (LANES - (group + 1) * HALO) % LANES, 1), fill)
                            for group in range(LANES // HALO)
                        ],
                        axis=0,
                    )
                    for rows, fill in zip(packed, (0.0, 1.0))
                ]
                value, noise = spread
            own[epoch, 0, tile] = jnp.where(usable, value / noise, 0.0)
            own[epoch, 1, tile] = jnp.where(usable, 1.0 / noise, 0.0)
    edges[...] = own[:, :, :, pl.ds(pl.multiple_of((1 - lower) * (height - MAXS), MAXS), MAXS)]


def pick(numbers, epochs, chunks, height):
    rows = chunks[0].shape[1]
    tiles = (rows - height * HALO // LANES) // height
    return pl.pallas_call(
        pick_kernel,
        in_specs=[pl.BlockSpec(memory_space=pltpu.SMEM)] + [pl.BlockSpec(memory_space=pltpu.VMEM)] * len(chunks),
        out_specs=[pl.BlockSpec(memory_space=pltpu.VMEM)] * 2,
        out_shape=[
            jax.ShapeDtypeStruct((epochs, 2, tiles + 1, depth, LANES), jnp.float32) for depth in (height, MAXS)
        ],
        scratch_shapes=[pltpu.VMEM((epochs, 2, rows, LANES), jnp.float32)],
        compiler_params=pltpu.CompilerParams(vmem_limit_bytes=VMEM),
        cost_estimate=pl.CostEstimate(flops=0, bytes_accessed=4 << 20, transcendentals=0),
    )(numbers, *chunks)


def correlate_kernel(place, own, border, bands_hbm, rows_ref, ext, high, low, summed, bands_ref, arrived, *, ksize):
    epochs, kinds, count, height, _ = own.shape
    tiles = count - 1
    members = high.shape[2] // (height + 2 * MAXS)
    copies = [pltpu.make_async_copy(bands_hbm.at[kind], bands_ref.at[kind], arrived.at[kind]) for kind in range(kinds)]
    for copy in copies:
        copy.start()
    first, lower = place[0] == 0, place[1]
    at_border = (1 - lower) * (MAXS + height)
    summed_rows = height * members
    blank = pl.ds(pl.multiple_of(lower * (MAXS + height) * members, 8), MAXS * members)
    ext[:, :, blank] = jnp.zeros((kinds, 2, MAXS * members, LANES), jnp.float32)
    nothing = jnp.zeros((height, LANES), jnp.float32)
    keep = jnp.where(first, 0.0, 1.0)

    def put(kind, half, member, value, beyond):
        ext[kind, half, pl.ds(MAXS * members + member, height, stride=members)] = value
        ext[kind, half, pl.ds(at_border * members + member, MAXS, stride=members)] = beyond

    for epoch in range(epochs):
        base = epoch * (tiles + 1)
        for kind in range(kinds):
            for tile in range(1, count):
                put(kind, 1, base + tile - 1, own[epoch, kind, tile], border[epoch, kind, tile])
                if tile < tiles:
                    put(kind, 0, base + tile, own[epoch, kind, tile], border[epoch, kind, tile])
            put(kind, 0, base, own[epoch, kind, 0] * keep, border[epoch, kind, 0] * keep)
            put(kind, 0, base + tiles, own[epoch, kind, 0], border[epoch, kind, 0])
            put(kind, 1, base + tiles, nothing, nothing[:MAXS])

    lanes = lax.broadcasted_iota(jnp.int32, (128, LANES), 1)

    def split(index, _):
        rows = pl.ds(pl.multiple_of(index * 128, 128), 128)
        for kind in range(kinds):
            halo = jnp.zeros((128, LANES), jnp.float32)
            for fold in range(FOLD):
                ahead = ext[kind, 0, pl.ds(pl.multiple_of(index * 128 + fold * members, 16), 128)]
                halo = jnp.where(lanes // HALO == fold, pltpu.roll(ahead, (fold + 1) * HALO % LANES, 1), halo)
            for half, value in enumerate((halo, ext[kind, 1, rows])):
                part = value.astype(jnp.bfloat16)
                high[kind, half, rows] = part
                low[kind, half, rows] = (value - part.astype(jnp.float32)).astype(jnp.bfloat16)
        return 0

    lax.fori_loop(0, high.shape[2] // 128, split, 0, unroll=4)

    lane = lax.broadcasted_iota(jnp.int32, (MAXS, LANES), 1)
    wrapped = jnp.logical_and(first, lane < MAXS)
    for kind in range(kinds):
        offsets = [pl.ds((row + MAXS - ksize // 2) * members, summed_rows) for row in range(ksize)]
        parts = []
        for base in range(0, ksize, FOLD):
            parts += [(1, rows) for rows in offsets[base : base + FOLD]] + [(0, offsets[base])]
        upper = jnp.concatenate([high[kind, half, rows] for half, rows in parts], axis=1)
        rest = jnp.concatenate([low[kind, half, rows] for half, rows in parts], axis=1)
        copies[kind].wait()
        weights = bands_ref[kind]
        pair = jnp.dot(upper, weights, preferred_element_type=jnp.float32)
        more = jnp.dot(rest, weights[:, :LANES], preferred_element_type=jnp.float32)
        summed[...] = pair[:, :LANES] + (pair[:, LANES:] + more)
        for half in range(2):
            start = (1 - lower if half == 0 else lower) * (height - MAXS)
            for epoch in range(epochs):
                base = epoch * (tiles + 1)

                def rows_of(tile):
                    return summed[pl.ds(start * members + base + tile, MAXS, stride=members)]

                rows_ref[half, epoch, kind, 0] = jnp.where(wrapped, rows_of(tiles), rows_of(0))
                for tile in range(1, tiles):
                    rows_ref[half, epoch, kind, tile] = rows_of(tile)


def correlate(place, own, border, bands, ksize):
    epochs, kinds, count, height, _ = own.shape
    tiles = count - 1
    members = -(-epochs * (tiles + 1) // 16) * 16
    depth = (height + 2 * MAXS) * members
    flops = 2 * 2 * kinds * members * height * bands.shape[1] * 2 * LANES
    return pl.pallas_call(
        functools.partial(correlate_kernel, ksize=ksize),
        in_specs=[pl.BlockSpec(memory_space=pltpu.SMEM)] + [pl.BlockSpec(memory_space=pltpu.VMEM)] * 2
        + [pl.BlockSpec(memory_space=pltpu.HBM)],
        out_specs=pl.BlockSpec(memory_space=pltpu.VMEM),
        out_shape=jax.ShapeDtypeStruct((2, epochs, kinds, tiles, MAXS, LANES), jnp.float32),
        scratch_shapes=[
            pltpu.VMEM((kinds, 2, depth + (FOLD - 1) * members, LANES), jnp.float32),
            pltpu.VMEM((kinds, 2, depth, LANES), jnp.bfloat16),
            pltpu.VMEM((kinds, 2, depth, LANES), jnp.bfloat16),
            pltpu.VMEM((height * members, LANES), jnp.float32),
            pltpu.VMEM(bands.shape, bands.dtype),
            pltpu.SemaphoreType.DMA((kinds,)),
        ],
        compiler_params=pltpu.CompilerParams(vmem_limit_bytes=LARGE),
        cost_estimate=pl.CostEstimate(flops=flops, bytes_accessed=12 << 20, transcendentals=0),
    )(place, own, border, bands)


def stack_kernel(place, shifts, floor, *refs, segments, sources, total, together):
    operands, out_ref = refs[:sources], refs[-6]
    raw, whole, lows, packed, scale = refs[-5:]
    step = pl.program_id(0)
    epochs, slots, reach = whole.shape[:3]
    velocities, height = out_ref.shape[:2]
    fold = height // 8
    steps = sum(len(held) - 1 for held in segments)
    lower = place[steps]
    at = [pl.multiple_of(row, MAXS) for row in (32 - 16 * lower, 16 + 16 * lower, 48 - 48 * lower)]
    blank = pl.multiple_of(48 * lower, MAXS)
    most_psi = ((1 << 23) - 1) // epochs
    most_phi = 255 // epochs * 64 + 63
    lane = lax.broadcasted_iota(jnp.int32, (8, LANES), 1)

    def assemble(first, held):
        tops = [jnp.zeros((MAXS, LANES), jnp.float32) for _ in range(2)]
        for slot, pieces in enumerate(held):
            for epoch in range(epochs):
                for kind in range(2):
                    raw[epoch, kind, slot, pl.ds(blank, MAXS)] = jnp.zeros((MAXS, LANES), jnp.float32)
                    for start, (source, index, tile) in zip(at, pieces):
                        value = operands[source][index, epoch, kind, tile]
                        tops[kind] = jnp.maximum(tops[kind], value if kind else jnp.abs(value))
                        raw[epoch, kind, slot, pl.ds(start, MAXS)] = value
        tops = [jnp.full((8, LANES), jnp.maximum(jnp.max(top), 1e-30), jnp.float32) for top in tops]
        per_psi, per_phi = (most_psi - 1) / tops[0], (most_phi - 1) / tops[1]
        scale[0] = floor[0] * per_phi
        scale[1] = jnp.sqrt(per_phi) / (per_psi * 256.0)

        def quantize(index, _):
            rows = pl.ds(pl.multiple_of(index * 8, 8), 8)
            for epoch in range(epochs):
                for slot in range(len(held)):
                    psi = jnp.floor(raw[epoch, 0, slot, rows] * per_psi + 0.5).astype(jnp.int32)
                    phi = (raw[epoch, 1, slot, rows] * per_phi + 0.5).astype(jnp.int32)
                    whole[epoch, slot, rows] = psi * 256 + (phi >> 6)
                    lows[epoch, slot, rows] = phi & 63
            return 0

        lax.fori_loop(0, reach // 8, quantize, 0, unroll=8)
        for epoch in range(epochs):
            for slot in range(len(held)):
                for top in range(0, reach - 8 * (fold - 1), 8):
                    word = lows[epoch, slot, top : top + 8]
                    for part in range(1, fold):
                        word = word + (lows[epoch, slot, top + 8 * part : top + 8 * part + 8] << (8 * part))
                    packed[epoch, slot, top : top + 8] = word
        for slot in range(len(held)):
            number = place[first + slot] if slot < len(held) - 1 else (place[first + slot - 1] + 1) % total
            for spot, keep in ((slots - 2, lane >= MAXS), (slots - 1, lane < MAXS)):

                @pl.when(number == 0)
                def _():
                    for epoch in range(epochs):
                        for ref in (whole, packed):
                            for top in range(0, ref.shape[2], 8):
                                rows = slice(top, top + 8)
                                ref[epoch, spot, rows] = jnp.where(keep, ref[epoch, slot, rows], 0)

    first, begin = 0, 0
    for held in segments:
        pl.when(step == first)(functools.partial(assemble, first, held))
        begin = jnp.where(step >= first, first, begin)
        first += len(held) - 1

    number = place[step]
    left = jnp.where(number == 0, slots - 2, step - begin)
    right = jnp.where(number == total - 1, slots - 1, step - begin + 1)
    least, unit = scale[0], scale[1]

    def one_velocity(velocity, _):
        start = velocity * epochs * 2
        totals, low_total = [None] * fold, None
        for epoch in range(epochs):
            row, col = shifts[start + 2 * epoch], shifts[start + 2 * epoch + 1]
            beyond, turn = lane < col, (LANES - col) & (LANES - 1)

            def moved(ref, top):
                rows = pl.ds(row + top, 8)
                return pltpu.roll(jnp.where(beyond, ref[epoch, right, rows], ref[epoch, left, rows]), turn, 1)

            for part in range(fold):
                word = moved(whole, 8 * part)
                totals[part] = word if epoch == 0 else totals[part] + word
            word = moved(packed, 0)
            low_total = word if epoch == 0 else low_total + word
        for part in range(fold):
            psi = totals[part].astype(jnp.float32)
            phi = (((totals[part] & 255) << 6) + ((low_total >> (8 * part)) & 255)).astype(jnp.float32)
            out_ref[velocity, 8 * part : 8 * part + 8] = psi * unit * lax.rsqrt(jnp.maximum(phi, least))
        return 0

    lax.fori_loop(0, velocities, one_velocity, 0, unroll=together)


def stack_tiles(numbers, lower, shifts, floor, segments, out, out_shape):
    velocities, height, columns = out_shape.shape
    operands, described = [], []
    for held in segments:
        tiles = []
        for pieces, tile in held:
            spots = []
            for array, index in pieces:
                source = next((i for i, other in enumerate(operands) if other is array), len(operands))
                operands += [array] if source == len(operands) else []
                spots.append((source, index, tile))
            tiles.append(spots)
        described.append(tiles)
    sources, epochs = len(operands), operands[0].shape[1]
    in_specs = [pl.BlockSpec(memory_space=pltpu.VMEM)] * sources
    aliases = {}
    if out is not None:
        in_specs.append(pl.BlockSpec(memory_space=pl.ANY))
        operands.append(out)
        aliases = {3 + sources: 0}
    steps, longest, reach = len(numbers), max(len(held) for held in segments), height + 2 * MAXS
    work = steps * velocities * height * LANES
    return pl.pallas_call(
        functools.partial(
            stack_kernel,
            segments=described,
            sources=sources,
            total=columns // LANES,
            together=next(size for size in (36, 18, 12, 9, 8, 6, 4, 3, 2, 1) if velocities % size == 0),
        ),
        grid_spec=pltpu.PrefetchScalarGridSpec(
            num_scalar_prefetch=3,
            grid=(steps,),
            in_specs=in_specs,
            out_specs=pl.BlockSpec((velocities, height, LANES), lambda step, place, *_: (0, 0, place[step])),
            scratch_shapes=[
                pltpu.VMEM((epochs, 2, longest, reach, LANES), jnp.float32),
                pltpu.VMEM((epochs, longest + 2, reach, LANES), jnp.int32),
                pltpu.VMEM((epochs, longest, reach, LANES), jnp.int32),
                pltpu.VMEM((epochs, longest + 2, reach - height + 8, LANES), jnp.int32),
                pltpu.VMEM((2, 8, LANES), jnp.float32),
            ],
        ),
        out_shape=out_shape,
        input_output_aliases=aliases,
        compiler_params=pltpu.CompilerParams(vmem_limit_bytes=VMEM),
        cost_estimate=pl.CostEstimate(flops=16 * work, bytes_accessed=24 * work, transcendentals=work),
    )(jnp.stack(numbers + [lower]).astype(jnp.int32), shifts + MAXS, floor, *operands)


def local(images, variance, spread_kernel, shifts, epoch_owner, valid_rows):
    height, columns = images.shape[1:]
    blocks = lax.axis_size("vel")
    width = columns // blocks
    me, lower = lax.axis_index("vel"), lax.axis_index("rows")
    swap = [(0, 1), (1, 0)]

    order = list(range(0, blocks, 2)) + list(range(1, blocks, 2))[::-1]
    right = [(order[i], order[(i + 1) % blocks]) for i in range(blocks)]
    left = [(b, a) for a, b in right]

    def position(index):
        return jnp.where(index % 2 == 0, index // 2, blocks - 1 - index // 2)

    mine = position(me)
    place = jnp.stack([mine, lower]).astype(jnp.int32)

    numbers = jnp.concatenate([jnp.stack([me, lower]).astype(jnp.int32), epoch_owner, valid_rows.reshape(-1)])
    starts = position(me ^ jnp.arange(blocks, dtype=jnp.int32)) * width
    chunks = list(cut(starts, jnp.concatenate([images, variance]), blocks))
    for step in range(1, blocks):
        chunks[step] = lax.ppermute(chunks[step], "vel", [(i, i ^ step) for i in range(blocks)])
    chunks[1], spread_kernel, numbers = lax.optimization_barrier((chunks[1], spread_kernel, numbers))
    bands, floor = make_bands(spread_kernel)
    chunks[-1], floor = lax.optimization_barrier((chunks[-1], floor))
    own, edges = pick(numbers, epoch_owner.shape[0], chunks, height)
    payload = correlate(place, own, lax.ppermute(edges, "rows", swap), bands, spread_kernel.shape[0])

    flat_shifts, floor = shifts.reshape(-1), floor[0, :1]
    out_shape = jax.ShapeDtypeStruct((shifts.shape[0], height, columns), jnp.float32)

    tiles, half = payload.shape[3], blocks // 2

    def stack_now(segments, out):
        numbers = [
            (mine + offset) % blocks * tiles + tile for held in segments for offset, tile in held[:-1]
        ]
        held = [[(have[offset], tile) for offset, tile in segment] for segment in segments]
        return stack_tiles(numbers, lower, flat_shifts, floor, held, out, out_shape)

    def block(offset):
        return [(offset, tile) for tile in range(tiles)]

    behind, ahead = lax.ppermute(payload, "vel", right), lax.ppermute(payload, "vel", left)
    border = lax.ppermute(payload[:1], "rows", swap)
    have = {0: ((payload, 0), (payload, 1), (border, 0))}
    out = stack_now([block(0)], None)
    for step in range(1, half + 1):
        if step < half:
            if step > 1:
                behind, ahead = lax.ppermute(behind, "vel", right), lax.ppermute(ahead, "vel", left)
            behind, ahead, out = lax.optimization_barrier((behind, ahead, out))
            border = lax.ppermute(jnp.concatenate([behind[:1], ahead[:1]]), "rows", swap)
            have[-step] = ((behind, 0), (behind, 1), (border, 0))
            have[step] = ((ahead, 0), (ahead, 1), (border, 1))
            segments = [block(-step) + [(1 - step, 0)], [(step - 1, tiles - 1)] + block(step)]
        else:
            behind, border = lax.ppermute(behind, "vel", right), lax.ppermute(border[1:], "vel", left)
            behind, border, out = lax.optimization_barrier((behind, border, out))
            have[step] = ((behind, 0), (behind, 1), (border, 0))
            segments = [[(step - 1, tiles - 1)] + block(step) + [(1 - step, 0)]]
        out = stack_now(segments, out)
    return out


def solution(mesh):
    in_specs = (
        P(("fields", "vel"), "rows", None),
        P(("fields", "vel"), "rows", None),
        P(),
        P(("fields", "vel"), None, None),
        P("fields"),
        P("fields", None),
    )
    out_specs = P(("fields", "vel"), "rows", None)
    return jax.shard_map(local, mesh=mesh, in_specs=in_specs, out_specs=out_specs, check_vma=False)
```

```python
import functools
import jax
import jax.numpy as jnp
from jax import lax
from jax.experimental import pallas as pl
from jax.experimental.pallas import tpu as pltpu
from jax.sharding import PartitionSpec as P

LANES = 128
MAXS = 16
HALO = 32
VMEM = 24 << 20
LARGE = 50 << 20


FOLD = LANES // HALO


def band_row(row, ksize):
    group, place = row // FOLD, row % FOLD
    base = group * (FOLD + 1) * LANES
    count = min(FOLD, ksize - group * FOLD) if isinstance(row, int) else jnp.minimum(FOLD, ksize - group * FOLD)
    return base + place * LANES, base + count * LANES + place * HALO


def band_kernel(taps, kernel, bands_ref, floor_ref):
    ksize = kernel.shape[0]
    skip = HALO - MAXS - ksize // 2
    shape = (HALO + LANES, LANES)
    offset = lax.broadcasted_iota(jnp.int32, shape, 0) - lax.broadcasted_iota(jnp.int32, shape, 1) - skip
    total = jnp.full((8, LANES), jnp.sum(kernel[...]), jnp.float32)
    norm = kernel[...] / total[:1, :1]
    floor_ref[...] = jnp.full(floor_ref.shape, 0.5 * jnp.sum(norm * norm), jnp.float32)
    bands_ref[:, -LANES:] = jnp.zeros((2, LANES, 2 * LANES), jnp.bfloat16)

    def one(row, _):
        band = jnp.zeros(shape, jnp.float32)
        for col in range(ksize):
            band = jnp.where(offset == col, taps[row * ksize + col], band)
        band = band / total[:1]
        for kind, value in enumerate((band, band * band)):
            high = value.astype(jnp.bfloat16)
            both = jnp.concatenate([high, (value - high.astype(jnp.float32)).astype(jnp.bfloat16)], axis=1)
            main, halo = (pl.multiple_of(at, HALO) for at in band_row(row, ksize))
            bands_ref[kind, pl.ds(main, LANES)] = both[HALO:]
            bands_ref[kind, pl.ds(halo, HALO)] = both[:HALO]
        return 0

    lax.fori_loop(0, ksize, one, 0)


def make_bands(spread_kernel):
    ksize = spread_kernel.shape[0]
    return pl.pallas_call(
        band_kernel,
        in_specs=[pl.BlockSpec(memory_space=pltpu.SMEM), pl.BlockSpec(memory_space=pltpu.VMEM)],
        out_specs=[pl.BlockSpec(memory_space=pltpu.VMEM)] * 2,
        out_shape=[
            jax.ShapeDtypeStruct((2, (ksize - (-ksize // FOLD)) * LANES, 2 * LANES), jnp.bfloat16),
            jax.ShapeDtypeStruct((8, LANES), jnp.float32),
        ],
        compiler_params=pltpu.CompilerParams(vmem_limit_bytes=VMEM),
        cost_estimate=pl.CostEstimate(flops=0, bytes_accessed=20 << 20, transcendentals=0),
    )(spread_kernel.reshape(-1), spread_kernel)


def cut_kernel(starts, pair, *chunk_refs):
    _, height, columns = pair.shape
    tiles = columns // len(chunk_refs) // LANES
    lane = lax.broadcasted_iota(jnp.int32, (8, LANES), 1)
    for index, ref in enumerate(chunk_refs):
        start = starts[index]
        ahead = jnp.where(start == 0, columns, start) - LANES
        for kind in range(2):
            for tile in range(tiles):
                at = pl.multiple_of(start + tile * LANES, LANES)
                ref[kind, tile * height : (tile + 1) * height] = pair[kind, :, pl.ds(at, LANES)]
            halo = jnp.zeros((8, LANES), jnp.float32)
            for group in range(LANES // HALO):
                rows = pair[kind, 8 * group : 8 * group + 8, pl.ds(pl.multiple_of(ahead, LANES), LANES)]
                moved = pltpu.roll(rows, (group + 1) * HALO % LANES, 1)
                halo = jnp.where(lane // HALO == group, moved, halo)
            ref[kind, tiles * height :] = halo


def cut(starts, pair, blocks):
    _, height, columns = pair.shape
    rows = columns // blocks // LANES * height + height * HALO // LANES
    return pl.pallas_call(
        cut_kernel,
        in_specs=[pl.BlockSpec(memory_space=pltpu.SMEM), pl.BlockSpec(memory_space=pltpu.VMEM)],
        out_specs=[pl.BlockSpec(memory_space=pltpu.VMEM)] * blocks,
        out_shape=[jax.ShapeDtypeStruct((2, rows, LANES), jnp.float32)] * blocks,
        compiler_params=pltpu.CompilerParams(vmem_limit_bytes=VMEM),
        cost_estimate=pl.CostEstimate(flops=0, bytes_accessed=16 * height * columns, transcendentals=0),
    )(starts, pair)


def pick_kernel(numbers, *refs):
    chunks, (own, edges, chosen) = refs[:-3], refs[-3:]
    epochs, _, count, height, _ = own.shape
    tiles = count - 1
    me, lower, valid = numbers[0], numbers[1], 2 + epochs
    for epoch in range(epochs):
        for step, chunk in enumerate(chunks):

            @pl.when(numbers[2 + epoch] ^ me == step)
            def _():
                chosen[epoch] = chunk[...]

    row_ids = lower * height + lax.broadcasted_iota(jnp.int32, (height, LANES), 0)
    behind = lax.broadcasted_iota(jnp.int32, (8, LANES), 1) >= LANES - HALO
    for epoch in range(epochs):
        first, last = numbers[valid + 2 * epoch], numbers[valid + 2 * epoch + 1]
        usable = jnp.logical_and(row_ids >= first, row_ids < last)
        for tile in range(count):
            if tile:
                value, noise = (chosen[epoch, kind, (tile - 1) * height : tile * height] for kind in range(2))
            else:
                packed = [chosen[epoch, kind, tiles * height :] for kind in range(2)]
                spread = [
                    jnp.concatenate(
                        [
                            jnp.where(behind, pltpu.roll(rows, (LANES - (group + 1) * HALO) % LANES, 1), fill)
                            for group in range(LANES // HALO)
                        ],
                        axis=0,
                    )
                    for rows, fill in zip(packed, (0.0, 1.0))
                ]
                value, noise = spread
            own[epoch, 0, tile] = jnp.where(usable, value / noise, 0.0)
            own[epoch, 1, tile] = jnp.where(usable, 1.0 / noise, 0.0)
    edges[...] = own[:, :, :, pl.ds(pl.multiple_of((1 - lower) * (height - MAXS), MAXS), MAXS)]


def pick(numbers, epochs, chunks, height):
    rows = chunks[0].shape[1]
    tiles = (rows - height * HALO // LANES) // height
    return pl.pallas_call(
        pick_kernel,
        in_specs=[pl.BlockSpec(memory_space=pltpu.SMEM)] + [pl.BlockSpec(memory_space=pltpu.VMEM)] * len(chunks),
        out_specs=[pl.BlockSpec(memory_space=pltpu.VMEM)] * 2,
        out_shape=[
            jax.ShapeDtypeStruct((epochs, 2, tiles + 1, depth, LANES), jnp.float32) for depth in (height, MAXS)
        ],
        scratch_shapes=[pltpu.VMEM((epochs, 2, rows, LANES), jnp.float32)],
        compiler_params=pltpu.CompilerParams(vmem_limit_bytes=VMEM),
        cost_estimate=pl.CostEstimate(flops=0, bytes_accessed=4 << 20, transcendentals=0),
    )(numbers, *chunks)


def correlate_kernel(place, own, border, bands_hbm, rows_ref, ext, high, low, summed, bands_ref, arrived, *, ksize):
    epochs, kinds, count, height, _ = own.shape
    tiles = count - 1
    members = high.shape[2] // (height + 2 * MAXS)
    copies = [pltpu.make_async_copy(bands_hbm.at[kind], bands_ref.at[kind], arrived.at[kind]) for kind in range(kinds)]
    for copy in copies:
        copy.start()
    first, lower = place[0] == 0, place[1]
    at_border = (1 - lower) * (MAXS + height)
    summed_rows = height * members
    blank = pl.ds(pl.multiple_of(lower * (MAXS + height) * members, 8), MAXS * members)
    ext[:, :, blank] = jnp.zeros((kinds, 2, MAXS * members, LANES), jnp.float32)
    nothing = jnp.zeros((height, LANES), jnp.float32)
    keep = jnp.where(first, 0.0, 1.0)

    def put(kind, half, member, value, beyond):
        ext[kind, half, pl.ds(MAXS * members + member, height, stride=members)] = value
        ext[kind, half, pl.ds(at_border * members + member, MAXS, stride=members)] = beyond

    for epoch in range(epochs):
        base = epoch * (tiles + 1)
        for kind in range(kinds):
            for tile in range(1, count):
                put(kind, 1, base + tile - 1, own[epoch, kind, tile], border[epoch, kind, tile])
                if tile < tiles:
                    put(kind, 0, base + tile, own[epoch, kind, tile], border[epoch, kind, tile])
            put(kind, 0, base, own[epoch, kind, 0] * keep, border[epoch, kind, 0] * keep)
            put(kind, 0, base + tiles, own[epoch, kind, 0], border[epoch, kind, 0])
            put(kind, 1, base + tiles, nothing, nothing[:MAXS])

    lanes = lax.broadcasted_iota(jnp.int32, (128, LANES), 1)

    def split(index, _):
        rows = pl.ds(pl.multiple_of(index * 128, 128), 128)
        for kind in range(kinds):
            halo = jnp.zeros((128, LANES), jnp.float32)
            for fold in range(FOLD):
                ahead = ext[kind, 0, pl.ds(pl.multiple_of(index * 128 + fold * members, 16), 128)]
                halo = jnp.where(lanes // HALO == fold, pltpu.roll(ahead, (fold + 1) * HALO % LANES, 1), halo)
            for half, value in enumerate((halo, ext[kind, 1, rows])):
                part = value.astype(jnp.bfloat16)
                high[kind, half, rows] = part
                low[kind, half, rows] = (value - part.astype(jnp.float32)).astype(jnp.bfloat16)
        return 0

    lax.fori_loop(0, high.shape[2] // 128, split, 0, unroll=4)

    lane = lax.broadcasted_iota(jnp.int32, (MAXS, LANES), 1)
    wrapped = jnp.logical_and(first, lane < MAXS)
    for kind in range(kinds):
        offsets = [pl.ds((row + MAXS - ksize // 2) * members, summed_rows) for row in range(ksize)]
        parts = []
        for base in range(0, ksize, FOLD):
            parts += [(1, rows) for rows in offsets[base : base + FOLD]] + [(0, offsets[base])]
        upper = jnp.concatenate([high[kind, half, rows] for half, rows in parts], axis=1)
        rest = jnp.concatenate([low[kind, half, rows] for half, rows in parts], axis=1)
        copies[kind].wait()
        weights = bands_ref[kind]
        pair = jnp.dot(upper, weights, preferred_element_type=jnp.float32)
        more = jnp.dot(rest, weights[:, :LANES], preferred_element_type=jnp.float32)
        summed[:summed_rows] = pair[:, :LANES] + (pair[:, LANES:] + more)
        for half in range(2):
            start = (1 - lower if half == 0 else lower) * (height - MAXS)
            for epoch in range(epochs):
                base = epoch * (tiles + 1)

                def rows_of(tile):
                    return summed[pl.ds(start * members + base + tile, MAXS, stride=members)]

                rows_ref[half, epoch, kind, 0] = jnp.where(wrapped, rows_of(tiles), rows_of(0))
                for tile in range(1, tiles):
                    rows_ref[half, epoch, kind, tile] = rows_of(tile)


def correlate(place, own, border, bands, ksize):
    epochs, kinds, count, height, _ = own.shape
    tiles = count - 1
    members = -(-epochs * (tiles + 1) // 16) * 16
    depth = (height + 2 * MAXS) * members
    flops = 2 * 2 * kinds * members * height * bands.shape[1] * 2 * LANES
    return pl.pallas_call(
        functools.partial(correlate_kernel, ksize=ksize),
        in_specs=[pl.BlockSpec(memory_space=pltpu.SMEM)] + [pl.BlockSpec(memory_space=pltpu.VMEM)] * 2
        + [pl.BlockSpec(memory_space=pltpu.HBM)],
        out_specs=pl.BlockSpec(memory_space=pltpu.VMEM),
        out_shape=jax.ShapeDtypeStruct((2, epochs, kinds, tiles, MAXS, LANES), jnp.float32),
        scratch_shapes=[
            pltpu.VMEM((kinds, 2, depth + (FOLD - 1) * members, LANES), jnp.float32),
            pltpu.VMEM((kinds, 2, depth, LANES), jnp.bfloat16),
            pltpu.VMEM((kinds, 2, depth, LANES), jnp.bfloat16),
            pltpu.VMEM(((height + 1) * members, LANES), jnp.float32),
            pltpu.VMEM(bands.shape, bands.dtype),
            pltpu.SemaphoreType.DMA((kinds,)),
        ],
        compiler_params=pltpu.CompilerParams(vmem_limit_bytes=LARGE),
        cost_estimate=pl.CostEstimate(flops=flops, bytes_accessed=12 << 20, transcendentals=0),
    )(place, own, border, bands)


def stack_kernel(place, shifts, floor, *refs, segments, sources, total, together):
    operands, out_ref = refs[:sources], refs[-6]
    raw, whole, lows, packed, scale = refs[-5:]
    step = pl.program_id(0)
    epochs, slots, reach = whole.shape[:3]
    velocities, height = out_ref.shape[:2]
    fold = height // 8
    steps = sum(len(held) - 1 for held in segments)
    lower = place[steps]
    at = [pl.multiple_of(row, MAXS) for row in (32 - 16 * lower, 16 + 16 * lower, 48 - 48 * lower)]
    blank = pl.multiple_of(48 * lower, MAXS)
    most_psi = ((1 << 23) - 1) // epochs
    most_phi = 255 // epochs * 64 + 63
    lane = lax.broadcasted_iota(jnp.int32, (8, LANES), 1)

    def assemble(first, held):
        tops = [jnp.zeros((MAXS, LANES), jnp.float32) for _ in range(2)]
        for slot, pieces in enumerate(held):
            for epoch in range(epochs):
                for kind in range(2):
                    raw[epoch, kind, slot, pl.ds(blank, MAXS)] = jnp.zeros((MAXS, LANES), jnp.float32)
                    for start, (source, index, tile) in zip(at, pieces):
                        value = operands[source][index, epoch, kind, tile]
                        tops[kind] = jnp.maximum(tops[kind], value if kind else jnp.abs(value))
                        raw[epoch, kind, slot, pl.ds(start, MAXS)] = value
        tops = [jnp.full((8, LANES), jnp.maximum(jnp.max(top), 1e-30), jnp.float32) for top in tops]
        per_psi, per_phi = (most_psi - 1) / tops[0], (most_phi - 1) / tops[1]
        scale[0] = floor[0] * per_phi
        scale[1] = jnp.sqrt(per_phi) / per_psi / 256.0

        def quantize(index, _):
            rows = pl.ds(pl.multiple_of(index * 8, 8), 8)
            for epoch in range(epochs):
                for slot in range(len(held)):
                    psi = jnp.floor(raw[epoch, 0, slot, rows] * per_psi + 0.5).astype(jnp.int32)
                    phi = (raw[epoch, 1, slot, rows] * per_phi + 0.5).astype(jnp.int32)
                    whole[epoch, slot, rows] = psi * 256 + (phi >> 6)
                    lows[epoch, slot, rows] = phi & 63
            return 0

        lax.fori_loop(0, reach // 8, quantize, 0, unroll=8)
        for epoch in range(epochs):
            for slot in range(len(held)):
                for top in range(0, reach - 8 * (fold - 1), 8):
                    word = lows[epoch, slot, top : top + 8]
                    for part in range(1, fold):
                        word = word + (lows[epoch, slot, top + 8 * part : top + 8 * part + 8] << (8 * part))
                    packed[epoch, slot, top : top + 8] = word
        for slot in range(len(held)):
            number = place[first + slot] if slot < len(held) - 1 else (place[first + slot - 1] + 1) % total
            for spot, keep in ((slots - 2, lane >= MAXS), (slots - 1, lane < MAXS)):

                @pl.when(number == 0)
                def _():
                    for epoch in range(epochs):
                        for ref in (whole, packed):
                            for top in range(0, ref.shape[2], 8):
                                rows = slice(top, top + 8)
                                ref[epoch, spot, rows] = jnp.where(keep, ref[epoch, slot, rows], 0)

    first, begin = 0, 0
    for held in segments:
        pl.when(step == first)(functools.partial(assemble, first, held))
        begin = jnp.where(step >= first, first, begin)
        first += len(held) - 1

    number = place[step]
    left = jnp.where(number == 0, slots - 2, step - begin)
    right = jnp.where(number == total - 1, slots - 1, step - begin + 1)
    least, unit = scale[0], scale[1]

    def one_velocity(velocity, _):
        start = velocity * epochs * 2
        totals, low_total = [None] * fold, None
        for epoch in range(epochs):
            row, col = shifts[start + 2 * epoch], shifts[start + 2 * epoch + 1]
            beyond, turn = lane < col, (LANES - col) & (LANES - 1)

            def moved(ref, top):
                rows = pl.ds(row + top, 8)
                return pltpu.roll(jnp.where(beyond, ref[epoch, right, rows], ref[epoch, left, rows]), turn, 1)

            for part in range(fold):
                word = moved(whole, 8 * part)
                totals[part] = word if epoch == 0 else totals[part] + word
            word = moved(packed, 0)
            low_total = word if epoch == 0 else low_total + word
        for part in range(fold):
            psi = totals[part].astype(jnp.float32)
            phi = (((totals[part] & 255) << 6) + ((low_total >> (8 * part)) & 255)).astype(jnp.float32)
            out_ref[velocity, 8 * part : 8 * part + 8] = psi * unit * lax.rsqrt(jnp.maximum(phi, least))
        return 0

    lax.fori_loop(0, velocities, one_velocity, 0, unroll=together)


def stack_tiles(numbers, lower, shifts, floor, segments, out, out_shape):
    velocities, height, columns = out_shape.shape
    operands, described = [], []
    for held in segments:
        tiles = []
        for pieces, tile in held:
            spots = []
            for array, index in pieces:
                source = next((i for i, other in enumerate(operands) if other is array), len(operands))
                operands += [array] if source == len(operands) else []
                spots.append((source, index, tile))
            tiles.append(spots)
        described.append(tiles)
    sources, epochs = len(operands), operands[0].shape[1]
    in_specs = [pl.BlockSpec(memory_space=pltpu.VMEM)] * sources
    aliases = {}
    if out is not None:
        in_specs.append(pl.BlockSpec(memory_space=pl.ANY))
        operands.append(out)
        aliases = {3 + sources: 0}
    steps, longest, reach = len(numbers), max(len(held) for held in segments), height + 2 * MAXS
    work = steps * velocities * height * LANES
    return pl.pallas_call(
        functools.partial(
            stack_kernel,
            segments=described,
            sources=sources,
            total=columns // LANES,
            together=next(size for size in (36, 18, 12, 9, 8, 6, 4, 3, 2, 1) if velocities % size == 0),
        ),
        grid_spec=pltpu.PrefetchScalarGridSpec(
            num_scalar_prefetch=3,
            grid=(steps,),
            in_specs=in_specs,
            out_specs=pl.BlockSpec((velocities, height, LANES), lambda step, place, *_: (0, 0, place[step])),
            scratch_shapes=[
                pltpu.VMEM((epochs, 2, longest, reach, LANES), jnp.float32),
                pltpu.VMEM((epochs, longest + 2, reach, LANES), jnp.int32),
                pltpu.VMEM((epochs, longest, reach, LANES), jnp.int32),
                pltpu.VMEM((epochs, longest + 2, reach - height + 8, LANES), jnp.int32),
                pltpu.VMEM((2, 8, LANES), jnp.float32),
            ],
        ),
        out_shape=out_shape,
        input_output_aliases=aliases,
        compiler_params=pltpu.CompilerParams(vmem_limit_bytes=VMEM),
        cost_estimate=pl.CostEstimate(flops=16 * work, bytes_accessed=24 * work, transcendentals=work),
    )(jnp.stack(numbers + [lower]).astype(jnp.int32), shifts + MAXS, floor, *operands)


def local(images, variance, spread_kernel, shifts, epoch_owner, valid_rows):
    height, columns = images.shape[1:]
    blocks = lax.axis_size("vel")
    width = columns // blocks
    me, lower = lax.axis_index("vel"), lax.axis_index("rows")
    swap = [(0, 1), (1, 0)]

    order = list(range(0, blocks, 2)) + list(range(1, blocks, 2))[::-1]
    right = [(order[i], order[(i + 1) % blocks]) for i in range(blocks)]
    left = [(b, a) for a, b in right]

    def position(index):
        return jnp.where(index % 2 == 0, index // 2, blocks - 1 - index // 2)

    mine = position(me)
    place = jnp.stack([mine, lower]).astype(jnp.int32)

    numbers = jnp.concatenate([jnp.stack([me, lower]).astype(jnp.int32), epoch_owner, valid_rows.reshape(-1)])
    starts = position(me ^ jnp.arange(blocks, dtype=jnp.int32)) * width
    chunks = list(cut(starts, jnp.concatenate([images, variance]), blocks))
    for step in range(1, blocks):
        chunks[step] = lax.ppermute(chunks[step], "vel", [(i, i ^ step) for i in range(blocks)])
    chunks[1], spread_kernel, numbers = lax.optimization_barrier((chunks[1], spread_kernel, numbers))
    bands, floor = make_bands(spread_kernel)
    chunks[-1], floor = lax.optimization_barrier((chunks[-1], floor))
    own, edges = pick(numbers, epoch_owner.shape[0], chunks, height)
    payload = correlate(place, own, lax.ppermute(edges, "rows", swap), bands, spread_kernel.shape[0])

    flat_shifts, floor = shifts.reshape(-1), floor[0, :1]
    out_shape = jax.ShapeDtypeStruct((shifts.shape[0], height, columns), jnp.float32)

    tiles, half = payload.shape[3], blocks // 2

    def stack_now(segments, out):
        numbers = [
            (mine + offset) % blocks * tiles + tile for held in segments for offset, tile in held[:-1]
        ]
        held = [[(have[offset], tile) for offset, tile in segment] for segment in segments]
        return stack_tiles(numbers, lower, flat_shifts, floor, held, out, out_shape)

    def block(offset):
        return [(offset, tile) for tile in range(tiles)]

    behind, ahead = lax.ppermute(payload, "vel", right), lax.ppermute(payload, "vel", left)
    border = lax.ppermute(payload[:1], "rows", swap)
    have = {0: ((payload, 0), (payload, 1), (border, 0))}
    out = stack_now([block(0)], None)
    for step in range(1, half + 1):
        if step < half:
            if step > 1:
                behind, ahead = lax.ppermute(behind, "vel", right), lax.ppermute(ahead, "vel", left)
            behind, ahead, out = lax.optimization_barrier((behind, ahead, out))
            border = lax.ppermute(jnp.concatenate([behind[:1], ahead[:1]]), "rows", swap)
            have[-step] = ((behind, 0), (behind, 1), (border, 0))
            have[step] = ((ahead, 0), (ahead, 1), (border, 1))
            segments = [block(-step) + [(1 - step, 0)], [(step - 1, tiles - 1)] + block(step)]
        else:
            behind, border = lax.ppermute(behind, "vel", right), lax.ppermute(border[1:], "vel", left)
            behind, border, out = lax.optimization_barrier((behind, border, out))
            have[step] = ((behind, 0), (behind, 1), (border, 0))
            segments = [[(step - 1, tiles - 1)] + block(step) + [(1 - step, 0)]]
        out = stack_now(segments, out)
    return out


def solution(mesh):
    in_specs = (
        P(("fields", "vel"), "rows", None),
        P(("fields", "vel"), "rows", None),
        P(),
        P(("fields", "vel"), None, None),
        P("fields"),
        P("fields", None),
    )
    out_specs = P(("fields", "vel"), "rows", None)
    return jax.shard_map(local, mesh=mesh, in_specs=in_specs, out_specs=out_specs, check_vma=False)
```

```python
import functools
import jax
import jax.numpy as jnp
from jax import lax
from jax.experimental import pallas as pl
from jax.experimental.pallas import tpu as pltpu
from jax.sharding import PartitionSpec as P

LANES = 128
MAXS = 16
HALO = 32
VMEM = 24 << 20
LARGE = 50 << 20


FOLD = LANES // HALO


def band_row(row, ksize):
    group, place = row // FOLD, row % FOLD
    base = group * (FOLD + 1) * LANES
    count = min(FOLD, ksize - group * FOLD) if isinstance(row, int) else jnp.minimum(FOLD, ksize - group * FOLD)
    return base + place * LANES, base + count * LANES + place * HALO


def band_kernel(taps, kernel, bands_ref, floor_ref):
    ksize = kernel.shape[0]
    skip = HALO - MAXS - ksize // 2
    shape = (HALO + LANES, LANES)
    offset = lax.broadcasted_iota(jnp.int32, shape, 0) - lax.broadcasted_iota(jnp.int32, shape, 1) - skip
    total = jnp.full((8, LANES), jnp.sum(kernel[...]), jnp.float32)
    norm = kernel[...] / total[:1, :1]
    floor_ref[...] = jnp.full(floor_ref.shape, 0.5 * jnp.sum(norm * norm), jnp.float32)
    bands_ref[:, -LANES:] = jnp.zeros((2, LANES, 2 * LANES), jnp.bfloat16)

    def one(row, _):
        band = jnp.zeros(shape, jnp.float32)
        for col in range(ksize):
            band = jnp.where(offset == col, taps[row * ksize + col], band)
        band = band / total[:1]
        for kind, value in enumerate((band, band * band)):
            high = value.astype(jnp.bfloat16)
            both = jnp.concatenate([high, (value - high.astype(jnp.float32)).astype(jnp.bfloat16)], axis=1)
            main, halo = (pl.multiple_of(at, HALO) for at in band_row(row, ksize))
            bands_ref[kind, pl.ds(main, LANES)] = both[HALO:]
            bands_ref[kind, pl.ds(halo, HALO)] = both[:HALO]
        return 0

    lax.fori_loop(0, ksize, one, 0)


def make_bands(spread_kernel):
    ksize = spread_kernel.shape[0]
    return pl.pallas_call(
        band_kernel,
        in_specs=[pl.BlockSpec(memory_space=pltpu.SMEM), pl.BlockSpec(memory_space=pltpu.VMEM)],
        out_specs=[pl.BlockSpec(memory_space=pltpu.VMEM)] * 2,
        out_shape=[
            jax.ShapeDtypeStruct((2, (ksize - (-ksize // FOLD)) * LANES, 2 * LANES), jnp.bfloat16),
            jax.ShapeDtypeStruct((8, LANES), jnp.float32),
        ],
        compiler_params=pltpu.CompilerParams(vmem_limit_bytes=VMEM),
        cost_estimate=pl.CostEstimate(flops=0, bytes_accessed=20 << 20, transcendentals=0),
    )(spread_kernel.reshape(-1), spread_kernel)


def cut_kernel(starts, pair, *chunk_refs):
    _, height, columns = pair.shape
    tiles = columns // len(chunk_refs) // LANES
    lane = lax.broadcasted_iota(jnp.int32, (8, LANES), 1)
    for index, ref in enumerate(chunk_refs):
        start = starts[index]
        ahead = jnp.where(start == 0, columns, start) - LANES
        for kind in range(2):
            for tile in range(tiles):
                at = pl.multiple_of(start + tile * LANES, LANES)
                ref[kind, tile * height : (tile + 1) * height] = pair[kind, :, pl.ds(at, LANES)]
            halo = jnp.zeros((8, LANES), jnp.float32)
            for group in range(LANES // HALO):
                rows = pair[kind, 8 * group : 8 * group + 8, pl.ds(pl.multiple_of(ahead, LANES), LANES)]
                moved = pltpu.roll(rows, (group + 1) * HALO % LANES, 1)
                halo = jnp.where(lane // HALO == group, moved, halo)
            ref[kind, tiles * height :] = halo


def cut(starts, pair, blocks):
    _, height, columns = pair.shape
    rows = columns // blocks // LANES * height + height * HALO // LANES
    return pl.pallas_call(
        cut_kernel,
        in_specs=[pl.BlockSpec(memory_space=pltpu.SMEM), pl.BlockSpec(memory_space=pltpu.VMEM)],
        out_specs=[pl.BlockSpec(memory_space=pltpu.VMEM)] * blocks,
        out_shape=[jax.ShapeDtypeStruct((2, rows, LANES), jnp.float32)] * blocks,
        compiler_params=pltpu.CompilerParams(vmem_limit_bytes=VMEM),
        cost_estimate=pl.CostEstimate(flops=0, bytes_accessed=16 * height * columns, transcendentals=0),
    )(starts, pair)


def pick_kernel(numbers, *refs):
    chunks, (own, edges, chosen) = refs[:-3], refs[-3:]
    epochs, _, count, height, _ = own.shape
    tiles = count - 1
    me, lower, valid = numbers[0], numbers[1], 2 + epochs
    for epoch in range(epochs):
        for step, chunk in enumerate(chunks):

            @pl.when(numbers[2 + epoch] ^ me == step)
            def _():
                chosen[epoch] = chunk[...]

    row_ids = lower * height + lax.broadcasted_iota(jnp.int32, (height, LANES), 0)
    behind = lax.broadcasted_iota(jnp.int32, (8, LANES), 1) >= LANES - HALO
    for epoch in range(epochs):
        first, last = numbers[valid + 2 * epoch], numbers[valid + 2 * epoch + 1]
        usable = jnp.logical_and(row_ids >= first, row_ids < last)
        for tile in range(count):
            if tile:
                value, noise = (chosen[epoch, kind, (tile - 1) * height : tile * height] for kind in range(2))
            else:
                packed = [chosen[epoch, kind, tiles * height :] for kind in range(2)]
                spread = [
                    jnp.concatenate(
                        [
                            jnp.where(behind, pltpu.roll(rows, (LANES - (group + 1) * HALO) % LANES, 1), fill)
                            for group in range(LANES // HALO)
                        ],
                        axis=0,
                    )
                    for rows, fill in zip(packed, (0.0, 1.0))
                ]
                value, noise = spread
            own[epoch, 0, tile] = jnp.where(usable, value / noise, 0.0)
            own[epoch, 1, tile] = jnp.where(usable, 1.0 / noise, 0.0)
    edges[...] = own[:, :, :, pl.ds(pl.multiple_of((1 - lower) * (height - MAXS), MAXS), MAXS)]


def pick(numbers, epochs, chunks, height):
    rows = chunks[0].shape[1]
    tiles = (rows - height * HALO // LANES) // height
    return pl.pallas_call(
        pick_kernel,
        in_specs=[pl.BlockSpec(memory_space=pltpu.SMEM)] + [pl.BlockSpec(memory_space=pltpu.VMEM)] * len(chunks),
        out_specs=[pl.BlockSpec(memory_space=pltpu.VMEM)] * 2,
        out_shape=[
            jax.ShapeDtypeStruct((epochs, 2, tiles + 1, depth, LANES), jnp.float32) for depth in (height, MAXS)
        ],
        scratch_shapes=[pltpu.VMEM((epochs, 2, rows, LANES), jnp.float32)],
        compiler_params=pltpu.CompilerParams(vmem_limit_bytes=VMEM),
        cost_estimate=pl.CostEstimate(flops=0, bytes_accessed=4 << 20, transcendentals=0),
    )(numbers, *chunks)


def correlate_kernel(place, own, border, bands_hbm, rows_ref, ext, high, low, summed, bands_ref, arrived, *, ksize):
    epochs, kinds, count, height, _ = own.shape
    tiles = count - 1
    members = high.shape[2] // (height + 2 * MAXS)
    copies = [pltpu.make_async_copy(bands_hbm.at[kind], bands_ref.at[kind], arrived.at[kind]) for kind in range(kinds)]
    for copy in copies:
        copy.start()
    first, lower = place[0] == 0, place[1]
    at_border = (1 - lower) * (MAXS + height)
    summed_rows = height * members
    blank = pl.ds(pl.multiple_of(lower * (MAXS + height) * members, 8), MAXS * members)
    ext[:, :, blank] = jnp.zeros((kinds, 2, MAXS * members, LANES), jnp.float32)
    nothing = jnp.zeros((height, LANES), jnp.float32)
    keep = jnp.where(first, 0.0, 1.0)

    def put(kind, half, member, value, beyond):
        ext[kind, half, pl.ds(MAXS * members + member, height, stride=members)] = value
        ext[kind, half, pl.ds(at_border * members + member, MAXS, stride=members)] = beyond

    for epoch in range(epochs):
        base = epoch * (tiles + 1)
        for kind in range(kinds):
            for tile in range(1, count):
                put(kind, 1, base + tile - 1, own[epoch, kind, tile], border[epoch, kind, tile])
                if tile < tiles:
                    put(kind, 0, base + tile, own[epoch, kind, tile], border[epoch, kind, tile])
            put(kind, 0, base, own[epoch, kind, 0] * keep, border[epoch, kind, 0] * keep)
            put(kind, 0, base + tiles, own[epoch, kind, 0], border[epoch, kind, 0])
            put(kind, 1, base + tiles, nothing, nothing[:MAXS])

    lanes = lax.broadcasted_iota(jnp.int32, (128, LANES), 1)

    def split(index, _):
        rows = pl.ds(pl.multiple_of(index * 128, 128), 128)
        for kind in range(kinds):
            halo = jnp.zeros((128, LANES), jnp.float32)
            for fold in range(FOLD):
                ahead = ext[kind, 0, pl.ds(pl.multiple_of(index * 128 + fold * members, 16), 128)]
                halo = jnp.where(lanes // HALO == fold, pltpu.roll(ahead, (fold + 1) * HALO % LANES, 1), halo)
            for half, value in enumerate((halo, ext[kind, 1, rows])):
                part = value.astype(jnp.bfloat16)
                high[kind, half, rows] = part
                low[kind, half, rows] = (value - part.astype(jnp.float32)).astype(jnp.bfloat16)
        return 0

    lax.fori_loop(0, high.shape[2] // 128, split, 0, unroll=4)

    lane = lax.broadcasted_iota(jnp.int32, (MAXS, LANES), 1)
    wrapped = jnp.logical_and(first, lane < MAXS)
    for kind in range(kinds):
        offsets = [pl.ds((row + MAXS - ksize // 2) * members, summed_rows) for row in range(ksize)]
        parts = []
        for base in range(0, ksize, FOLD):
            parts += [(1, rows) for rows in offsets[base : base + FOLD]] + [(0, offsets[base])]
        upper = jnp.concatenate([high[kind, half, rows] for half, rows in parts], axis=1)
        rest = jnp.concatenate([low[kind, half, rows] for half, rows in parts], axis=1)
        copies[kind].wait()
        weights = bands_ref[kind]
        pair = jnp.dot(upper, weights, preferred_element_type=jnp.float32)
        more = jnp.dot(rest, weights[:, :LANES], preferred_element_type=jnp.float32)
        summed[:summed_rows] = pair[:, :LANES] + (pair[:, LANES:] + more)
        for half in range(2):
            start = (1 - lower if half == 0 else lower) * (height - MAXS)
            for epoch in range(epochs):
                base = epoch * (tiles + 1)

                def rows_of(tile):
                    return summed[pl.ds(start * members + base + tile, MAXS, stride=members)]

                rows_ref[half, epoch, kind, 0] = jnp.where(wrapped, rows_of(tiles), rows_of(0))
                for tile in range(1, tiles):
                    rows_ref[half, epoch, kind, tile] = rows_of(tile)


def correlate(place, own, border, bands, ksize):
    epochs, kinds, count, height, _ = own.shape
    tiles = count - 1
    members = -(-epochs * (tiles + 1) // 16) * 16
    depth = (height + 2 * MAXS) * members
    flops = 2 * 2 * kinds * members * height * bands.shape[1] * 2 * LANES
    return pl.pallas_call(
        functools.partial(correlate_kernel, ksize=ksize),
        in_specs=[pl.BlockSpec(memory_space=pltpu.SMEM)] + [pl.BlockSpec(memory_space=pltpu.VMEM)] * 2
        + [pl.BlockSpec(memory_space=pltpu.HBM)],
        out_specs=pl.BlockSpec(memory_space=pltpu.VMEM),
        out_shape=jax.ShapeDtypeStruct((2, epochs, kinds, tiles, MAXS, LANES), jnp.float32),
        scratch_shapes=[
            pltpu.VMEM((kinds, 2, depth + (FOLD - 1) * members, LANES), jnp.float32),
            pltpu.VMEM((kinds, 2, depth, LANES), jnp.bfloat16),
            pltpu.VMEM((kinds, 2, depth, LANES), jnp.bfloat16),
            pltpu.VMEM(((height + 1) * members, LANES), jnp.float32),
            pltpu.VMEM(bands.shape, bands.dtype),
            pltpu.SemaphoreType.DMA((kinds,)),
        ],
        compiler_params=pltpu.CompilerParams(vmem_limit_bytes=LARGE),
        cost_estimate=pl.CostEstimate(flops=flops, bytes_accessed=12 << 20, transcendentals=0),
    )(place, own, border, bands)


def stack_kernel(place, shifts, floor, *refs, segments, sources, total, together):
    operands, out_ref = refs[:sources], refs[-6]
    raw, whole, lows, packed, scale = refs[-5:]
    step = pl.program_id(0)
    epochs, slots, reach = whole.shape[:3]
    velocities, height = out_ref.shape[:2]
    fold = height // 8
    steps = sum(len(held) - 1 for held in segments)
    lower = place[steps]
    at = [pl.multiple_of(row, MAXS) for row in (32 - 16 * lower, 16 + 16 * lower, 48 - 48 * lower)]
    blank = pl.multiple_of(48 * lower, MAXS)
    most_psi = ((1 << 23) - 1) // epochs
    most_phi = 255 // epochs * 64 + 63
    lane = lax.broadcasted_iota(jnp.int32, (8, LANES), 1)

    def assemble(first, held):
        tops = [jnp.zeros((MAXS, LANES), jnp.float32) for _ in range(2)]
        for slot, pieces in enumerate(held):
            for epoch in range(epochs):
                for kind in range(2):
                    raw[epoch, kind, slot, pl.ds(blank, MAXS)] = jnp.zeros((MAXS, LANES), jnp.float32)
                    for start, (source, index, tile) in zip(at, pieces):
                        value = operands[source][index, epoch, kind, tile]
                        tops[kind] = jnp.maximum(tops[kind], value if kind else jnp.abs(value))
                        raw[epoch, kind, slot, pl.ds(start, MAXS)] = value
        tops = [jnp.full((8, LANES), jnp.maximum(jnp.max(top), 1e-30), jnp.float32) for top in tops]
        per_psi, per_phi = (most_psi - 1) / tops[0], (most_phi - 1) / tops[1]
        scale[0] = floor[0] * per_phi
        scale[1] = jnp.sqrt(per_phi) / per_psi / 256.0

        def quantize(index, _):
            rows = pl.ds(pl.multiple_of(index * 8, 8), 8)
            for epoch in range(epochs):
                for slot in range(len(held)):
                    psi = jnp.floor(raw[epoch, 0, slot, rows] * per_psi + 0.5).astype(jnp.int32)
                    phi = (raw[epoch, 1, slot, rows] * per_phi + 0.5).astype(jnp.int32)
                    whole[epoch, slot, rows] = psi * 256 + (phi >> 6)
                    lows[epoch, slot, rows] = phi & 63
            return 0

        lax.fori_loop(0, reach // 8, quantize, 0, unroll=8)
        for epoch in range(epochs):
            for slot in range(len(held)):
                for top in range(0, reach - 8 * (fold - 1), 8):
                    word = lows[epoch, slot, top : top + 8]
                    for part in range(1, fold):
                        word = word + (lows[epoch, slot, top + 8 * part : top + 8 * part + 8] << (8 * part))
                    packed[epoch, slot, top : top + 8] = word
        for slot in range(len(held)):
            number = place[first + slot] if slot < len(held) - 1 else (place[first + slot - 1] + 1) % total
            for spot, keep in ((slots - 2, lane >= MAXS), (slots - 1, lane < MAXS)):

                @pl.when(number == 0)
                def _():
                    for epoch in range(epochs):
                        for ref in (whole, packed):
                            for top in range(0, ref.shape[2], 8):
                                rows = slice(top, top + 8)
                                ref[epoch, spot, rows] = jnp.where(keep, ref[epoch, slot, rows], 0)

    first, begin = 0, 0
    for held in segments:
        pl.when(step == first)(functools.partial(assemble, first, held))
        begin = jnp.where(step >= first, first, begin)
        first += len(held) - 1

    number = place[step]
    left = jnp.where(number == 0, slots - 2, step - begin)
    right = jnp.where(number == total - 1, slots - 1, step - begin + 1)
    least, unit = scale[0], scale[1]

    def one_velocity(velocity, _):
        start = velocity * epochs * 2
        totals, low_total = [None] * fold, None
        for epoch in range(epochs):
            row, col = shifts[start + 2 * epoch], shifts[start + 2 * epoch + 1]
            beyond, turn = lane < col, (LANES - col) & (LANES - 1)

            def moved(ref, top):
                rows = pl.ds(row + top, 8)
                return pltpu.roll(jnp.where(beyond, ref[epoch, right, rows], ref[epoch, left, rows]), turn, 1)

            for part in range(fold):
                word = moved(whole, 8 * part)
                totals[part] = word if epoch == 0 else totals[part] + word
            word = moved(packed, 0)
            low_total = word if epoch == 0 else low_total + word
        for part in range(fold):
            psi = totals[part].astype(jnp.float32)
            phi = (((totals[part] & 255) << 6) + ((low_total >> (8 * part)) & 255)).astype(jnp.float32)
            out_ref[velocity, 8 * part : 8 * part + 8] = psi * unit * lax.rsqrt(jnp.maximum(phi, least))
        return 0

    lax.fori_loop(0, velocities, one_velocity, 0, unroll=together)


def stack_tiles(numbers, lower, shifts, floor, segments, out, out_shape):
    velocities, height, columns = out_shape.shape
    operands, described = [], []
    for held in segments:
        tiles = []
        for pieces, tile in held:
            spots = []
            for array, index in pieces:
                source = next((i for i, other in enumerate(operands) if other is array), len(operands))
                operands += [array] if source == len(operands) else []
                spots.append((source, index, tile))
            tiles.append(spots)
        described.append(tiles)
    sources, epochs = len(operands), operands[0].shape[1]
    in_specs = [pl.BlockSpec(memory_space=pltpu.VMEM)] * sources
    aliases = {}
    if out is not None:
        in_specs.append(pl.BlockSpec(memory_space=pl.ANY))
        operands.append(out)
        aliases = {3 + sources: 0}
    steps, longest, reach = len(numbers), max(len(held) for held in segments), height + 2 * MAXS
    work = steps * velocities * height * LANES
    return pl.pallas_call(
        functools.partial(
            stack_kernel,
            segments=described,
            sources=sources,
            total=columns // LANES,
            together=next(size for size in (36, 18, 12, 9, 8, 6, 4, 3, 2, 1) if velocities % size == 0),
        ),
        grid_spec=pltpu.PrefetchScalarGridSpec(
            num_scalar_prefetch=3,
            grid=(steps,),
            in_specs=in_specs,
            out_specs=pl.BlockSpec((velocities, height, LANES), lambda step, place, *_: (0, 0, place[step])),
            scratch_shapes=[
                pltpu.VMEM((epochs, 2, longest, reach, LANES), jnp.float32),
                pltpu.VMEM((epochs, longest + 2, reach, LANES), jnp.int32),
                pltpu.VMEM((epochs, longest, reach, LANES), jnp.int32),
                pltpu.VMEM((epochs, longest + 2, reach - height + 8, LANES), jnp.int32),
                pltpu.VMEM((2, 8, LANES), jnp.float32),
            ],
        ),
        out_shape=out_shape,
        input_output_aliases=aliases,
        compiler_params=pltpu.CompilerParams(vmem_limit_bytes=VMEM),
        cost_estimate=pl.CostEstimate(flops=16 * work, bytes_accessed=24 * work, transcendentals=work),
    )(jnp.stack(numbers + [lower]).astype(jnp.int32), shifts + MAXS, floor, *operands)


def local(images, variance, spread_kernel, shifts, epoch_owner, valid_rows):
    height, columns = images.shape[1:]
    blocks = lax.axis_size("vel")
    width = columns // blocks
    me, lower = lax.axis_index("vel"), lax.axis_index("rows")
    swap = [(0, 1), (1, 0)]

    order = list(range(0, blocks, 2)) + list(range(1, blocks, 2))[::-1]
    right = [(order[i], order[(i + 1) % blocks]) for i in range(blocks)]
    left = [(b, a) for a, b in right]

    def position(index):
        return jnp.where(index % 2 == 0, index // 2, blocks - 1 - index // 2)

    mine = position(me)
    place = jnp.stack([mine, lower]).astype(jnp.int32)

    numbers = jnp.concatenate([jnp.stack([me, lower]).astype(jnp.int32), epoch_owner, valid_rows.reshape(-1)])
    starts = position(me ^ jnp.arange(blocks, dtype=jnp.int32)) * width
    chunks = list(cut(starts, jnp.concatenate([images, variance]), blocks))
    for step in sorted(range(1, blocks), key=lambda step: (step & (step - 1) > 0, step)):
        chunks[step] = lax.ppermute(chunks[step], "vel", [(i, i ^ step) for i in range(blocks)])
    chunks[1], spread_kernel, numbers = lax.optimization_barrier((chunks[1], spread_kernel, numbers))
    bands, floor = make_bands(spread_kernel)
    chunks[-1], floor = lax.optimization_barrier((chunks[-1], floor))
    own, edges = pick(numbers, epoch_owner.shape[0], chunks, height)
    payload = correlate(place, own, lax.ppermute(edges, "rows", swap), bands, spread_kernel.shape[0])

    flat_shifts, floor = shifts.reshape(-1), floor[0, :1]
    out_shape = jax.ShapeDtypeStruct((shifts.shape[0], height, columns), jnp.float32)

    tiles, half = payload.shape[3], blocks // 2

    def stack_now(segments, out):
        numbers = [
            (mine + offset) % blocks * tiles + tile for held in segments for offset, tile in held[:-1]
        ]
        held = [[(have[offset], tile) for offset, tile in segment] for segment in segments]
        return stack_tiles(numbers, lower, flat_shifts, floor, held, out, out_shape)

    def block(offset):
        return [(offset, tile) for tile in range(tiles)]

    behind, ahead = lax.ppermute(payload, "vel", right), lax.ppermute(payload, "vel", left)
    border = lax.ppermute(payload[:1], "rows", swap)
    have = {0: ((payload, 0), (payload, 1), (border, 0))}
    out = stack_now([block(0)], None)
    for step in range(1, half + 1):
        if step < half:
            if step > 1:
                behind, ahead = lax.ppermute(behind, "vel", right), lax.ppermute(ahead, "vel", left)
            behind, ahead, out = lax.optimization_barrier((behind, ahead, out))
            border = lax.ppermute(jnp.concatenate([behind[:1], ahead[:1]]), "rows", swap)
            have[-step] = ((behind, 0), (behind, 1), (border, 0))
            have[step] = ((ahead, 0), (ahead, 1), (border, 1))
            segments = [block(-step) + [(1 - step, 0)], [(step - 1, tiles - 1)] + block(step)]
        else:
            behind, border = lax.ppermute(behind, "vel", right), lax.ppermute(border[1:], "vel", left)
            behind, border, out = lax.optimization_barrier((behind, border, out))
            have[step] = ((behind, 0), (behind, 1), (border, 0))
            segments = [[(step - 1, tiles - 1)] + block(step) + [(1 - step, 0)]]
        out = stack_now(segments, out)
    return out


def solution(mesh):
    in_specs = (
        P(("fields", "vel"), "rows", None),
        P(("fields", "vel"), "rows", None),
        P(),
        P(("fields", "vel"), None, None),
        P("fields"),
        P("fields", None),
    )
    out_specs = P(("fields", "vel"), "rows", None)
    return jax.shard_map(local, mesh=mesh, in_specs=in_specs, out_specs=out_specs, check_vma=False)
```
